512 devices in a mesh: gz: 64 (over z_lo, y, x), gy: 8 (over z_hi, core).
Axes of the slice: x: 4, y: 8, z: 8 (z_hi: 4, z_lo: 2; z = z_hi * 2 + z_lo), core: 2. Of those that a mesh axis runs over, the one named last changes fastest.
Arguments:
- features: bfloat16 [16, 256, 64, 128], P(None, 'gz', 'gy'), may hold values from -16 to 16
- field: float32 [256, 64, 128], P('gz', 'gy'), may hold values from -6 to 6
- velocity: float32 [3, 256, 64, 128], P(None, 'gz', 'gy'), may hold values from -3 to 3
- weight: bfloat16 [16, 432], replicated, may hold values from -0.3125 to 0.3125
- cotangent: float32 [256, 64, 128], P('gz', 'gy'), may hold values from -12 to 12
Outputs:
- grad_field: float32 [256, 64, 128], P('gz', 'gy')
- grad_features: bfloat16 [16, 256, 64, 128], P(None, 'gz', 'gy')
- grad_weight: float32 [16, 432], replicated
- factor_patch: float32 [432, 432], replicated
- factor_grad: float32 [16, 16], replicated
The draws below stay inside these ranges and needn't reach their ends.
All inputs are finite; a program needn't handle non-finite values.
Results may differ from the reference program's by a relative error of at most 0.0049.
Values may be sent and summed in bfloat16 or wider, within the bound.
No kernel may reach another device: no remote copies, remote signals or barrier semaphores. Data moves between devices by JAX's collectives and lax.ppermute only.
A program may use at most 64 MiB of HBM per device.

```python
import math
import jax
import jax.numpy as jnp
from jax import lax

C = 16
P_SIZE = 432
STEPS = 2
CZ = 4
NX = 128
NZ = 256
NY = 64


def draw_features(key, part):
    key = jax.random.fold_in(key, 11)
    key_base = jax.random.fold_in(key, 1)
    key_chan = jax.random.fold_in(key, 2)
    depth_pos = (jnp.arange(NZ, dtype=jnp.float32) + 0.5) / NZ - 0.5
    chan_scale = jnp.exp(jax.random.uniform(key_chan, (C,), minval=math.log(0.3), maxval=math.log(3.0)))
    base_draw = jax.random.normal(key_base, (C, NZ, NY, NX))
    ramp = jnp.exp(math.log(3.0) * depth_pos)
    values = base_draw * chan_scale[:, None, None, None] * ramp[None, :, None, None]
    return jnp.clip(values, -16.0, 16.0).astype(jnp.bfloat16)


def draw_cotangent(key, part):
    key = jax.random.fold_in(key, 23)
    depth_pos = (jnp.arange(NZ, dtype=jnp.float32) + 0.5) / NZ - 0.5
    base_draw = jax.random.normal(key, (NZ, NY, NX))
    ramp = jnp.exp(math.log(3.0) * depth_pos)
    values = base_draw * ramp[:, None, None]
    return jnp.clip(values, -12.0, 12.0).astype(jnp.float32)


def block_levels(key, dims, cuts, smallest, top_value):
    level, own = 1.0, jax.random.fold_in(key, 6)
    for axis_at, blocks in cuts:
        heights = jnp.exp(jax.random.uniform(jax.random.fold_in(own, axis_at), (blocks,), jnp.float32, smallest / len(cuts), top_value / len(cuts)))
        level = level * jnp.repeat(heights, dims[axis_at] // blocks).reshape([-1 if axis == axis_at else 1 for axis in range(len(dims))])
    return level


def normal_values(stream_key, extent, deviation, reach, cuts=(), held_as=jnp.bfloat16):
    level = block_levels(stream_key, extent, cuts, -0.22, 0.18) if cuts else 1.0
    array = jax.random.normal(stream_key, extent, jnp.float32) * deviation * level
    return jnp.minimum(jnp.maximum(array, -reach), reach).astype(held_as)


def setup_inputs(seed: int = 0) -> dict:
    arg_keys = jax.random.split(jax.random.key(seed), 6)
    return {
        "features": draw_features(jax.random.fold_in(arg_keys[5], 71), 0),
        "field": normal_values(arg_keys[1], (NZ, NY, NX), 1.0, 6.0, ((0, 64), (1, 8)), jnp.float32),
        "velocity": normal_values(arg_keys[2], (3, NZ, NY, NX), 0.5, 3.0, ((1, 64), (2, 8)), jnp.float32),
        "weight": normal_values(arg_keys[3], (C, P_SIZE), P_SIZE ** -0.5, 0.3125),
        "cotangent": draw_cotangent(jax.random.fold_in(arg_keys[5], 71), 0),
    }


step_size = 0.15
face_weights = (2.0 / 60.0, -13.0 / 60.0, 47.0 / 60.0, 27.0 / 60.0, -3.0 / 60.0)
contract_cells = (((1,), (1,)), ((), ()))

def patches(padded, z_first, z_cells, mirror):
    z_slab = lax.dynamic_slice_in_dim(padded, z_first, z_cells + 2, 1)
    channels = z_slab.shape[0]
    y_span = z_slab.shape[2]
    x_span = z_slab.shape[3]
    pieces = []
    for shift_z in (-1, 0, 1):
        for shift_y in (-1, 0, 1):
            for shift_x in (-1, 0, 1):
                first_z = 1 + mirror * shift_z
                first_y = 1 + mirror * shift_y
                first_x = 1 + mirror * shift_x
                pieces.append(z_slab[:, first_z:first_z + z_cells, first_y:first_y + y_span - 2, first_x:first_x + x_span - 2])
    return jnp.stack(pieces, axis=1).reshape(channels * 27, -1)

def advance_full(field_now, coefficients, velocities):
    updated = field_now * (1.0 + step_size * coefficients[15])
    for direction in range(3):
        face_flux = jnp.zeros_like(field_now)
        for offset in range(-2, 3):
            weights_face = face_weights[offset + 2] + coefficients[direction * 5 + offset + 2]
            face_flux = face_flux + weights_face * jnp.roll(field_now, -offset, direction)
        face_flux = velocities[direction] * face_flux
        updated = updated - step_size * (face_flux - jnp.roll(face_flux, 1, direction))
    return updated

def retreat_full(adjoint_now, field_now, coefficients, velocities):
    earlier = adjoint_now * (1.0 + step_size * coefficients[15])
    grads = []
    for direction in range(3):
        face_drive = -step_size * (adjoint_now - jnp.roll(adjoint_now, -1, direction)) * velocities[direction]
        for offset in range(-2, 3):
            weights_face = face_weights[offset + 2] + coefficients[direction * 5 + offset + 2]
            earlier = earlier + jnp.roll(face_drive * weights_face, offset, direction)
            grads.append(face_drive * jnp.roll(field_now, -offset, direction))
    grads.append(step_size * adjoint_now * field_now)
    return (earlier, grads)

def reference(features, field, velocity, weight, cotangent):
    cell_count = NZ * NY * NX
    padded = jnp.pad(features, ((0, 0), (1, 1), (1, 1), (1, 1)), mode='wrap')
    starts = jnp.arange(NZ // CZ, dtype=jnp.int32) * CZ

    def conv_block(start):
        return jnp.dot(weight, patches(padded, start, CZ, 1), preferred_element_type=jnp.float32).reshape(C, CZ, NY, NX)
    coefficients = jnp.moveaxis(lax.map(conv_block, starts), 1, 0).reshape(C, NZ, NY, NX)
    states = [field]
    for step_index in range(STEPS - 1):
        states.append(advance_full(states[-1], coefficients, velocity))
    adjoint = cotangent
    grad_total = None
    for step_index in reversed(range(STEPS)):
        adjoint, grads = retreat_full(adjoint, states[step_index], coefficients, velocity)
        stacked = jnp.stack(grads)
        grad_total = stacked if grad_total is None else grad_total + stacked
    grad_bf = grad_total.astype(jnp.bfloat16)
    flipped = weight.reshape(C, C, 27).transpose(1, 0, 2).reshape(C, C * 27)
    grad_pad = jnp.pad(grad_bf, ((0, 0), (1, 1), (1, 1), (1, 1)), mode='wrap')

    def back_block(start):
        values = jnp.dot(flipped, patches(grad_pad, start, CZ, -1), preferred_element_type=jnp.float32)
        return values.astype(jnp.bfloat16).reshape(C, CZ, NY, NX)
    grad_features = jnp.moveaxis(lax.map(back_block, starts), 1, 0).reshape(C, NZ, NY, NX)

    def accumulate(position, state):
        patch_gram, grad_w = state
        start = (position * CZ).astype(jnp.int32)
        patch_block = patches(padded, start, CZ, 1)
        local_part = lax.dynamic_slice_in_dim(grad_bf, start, CZ, 1).reshape(C, -1)
        patch_gram = patch_gram + lax.dot_general(patch_block, patch_block, contract_cells, preferred_element_type=jnp.float32)
        grad_w = grad_w + lax.dot_general(local_part, patch_block, contract_cells, preferred_element_type=jnp.float32)
        return (patch_gram, grad_w)
    patch_gram, grad_w = lax.fori_loop(0, NZ // CZ, accumulate, (jnp.zeros((P_SIZE, P_SIZE), jnp.float32), jnp.zeros((C, P_SIZE), jnp.float32)))
    grad_flat = grad_bf.reshape(C, -1)
    factor_grad = lax.dot_general(grad_flat, grad_flat, contract_cells, preferred_element_type=jnp.float32) / cell_count
    return (adjoint, grad_features, grad_w / math.sqrt(cell_count), patch_gram / cell_count, factor_grad)
```

```python
import math

import jax
import jax.numpy as jnp
import numpy as np
from jax import lax
from jax.experimental import pallas as pl
from jax.experimental.pallas import tpu as pltpu
from jax.sharding import PartitionSpec as P

H = 0.15
BASE = (2.0 / 60.0, -13.0 / 60.0, 47.0 / 60.0, 27.0 / 60.0, -3.0 / 60.0)
F32 = jnp.float32
BF16 = jnp.bfloat16
NT = (((1,), (1,)), ((), ()))

ROWS_IN = 19
ROWS_OUT = 17
PREV = 5
NEXT = 6

_VM = pl.BlockSpec(memory_space=pltpu.VMEM)


def call(kernel, outs, scratch, args):
    return pl.pallas_call(
        kernel,
        out_shape=[jax.ShapeDtypeStruct(s, t) for s, t in outs],
        in_specs=[_VM] * len(args),
        out_specs=[_VM] * len(outs),
        scratch_shapes=scratch,
        compiler_params=pltpu.CompilerParams(vmem_limit_bytes=48 * 1024 * 1024),
    )(*args)


def roll(value, shift, axis):
    shift %= value.shape[axis]
    return value if shift == 0 else pltpu.roll(value, shift, axis)


def split(plane):
    lead = plane.astype(BF16).astype(F32)
    return jnp.concatenate([lead, plane - lead], axis=0).astype(BF16)


def join(tile):
    both = tile.astype(F32)
    return both[:8] + both[8:]


def pack_y(feat, field, vel, cot, own_feat, own_fields, to_next, to_prev, turn):
    for c in range(16):
        turn[pl.ds(c, 32, stride=16), :] = feat[c].astype(F32)
    for zy in range(32):
        tile = turn[zy * 16 : (zy + 1) * 16, :].astype(BF16)
        own_feat[zy] = tile
        z, y = divmod(zy, 8)
        if y >= 8 - PREV:
            to_next[z * PREV + y - (8 - PREV)] = tile
        if y < NEXT:
            to_prev[z * NEXT + y] = tile
    for i in range(20):
        z = i % 4
        source = field if i < 4 else cot if i < 8 else vel
        plane = source[z] if i < 8 else source[i // 4 - 2, z]
        tile = split(plane)
        own_fields[i] = tile
        to_next[4 * PREV + i] = tile
        to_prev[4 * NEXT + i] = tile


UP_FIELDS = [1, 2, 3, 7, 11, 15, 19]
DOWN_FIELDS = [0, 1, 2, 4, 5, 8, 12, 16]


def pack_z(own_feat, own_fields, before, after, to_up, to_down):
    for out, z, fields in ((to_up, 3, UP_FIELDS), (to_down, 0, DOWN_FIELDS)):
        out[0:PREV] = before[z * PREV : (z + 1) * PREV]
        out[PREV : PREV + 8] = own_feat[z * 8 : (z + 1) * 8]
        out[PREV + 8 : ROWS_IN] = after[z * NEXT : (z + 1) * NEXT]
        at = ROWS_IN
        for i in fields:
            out[at] = before[4 * PREV + i]
            out[at + 1] = own_fields[i]
            out[at + 2] = after[4 * NEXT + i]
            at += 3


def fill_columns(columns, shifted, z, rows):
    for a in range(3):
        for b in range(3):
            at = pl.multiple_of(z * 144 + (a * 3 + b) * 16, 16)
            for y in range(rows):
                columns[pl.ds(at, 16), y * 128 : (y + 1) * 128] = shifted[
                    b, z, (y + a) * 16 : (y + a + 1) * 16, :
                ]


def stage_one(
    own_feat, before, after, below, above, field, vel, cot, w_rows, shift,
    send_up, send_down, gram, columns_own, coef, u0, lam2, velx, u1_part, lam_part, face3,
    shifted, columns,
):
    shift_value = shift[...]
    for z in range(6):
        if z == 0:
            tiles = below[0:ROWS_IN].reshape(ROWS_IN * 16, 128)
        elif z == 5:
            tiles = above[0:ROWS_IN].reshape(ROWS_IN * 16, 128)
        else:
            p = z - 1
            tiles = jnp.concatenate(
                [
                    before[p * PREV : (p + 1) * PREV].reshape(PREV * 16, 128),
                    own_feat[p * 8 : (p + 1) * 8].reshape(128, 128),
                    after[p * NEXT : (p + 1) * NEXT].reshape(NEXT * 16, 128),
                ],
                axis=0,
            )
        shifted[1, z] = tiles
        both = jnp.dot(tiles, shift_value, preferred_element_type=F32).astype(BF16)
        shifted[0, z] = both[:, :128]
        shifted[2, z] = both[:, 128:]

    def extended(i, own):
        return jnp.concatenate(
            [join(before[4 * PREV + i]), own, join(after[4 * NEXT + i])], axis=0
        )

    def received(source, slot):
        at = ROWS_IN + 3 * slot
        return jnp.concatenate([join(source[at + j]) for j in range(3)], axis=0)

    for j in range(3):
        u0[j] = received(below, j)
        u0[7 + j] = received(above, j)
        velx[j, 0] = received(below, 4 + j)
        velx[j, 5] = received(above, 5 + j)
    lam2[0] = received(below, 3)
    lam2[5] = received(above, 3)
    lam2[6] = received(above, 4)
    for z in range(4):
        u0[3 + z] = extended(z, field[z])
        lam2[1 + z] = extended(4 + z, cot[z])
        for d in range(3):
            velx[d, 1 + z] = extended(8 + 4 * d + z, vel[d, z])

    def fill(z, carry):
        fill_columns(columns, shifted, z, ROWS_OUT)
        return carry

    lax.fori_loop(0, 6, fill, 0)

    w_value = w_rows[...]
    for p in range(4):
        plane = jnp.dot(
            w_value, columns[p * 144 : p * 144 + 432, :], preferred_element_type=F32
        )
        for y in range(ROWS_OUT):
            coef[p, (4 + y) * 16 : (5 + y) * 16, :] = plane[:, y * 128 : (y + 1) * 128]

    total = None
    for p in range(4):
        part = lax.dot_general(
            columns[p * 144 : (p + 1) * 144, 512:1536],
            columns[p * 144 + 48 : p * 144 + 432, 512:1536],
            NT,
            preferred_element_type=F32,
        )
        total = part if total is None else total + part
    for t in range(3):
        gram[t * 144 : (t + 1) * 144, :] = total[:, t * 128 : (t + 1) * 128]
    gram[432:, :] = jnp.zeros((gram.shape[0] - 432, 128), F32)
    columns_own[...] = columns[:, 512:1536]

    def a(p, k):
        value = coef[p, pl.ds(k, 24, stride=16), :]
        return value + BASE[k % 5]

    pushed = [None] * 8

    def push(slot, value):
        pushed[slot] = value if pushed[slot] is None else pushed[slot] + value

    faces_z = []
    states = []
    for p in range(4):
        rate = 1.0 + H * coef[p, pl.ds(15, 24, stride=16), :]
        u = u0[3 + p]
        lam = lam2[1 + p]
        state = u * rate
        push(p + 2, lam * rate)
        for d in range(3):
            beyond = lam2[2 + p] if d == 0 else roll(lam, -1, d - 1)
            drive = (-H) * (lam - beyond) * velx[d, 1 + p]
            face = None
            for s in range(-2, 3):
                weight = a(p, 5 * d + s + 2)
                term = weight * (u0[3 + p + s] if d == 0 else roll(u, -s, d - 1))
                face = term if face is None else face + term
                back = drive * weight
                if d == 0:
                    push(p + 2 + s, back)
                else:
                    push(p + 2, roll(back, s, d - 1))
            face = (H * velx[d, 1 + p]) * face
            if d == 0:
                faces_z.append(face)
                state = state - (face if p == 0 else face - faces_z[p - 1])
            else:
                state = state - (face - roll(face, 1, d - 1))
        states.append(state)
    for p in range(4):
        u1_part[p] = states[p]
    for j in range(8):
        lam_part[j] = pushed[j]
    face3[...] = faces_z[3]
    ups = [states[1], states[2], states[3], faces_z[3], pushed[5], pushed[6], pushed[7]]
    downs = [states[0], states[1], states[2], pushed[2], pushed[3], pushed[0], pushed[1]]
    for j in range(7):
        send_up[j] = ups[j][4:20]
        send_down[j] = downs[j][4:20]


def stage_two(
    below, above, u1_part, lam_part, face3, u0, lam2, velx, coef, columns_own, w_back, shift,
    grad_w, grad_feat, lam0, push_up, push_down,
    u1, lam1, turn, shifted, columns, row, turn_out,
):
    def padded(value):
        zero = jnp.zeros((4, 128), F32)
        return jnp.concatenate([zero, value, zero], axis=0)

    low = [padded(below[j]) for j in range(7)]
    high = [padded(above[j]) for j in range(7)]
    for j in range(3):
        u1[j] = low[j]
        u1[7 + j] = high[j] + (face3[...] if j == 0 else 0.0)
        u1[4 + j] = u1_part[1 + j]
    u1[3] = u1_part[0] + low[3]
    lam1[0] = low[4] + lam_part[1]
    lam1[1] = lam_part[2] + low[5]
    lam1[2] = lam_part[3] + low[6]
    lam1[3] = lam_part[4] + high[5]
    lam1[4] = lam_part[5] + high[6]
    lam1[5] = high[3] + lam_part[6]
    lam1[6] = high[4] + lam_part[7]

    pushed = [None] * 8

    def push(slot, value):
        pushed[slot] = value if pushed[slot] is None else pushed[slot] + value

    for z in range(6):
        later, first = lam2[z], lam1[z]
        v, u = u1[z + 2], u0[z + 2]
        own = 1 <= z <= 4
        p = z - 1
        if own:
            push(z + 1, first * (1.0 + H * coef[p, pl.ds(15, 24, stride=16), :]))
        for d in range(3):
            speed = velx[d, z]
            beyond_later = lam2[z + 1] if d == 0 else roll(later, -1, d - 1)
            beyond_first = lam1[z + 1] if d == 0 else roll(first, -1, d - 1)
            drive_later = (-H) * (later - beyond_later) * speed
            drive_first = (-H) * (first - beyond_first) * speed
            for s in range(-2, 3):
                k = 5 * d + s + 2
                there_later = u1[z + 2 + s] if d == 0 else roll(v, -s, d - 1)
                there_first = u0[z + 2 + s] if d == 0 else roll(u, -s, d - 1)
                turn[z, pl.ds(k, 24, stride=16), :] = (
                    drive_later * there_later + drive_first * there_first
                )
                if own:
                    back = drive_first * (coef[p, pl.ds(k, 24, stride=16), :] + BASE[s + 2])
                    if d == 0:
                        push(z + 1 + s, back)
                    else:
                        push(z + 1, roll(back, s, d - 1))
        turn[z, pl.ds(15, 24, stride=16), :] = H * later * v + H * first * u
    for p in range(4):
        lam0[p] = pushed[2 + p][8:16]
    for j in range(2):
        push_up[j] = pushed[6 + j][8:16]
        push_down[j] = pushed[j][8:16]

    shift_value = shift[...]
    for z in range(6):
        tiles = turn[z, 7 * 16 : 17 * 16, :].astype(BF16)
        shifted[1, z] = tiles
        both = jnp.dot(tiles, shift_value, preferred_element_type=F32).astype(BF16)
        shifted[0, z] = both[:, :128]
        shifted[2, z] = both[:, 128:]

    def fill(z, carry):
        fill_columns(columns, shifted, z, 8)
        return carry

    lax.fori_loop(0, 6, fill, 0)

    sum_w = None
    sum_g = None
    for p in range(4):
        at = (p + 1) * 144 + 64
        mine = columns[at : at + 16, :]
        part_w = lax.dot_general(
            mine, columns_own[p * 144 : p * 144 + 432, :], NT, preferred_element_type=F32
        )
        part_g = lax.dot_general(mine, mine, NT, preferred_element_type=F32)
        sum_w = part_w if sum_w is None else sum_w + part_w
        sum_g = part_g if sum_g is None else sum_g + part_g
    row[...] = jnp.zeros((16, 512), F32)
    row[:, 0:432] = sum_w
    row[:, 432:448] = sum_g
    for t in range(4):
        grad_w[t * 16 : (t + 1) * 16, :] = row[:, t * 128 : (t + 1) * 128]

    w_value = w_back[...]
    for p in range(4):
        plane = jnp.dot(
            w_value, columns[p * 144 : p * 144 + 432, :], preferred_element_type=F32
        )
        for y in range(8):
            turn_out[pl.ds(p * 8 + y, 16, stride=32), :] = plane[:, y * 128 : (y + 1) * 128]
    for c in range(16):
        grad_feat[c] = turn_out[c * 32 : (c + 1) * 32, :].astype(BF16)


def pieces(value):
    one = value.astype(BF16)
    rest = value - one.astype(F32)
    two = rest.astype(BF16)
    three = (rest - two.astype(F32)).astype(BF16)
    return one, two, three


def to_channel_major(value):
    i = lax.broadcasted_iota(jnp.int32, (432, 432), 0)
    j = lax.broadcasted_iota(jnp.int32, (432, 432), 1)
    place = jnp.where((i % 16) * 27 + i // 16 == j, 1.0, 0.0).astype(BF16)
    parts = [jnp.dot(v, place, preferred_element_type=F32) for v in pieces(value)]
    return parts[2] + parts[1] + parts[0]


def finish_gram(scale, chunks, out, square, block, turn):
    for t in range(3):
        square[0:144, 48 + t * 128 : 48 + (t + 1) * 128] = chunks[t * 144 : (t + 1) * 144, :] * scale
    square[0:48, 0:48] = square[48:96, 48:96]
    block[...] = jnp.zeros((256, 256), F32)
    block[0:48, 0:96] = square[0:48, 48:144]
    square[48:144, 0:48] = jnp.transpose(block[...])[0:96, 0:48]
    square[144:288, 144:432] = square[0:144, 0:288]
    square[288:432, 288:432] = square[0:144, 0:144]
    block[0:144, 0:144] = square[0:144, 144:288]
    turned = jnp.transpose(block[...])[0:144, 0:144]
    square[144:288, 0:144] = turned
    square[288:432, 144:288] = turned
    block[0:144, 0:144] = square[0:144, 288:432]
    square[288:432, 0:144] = jnp.transpose(block[...])[0:144, 0:144]
    ready = to_channel_major(square[...])
    for t in range(4):
        wide = min(128, 432 - t * 128)
        for o in range(27):
            turn[t, pl.ds(o, 16, stride=27), 0:wide] = ready[
                o * 16 : (o + 1) * 16, t * 128 : t * 128 + wide
            ]
        out[:, t * 128 : t * 128 + wide] = turn[t, :, 0:wide]


def finish_weight(scale_w, scale_g, chunks, out_w, out_g, row):
    for t in range(4):
        row[:, t * 128 : (t + 1) * 128] = chunks[t * 16 : (t + 1) * 16, :]
    out_w[...] = to_channel_major(row[:, 0:432] * scale_w)
    out_g[...] = row[:, 432:448] * scale_g


def neighbours(to_next, to_prev, axis):
    size = lax.axis_size(axis)
    up = [(i, (i + 1) % size) for i in range(size)]
    down = [(j, i) for i, j in up]
    return lax.ppermute(to_next, axis, up), lax.ppermute(to_prev, axis, down)


def body(features, field, velocity, weight, cotangent):
    nz, ny = lax.axis_size("gz"), lax.axis_size("gy")
    cells = float(4096 * nz * ny)
    by_offset = weight.reshape(16, 16, 27)
    w_rows = by_offset.transpose(0, 2, 1).reshape(16, 432)
    w_back = by_offset.transpose(1, 2, 0)[:, ::-1, :].reshape(16, 432)
    eye = np.eye(128)
    shift = jnp.asarray(
        np.concatenate([np.roll(eye, 1, axis=1), np.roll(eye, -1, axis=1)], axis=1), BF16
    )
    tile = (16, 128)
    own_feat, own_fields, to_next, to_prev = call(
        pack_y,
        [((32,) + tile, BF16), ((20,) + tile, BF16), ((4 * PREV + 20,) + tile, BF16),
         ((4 * NEXT + 20,) + tile, BF16)],
        [pltpu.VMEM((512, 128), F32)],
        (features.reshape(16, 32, 128), field, velocity, cotangent),
    )
    before, after = neighbours(to_next, to_prev, "gy")
    to_up, to_down = call(
        pack_z,
        [((ROWS_IN + 3 * len(UP_FIELDS),) + tile, BF16), ((ROWS_IN + 3 * len(DOWN_FIELDS),) + tile, BF16)],
        [],
        (own_feat, own_fields, before, after),
    )
    below, above = neighbours(to_up, to_down, "gz")
    send_up, send_down, gram, columns_own, coef, u0, lam2, velx, u1_part, lam_part, face3 = call(
        stage_one,
        [((7, 16, 128), F32), ((7, 16, 128), F32), ((512, 128), F32), ((864, 1024), BF16),
         ((4, 384, 128), F32), ((10, 24, 128), F32), ((7, 24, 128), F32), ((3, 6, 24, 128), F32),
         ((4, 24, 128), F32), ((8, 24, 128), F32), ((24, 128), F32)],
        [pltpu.VMEM((3, 6, ROWS_IN * 16, 128), BF16), pltpu.VMEM((864, ROWS_OUT * 128), BF16)],
        (own_feat, before, after, below, above, field, velocity, cotangent, w_rows, shift),
    )
    below1, above1 = neighbours(send_up, send_down, "gz")
    gram_parts = lax.all_to_all(gram.reshape(nz, 512 // nz, 128), "gz", 0, 0)
    gram_sum = jnp.sum(gram_parts, axis=0)
    grad_w, grad_feat, lam0, push_up, push_down = call(
        stage_two,
        [((64, 128), F32), ((16, 32, 128), BF16), ((4, 8, 128), F32), ((2, 8, 128), F32),
         ((2, 8, 128), F32)],
        [pltpu.VMEM((10, 24, 128), F32), pltpu.VMEM((7, 24, 128), F32),
         pltpu.VMEM((6, 384, 128), F32), pltpu.VMEM((3, 6, 160, 128), BF16),
         pltpu.VMEM((864, 1024), BF16), pltpu.VMEM((16, 512), F32), pltpu.VMEM((512, 128), F32)],
        (below1, above1, u1_part, lam_part, face3, u0, lam2, velx, coef, columns_own, w_back, shift),
    )
    wr, gr = 64 // ny, 512 // nz
    mixed = jnp.concatenate(
        [grad_w.reshape(ny, wr, 128), jnp.broadcast_to(gram_sum[None], (ny, gr, 128))], axis=1
    )
    mixed = jnp.sum(lax.all_to_all(mixed, "gy", 0, 0), axis=0)
    everyone = lax.all_to_all(jnp.broadcast_to(mixed[None], (nz, wr + gr, 128)), "gz", 0, 0)
    weight_sum = jnp.sum(everyone[:, :wr], axis=0)
    weight_all = lax.all_to_all(jnp.broadcast_to(weight_sum[None], (ny, wr, 128)), "gy", 0, 0)
    low, high = neighbours(push_up, push_down, "gz")
    grad_field = lam0 + jnp.concatenate([low, high], axis=0)
    (factor_patch,) = call(
        lambda *refs: finish_gram(1.0 / cells, *refs),
        [((432, 432), F32)],
        [pltpu.VMEM((432, 432), F32), pltpu.VMEM((256, 256), F32), pltpu.VMEM((4, 432, 128), F32)],
        (everyone[:, wr:].reshape(512, 128),),
    )
    grad_weight, factor_grad = call(
        lambda *refs: finish_weight(1.0 / math.sqrt(cells), 1.0 / cells, *refs),
        [((16, 432), F32), ((16, 16), F32)],
        [pltpu.VMEM((16, 512), F32)],
        (weight_all.reshape(64, 128),),
    )
    return (grad_field, grad_feat.reshape(16, 4, 8, 128), grad_weight, factor_patch, factor_grad)


def solution(mesh):
    placed = (
        P(None, "gz", "gy", None),
        P("gz", "gy", None),
        P(None, "gz", "gy", None),
        P(),
        P("gz", "gy", None),
    )
    return jax.shard_map(
        body,
        mesh=mesh,
        in_specs=placed,
        out_specs=(P("gz", "gy", None), P(None, "gz", "gy", None), P(), P(), P()),
        check_vma=False,
    )
```

```python
import math

import jax
import jax.numpy as jnp
from jax import lax
from jax.experimental import pallas as pl
from jax.experimental.pallas import tpu as pltpu
from jax.sharding import PartitionSpec as P

H = 0.15
BASE = (2.0 / 60.0, -13.0 / 60.0, 47.0 / 60.0, 27.0 / 60.0, -3.0 / 60.0)
F32 = jnp.float32
BF16 = jnp.bfloat16
NT = (((1,), (1,)), ((), ()))

ROWS_IN = 19
ROWS_OUT = 17
PREV = 5
NEXT = 6

_HBM = pl.BlockSpec(memory_space=pltpu.HBM)


def call(kernel, outs, scratch, args):
    n_in, n_out = len(args), len(outs)

    def run(*refs):
        source, target = refs[:n_in], refs[n_in : n_in + n_out]
        arrived, left = refs[n_in + n_out : n_in + n_out + 2]
        held = refs[n_in + n_out + 2 :]
        here, there = held[:n_in], held[n_in : n_in + n_out]
        coming = {i: pltpu.make_async_copy(source[i], here[i], arrived.at[i]) for i in range(n_in)}
        going = {i: pltpu.make_async_copy(there[i], target[i], left.at[i]) for i in range(n_out)}
        sent = []
        for i in range(n_in):
            coming[i].start()

        def need(*which):
            for i in which:
                coming.pop(i).wait()

        def done(*which):
            for i in which:
                going[i].start()
                sent.append(i)

        kernel(need, done, *held)
        need(*list(coming))
        done(*[i for i in range(n_out) if i not in sent])
        for i in range(n_out):
            going[i].wait()

    return pl.pallas_call(
        run,
        out_shape=[jax.ShapeDtypeStruct(s, t) for s, t in outs],
        in_specs=[_HBM] * n_in,
        out_specs=[_HBM] * n_out,
        scratch_shapes=[pltpu.SemaphoreType.DMA((n_in,)), pltpu.SemaphoreType.DMA((n_out,))]
        + [pltpu.VMEM(a.shape, a.dtype) for a in args]
        + [pltpu.VMEM(s, t) for s, t in outs]
        + scratch,
        compiler_params=pltpu.CompilerParams(vmem_limit_bytes=64 * 1024 * 1024),
    )(*args)


def shift_both():
    i = lax.broadcasted_iota(jnp.int32, (128, 256), 0)
    j = lax.broadcasted_iota(jnp.int32, (128, 256), 1)
    source = jnp.where(j < 128, j + 127, j + 1) % 128
    return jnp.where(i == source, 1.0, 0.0).astype(BF16)


def roll(value, shift, axis):
    shift %= value.shape[axis]
    return value if shift == 0 else pltpu.roll(value, shift, axis)


def split(plane):
    lead = plane.astype(BF16).astype(F32)
    return jnp.concatenate([lead, plane - lead], axis=0).astype(BF16)


def join(tile):
    both = tile.astype(F32)
    return both[:8] + both[8:]


ORDER = [
    ("l", 3), (0, 3), (1, 3), (2, 3), ("u", 3), ("u", 1), ("u", 2), ("u", 0), ("l", 0), ("l", 1),
    (0, 0), (1, 0), (2, 0), ("l", 2), (0, 1), (0, 2), (1, 1), (1, 2), (2, 1), (2, 2),
]
UP, DOWN = (0, 7), (5, 13)


def pack_y(
    need, done, feat, field, vel, cot, own_feat, own_fields, to_next, to_prev, turn
):
    need(0)
    for c in range(16):
        turn[pl.ds(c, 32, stride=16), :] = feat[c].astype(F32)
    for zy in range(32):
        tile = turn[zy * 16 : (zy + 1) * 16, :].astype(BF16)
        own_feat[zy] = tile
        z, y = divmod(zy, 8)
        if y >= 8 - PREV:
            to_next[z * PREV + y - (8 - PREV)] = tile
        if y < NEXT:
            to_prev[z * NEXT + y] = tile
    need(1, 2, 3)
    for i, (kind, z) in enumerate(ORDER):
        tile = split(field[z] if kind == "u" else cot[z] if kind == "l" else vel[kind, z])
        own_fields[i] = tile
        to_next[4 * PREV + i] = tile
        to_prev[4 * NEXT + i] = tile


def pack_z(own_feat, own_fields, before, after, to_up, to_down, moved):
    copies = []

    def move(source, at, out, to, count):
        copies.append(
            pltpu.make_async_copy(
                source.at[at : at + count], out.at[to : to + count], moved.at[len(copies)]
            )
        )

    for out, z, (first, stop) in ((to_up, 3, UP), (to_down, 0, DOWN)):
        n = stop - first
        move(before, z * PREV, out, 0, PREV)
        move(own_feat, z * 8, out, PREV, 8)
        move(after, z * NEXT, out, PREV + 8, NEXT)
        move(before, 4 * PREV + first, out, ROWS_IN, n)
        move(own_fields, first, out, ROWS_IN + n, n)
        move(after, 4 * NEXT + first, out, ROWS_IN + 2 * n, n)
    for copy in copies:
        copy.start()
    for copy in copies:
        copy.wait()


def fill_columns(columns, shifted, z, rows):
    for a in range(3):
        for b in range(3):
            at = pl.multiple_of(z * 144 + (a * 3 + b) * 16, 16)
            for y in range(rows):
                columns[pl.ds(at, 16), y * 128 : (y + 1) * 128] = shifted[
                    b, z, (y + a) * 16 : (y + a + 1) * 16, :
                ]


U0, LAM2, U1, LAM1, FACE = slice(0, 10), slice(10, 17), slice(35, 39), slice(39, 47), 47
VEL = (slice(17, 23), slice(23, 29), slice(29, 35))
FAR = [(2, 2), (3, 1), (3, 2), (1, -2), (0, -1), (0, -2)]


def stage_one(
    need, done, own_feat, before, after, below, above, field, vel, cot, w_rows,
    send_up, send_down, send_far, gram, columns_own, coef, kept,
    shifted, columns,
):
    u0, lam2 = kept.at[U0], kept.at[LAM2]
    velx = [kept.at[v] for v in VEL]
    shift_value = shift_both()
    need(0, 1, 2, 3, 4)
    for z in range(6):
        if z == 0:
            tiles = below[0:ROWS_IN].reshape(ROWS_IN * 16, 128)
        elif z == 5:
            tiles = above[0:ROWS_IN].reshape(ROWS_IN * 16, 128)
        else:
            p = z - 1
            tiles = jnp.concatenate(
                [
                    before[p * PREV : (p + 1) * PREV].reshape(PREV * 16, 128),
                    own_feat[p * 8 : (p + 1) * 8].reshape(128, 128),
                    after[p * NEXT : (p + 1) * NEXT].reshape(NEXT * 16, 128),
                ],
                axis=0,
            )
        shifted[1, z] = tiles
        both = jnp.dot(tiles, shift_value, preferred_element_type=F32).astype(BF16)
        shifted[0, z] = both[:, :128]
        shifted[2, z] = both[:, 128:]

    need(5, 6, 7)

    def extended(kind, z, own):
        i = ORDER.index((kind, z))
        return jnp.concatenate(
            [join(before[4 * PREV + i]), own, join(after[4 * NEXT + i])], axis=0
        )

    def received(source, part, kind, z):
        n = part[1] - part[0]
        at = ROWS_IN + ORDER.index((kind, z)) - part[0]
        return jnp.concatenate([join(source[at + n * j]) for j in range(3)], axis=0)

    for j in range(3):
        u0[j] = received(below, UP, "u", 1 + j)
        u0[7 + j] = received(above, DOWN, "u", j)
        velx[j][0] = received(below, UP, j, 3)
        velx[j][5] = received(above, DOWN, j, 0)
    lam2[0] = received(below, UP, "l", 3)
    lam2[5] = received(above, DOWN, "l", 0)
    lam2[6] = received(above, DOWN, "l", 1)
    for z in range(4):
        u0[3 + z] = extended("u", z, field[z])
        lam2[1 + z] = extended("l", z, cot[z])
        for d in range(3):
            velx[d][1 + z] = extended(d, z, vel[d, z])

    def fill(z, carry):
        fill_columns(columns, shifted, z, ROWS_OUT)
        return carry

    lax.fori_loop(0, 6, fill, 0)

    need(8)
    w_value = w_rows[...]
    for p in range(4):
        plane = jnp.dot(
            w_value, columns[p * 144 : p * 144 + 432, :], preferred_element_type=F32
        )
        for y in range(ROWS_OUT):
            coef[p, (4 + y) * 16 : (5 + y) * 16, :] = plane[:, y * 128 : (y + 1) * 128]

    total = None
    for p in range(4):
        part = lax.dot_general(
            columns[p * 144 : (p + 1) * 144, 512:1536],
            columns[p * 144 + 48 : p * 144 + 432, 512:1536],
            NT,
            preferred_element_type=F32,
        )
        total = part if total is None else total + part
    for t in range(3):
        gram[t * 144 : (t + 1) * 144, :] = total[:, t * 128 : (t + 1) * 128]
    gram[432:, :] = jnp.zeros((gram.shape[0] - 432, 128), F32)
    columns_own[...] = columns[:, 512:1536]
    done(3, 4, 5)

    def a(p, k):
        value = coef[p, pl.ds(k, 24, stride=16), :]
        return value + BASE[k % 5]

    pushed = [None] * 8

    def push(slot, value):
        pushed[slot] = value if pushed[slot] is None else pushed[slot] + value

    faces_z = []
    states = []
    carried = {}
    for p in range(4):
        rate = 1.0 + H * coef[p, pl.ds(15, 24, stride=16), :]
        u = u0[3 + p]
        lam = lam2[1 + p]
        state = u * rate
        push(p + 2, lam * rate)
        for d in range(3):
            beyond = lam2[2 + p] if d == 0 else roll(lam, -1, d - 1)
            drive = (-H) * (lam - beyond) * velx[d][1 + p]
            face = None
            for s in range(-2, 3):
                weight = a(p, 5 * d + s + 2)
                term = weight * (u0[3 + p + s] if d == 0 else roll(u, -s, d - 1))
                face = term if face is None else face + term
                back = drive * weight
                if d == 0:
                    push(p + 2 + s, back)
                    if (p, s) in FAR:
                        carried[p, s] = velx[0][1 + p] * weight
                else:
                    push(p + 2, roll(back, s, d - 1))
            face = (H * velx[d][1 + p]) * face
            if d == 0:
                faces_z.append(face)
                state = state - (face if p == 0 else face - faces_z[p - 1])
            else:
                state = state - (face - roll(face, 1, d - 1))
        states.append(state)
    u1_part, lam_part = kept.at[U1], kept.at[LAM1]
    for p in range(4):
        u1_part[p] = states[p]
    for j in range(8):
        lam_part[j] = pushed[j]
    kept[FACE] = faces_z[3]
    ups = [states[1], states[2], states[3], faces_z[3], pushed[5], pushed[6], pushed[7], pushed[4]]
    downs = [states[0], states[1], states[2], pushed[2], pushed[3], pushed[0], pushed[1], pushed[4]]
    for j in range(8):
        send_up[j] = ups[j][4:20]
        send_down[j] = downs[j][4:20]
    for out, keys in ((send_up, FAR[:3]), (send_down, FAR[3:])):
        out[8, 0:8, :] = carried[keys[0]][8:16]
        out[8, 8:16, :] = carried[keys[1]][8:16]
        out[9, 0:8, :] = carried[keys[2]][8:16]
        out[9, 8:16, :] = carried[keys[2]][8:16]
    send_far[...] = pushed[0][8:16]


def stage_two(
    need, done, below, above, far, state, coef, columns_own, w_back,
    grad_w, grad_feat, lam0,
    u1, lam1, turn, shifted, columns, row, turn_out,
):
    u0, lam2, u1_part, lam_part = state.at[U0], state.at[LAM2], state.at[U1], state.at[LAM1]
    velx = [state.at[v] for v in VEL]
    need(0, 1, 2, 3, 4)

    def padded(value):
        zero = jnp.zeros((4, 128), F32)
        return jnp.concatenate([zero, value, zero], axis=0)

    low = [padded(below[j]) for j in range(8)]
    high = [padded(above[j]) for j in range(8)]
    for j in range(3):
        u1[j] = low[j]
        u1[7 + j] = high[j] + (state[FACE] if j == 0 else 0.0)
        u1[4 + j] = u1_part[1 + j]
    u1[3] = u1_part[0] + low[3]
    lam1[0] = low[4] + lam_part[1]
    lam1[1] = lam_part[2] + low[5]
    lam1[2] = lam_part[3] + low[6]
    lam1[3] = lam_part[4] + high[5]
    lam1[4] = lam_part[5] + high[6]
    lam1[5] = high[3] + lam_part[6]
    lam1[6] = high[4] + lam_part[7]

    pushed = [None] * 8

    def push(slot, value):
        pushed[slot] = value if pushed[slot] is None else pushed[slot] + value

    own_rows = slice(8, 16)
    lowest = lam_part[0][own_rows] + low[7][own_rows]
    highest = high[7][own_rows] + far[...]
    fall = [lowest, lam1[0, own_rows], lam1[1, own_rows]]
    rise = [lam1[5, own_rows], lam1[6, own_rows], highest]
    outer = [(-H) * (fall[0] - fall[1]), (-H) * (fall[1] - fall[2])]
    inner = [(-H) * (rise[0] - rise[1]), (-H) * (rise[1] - rise[2])]
    edge = [
        outer[0] * below[8, 0:8, :] + outer[1] * below[8, 8:16, :],
        outer[1] * below[9, 0:8, :],
        inner[0] * above[9, 0:8, :],
        inner[0] * above[8, 8:16, :] + inner[1] * above[8, 0:8, :],
    ]

    for z in range(6):
        later, first = lam2[z], lam1[z]
        v, u = u1[z + 2], u0[z + 2]
        own = 1 <= z <= 4
        p = z - 1
        if own:
            push(z + 1, first * (1.0 + H * coef[p, pl.ds(15, 24, stride=16), :]))
        for d in range(3):
            speed = velx[d][z]
            beyond_later = lam2[z + 1] if d == 0 else roll(later, -1, d - 1)
            beyond_first = lam1[z + 1] if d == 0 else roll(first, -1, d - 1)
            drive_later = (-H) * (later - beyond_later) * speed
            drive_first = (-H) * (first - beyond_first) * speed
            for s in range(-2, 3):
                k = 5 * d + s + 2
                there_later = u1[z + 2 + s] if d == 0 else roll(v, -s, d - 1)
                there_first = u0[z + 2 + s] if d == 0 else roll(u, -s, d - 1)
                turn[z, pl.ds(k, 24, stride=16), :] = (
                    drive_later * there_later + drive_first * there_first
                )
                if own:
                    back = drive_first * (coef[p, pl.ds(k, 24, stride=16), :] + BASE[s + 2])
                    if d == 0:
                        push(z + 1 + s, back)
                    else:
                        push(z + 1, roll(back, s, d - 1))
        turn[z, pl.ds(15, 24, stride=16), :] = H * later * v + H * first * u
    for p in range(4):
        lam0[p] = pushed[2 + p][own_rows] + edge[p]
    done(2)

    shift_value = shift_both()
    for z in range(6):
        tiles = turn[z, 7 * 16 : 17 * 16, :].astype(BF16)
        shifted[1, z] = tiles
        both = jnp.dot(tiles, shift_value, preferred_element_type=F32).astype(BF16)
        shifted[0, z] = both[:, :128]
        shifted[2, z] = both[:, 128:]

    def fill(z, carry):
        fill_columns(columns, shifted, z, 8)
        return carry

    lax.fori_loop(0, 6, fill, 0)

    need(5, 6)
    sum_w = None
    sum_g = None
    for p in range(4):
        at = (p + 1) * 144 + 64
        mine = columns[at : at + 16, :]
        part_w = lax.dot_general(
            mine, columns_own[p * 144 : p * 144 + 432, :], NT, preferred_element_type=F32
        )
        part_g = lax.dot_general(mine, mine, NT, preferred_element_type=F32)
        sum_w = part_w if sum_w is None else sum_w + part_w
        sum_g = part_g if sum_g is None else sum_g + part_g
    row[...] = jnp.zeros((16, 512), F32)
    row[:, 0:432] = sum_w
    row[:, 432:448] = sum_g
    for t in range(4):
        grad_w[t * 16 : (t + 1) * 16, :] = row[:, t * 128 : (t + 1) * 128]
    done(0)

    w_value = w_back[...]
    for p in range(4):
        plane = jnp.dot(
            w_value, columns[p * 144 : p * 144 + 432, :], preferred_element_type=F32
        )
        for y in range(8):
            turn_out[pl.ds(p * 8 + y, 16, stride=32), :] = plane[:, y * 128 : (y + 1) * 128]
    for c in range(16):
        grad_feat[c] = turn_out[c * 32 : (c + 1) * 32, :].astype(BF16)


def pieces(value):
    one = value.astype(BF16)
    rest = value - one.astype(F32)
    two = rest.astype(BF16)
    three = (rest - two.astype(F32)).astype(BF16)
    return one, two, three


def to_channel_major(value):
    i = lax.broadcasted_iota(jnp.int32, (432, 432), 0)
    j = lax.broadcasted_iota(jnp.int32, (432, 432), 1)
    place = jnp.where((i % 16) * 27 + i // 16 == j, 1.0, 0.0).astype(BF16)
    parts = [jnp.dot(v, place, preferred_element_type=F32) for v in pieces(value)]
    return parts[2] + parts[1] + parts[0]


def finish_gram(scale, need, done, chunks, out, square, block, turn):
    need(0)
    for t in range(3):
        square[0:144, 48 + t * 128 : 48 + (t + 1) * 128] = chunks[t * 144 : (t + 1) * 144, :] * scale
    square[0:48, 0:48] = square[48:96, 48:96]
    block[...] = jnp.zeros((256, 256), F32)
    block[0:48, 0:96] = square[0:48, 48:144]
    square[48:144, 0:48] = jnp.transpose(block[...])[0:96, 0:48]
    square[144:288, 144:432] = square[0:144, 0:288]
    square[288:432, 288:432] = square[0:144, 0:144]
    block[0:144, 0:144] = square[0:144, 144:288]
    turned = jnp.transpose(block[...])[0:144, 0:144]
    square[144:288, 0:144] = turned
    square[288:432, 144:288] = turned
    block[0:144, 0:144] = square[0:144, 288:432]
    square[288:432, 0:144] = jnp.transpose(block[...])[0:144, 0:144]
    ready = to_channel_major(square[...])
    for t in range(4):
        wide = min(128, 432 - t * 128)
        for o in range(27):
            turn[t, pl.ds(o, 16, stride=27), 0:wide] = ready[
                o * 16 : (o + 1) * 16, t * 128 : t * 128 + wide
            ]
        out[:, t * 128 : t * 128 + wide] = turn[t, :, 0:wide]


def finish_weight(scale_w, scale_g, need, done, chunks, out_w, out_g, row):
    need(0)
    for t in range(4):
        row[:, t * 128 : (t + 1) * 128] = chunks[t * 16 : (t + 1) * 16, :]
    out_w[...] = to_channel_major(row[:, 0:432] * scale_w)
    out_g[...] = row[:, 432:448] * scale_g


def neighbours(to_next, to_prev, axis):
    size = lax.axis_size(axis)
    up = [(i, (i + 1) % size) for i in range(size)]
    down = [(j, i) for i, j in up]
    return lax.ppermute(to_next, axis, up), lax.ppermute(to_prev, axis, down)


def body(features, field, velocity, weight, cotangent):
    nz, ny = lax.axis_size("gz"), lax.axis_size("gy")
    cells = float(4096 * nz * ny)
    by_offset = weight.reshape(16, 16, 27)
    w_rows = by_offset.transpose(0, 2, 1).reshape(16, 432)
    w_back = by_offset.transpose(1, 2, 0)[:, ::-1, :].reshape(16, 432)
    tile = (16, 128)
    own_feat, own_fields, to_next, to_prev = call(
        pack_y,
        [((32,) + tile, BF16), ((20,) + tile, BF16), ((4 * PREV + 20,) + tile, BF16),
         ((4 * NEXT + 20,) + tile, BF16)],
        [pltpu.VMEM((512, 128), F32)],
        (features.reshape(16, 32, 128), field, velocity, cotangent),
    )
    before, after = neighbours(to_next, to_prev, "gy")
    to_up, to_down = pl.pallas_call(
        pack_z,
        out_shape=[
            jax.ShapeDtypeStruct((ROWS_IN + 3 * (stop - first),) + tile, BF16)
            for first, stop in (UP, DOWN)
        ],
        in_specs=[_HBM] * 4,
        out_specs=[_HBM] * 2,
        scratch_shapes=[pltpu.SemaphoreType.DMA((12,))],
        compiler_params=pltpu.CompilerParams(vmem_limit_bytes=64 * 1024 * 1024),
    )(own_feat, own_fields, before, after)
    below, above = neighbours(to_up, to_down, "gz")
    send_up, send_down, send_far, gram, columns_own, coef, state = call(
        stage_one,
        [((10, 16, 128), F32), ((10, 16, 128), F32), ((8, 128), F32), ((512, 128), F32),
         ((864, 1024), BF16), ((4, 384, 128), F32), ((48, 24, 128), F32)],
        [pltpu.VMEM((3, 6, ROWS_IN * 16, 128), BF16), pltpu.VMEM((864, ROWS_OUT * 128), BF16)],
        (own_feat, before, after, below, above, field, velocity, cotangent, w_rows),
    )
    below1, above1 = neighbours(send_up, send_down, "gz")
    far = lax.ppermute(send_far, "gz", [((i + 2) % nz, i) for i in range(nz)])
    gram_parts = lax.all_to_all(gram.reshape(nz, 512 // nz, 128), "gz", 0, 0)
    gram_sum = jnp.sum(gram_parts, axis=0)
    grad_w, grad_feat, grad_field = call(
        stage_two,
        [((64, 128), F32), ((16, 32, 128), BF16), ((4, 8, 128), F32)],
        [pltpu.VMEM((10, 24, 128), F32), pltpu.VMEM((7, 24, 128), F32),
         pltpu.VMEM((6, 384, 128), F32), pltpu.VMEM((3, 6, 160, 128), BF16),
         pltpu.VMEM((864, 1024), BF16), pltpu.VMEM((16, 512), F32), pltpu.VMEM((512, 128), F32)],
        (below1, above1, far, state, coef, columns_own, w_back),
    )
    wr, gr = 64 // ny, 512 // nz
    mixed = jnp.concatenate(
        [grad_w.reshape(ny, wr, 128), jnp.broadcast_to(gram_sum[None], (ny, gr, 128))], axis=1
    )
    mixed = jnp.sum(lax.all_to_all(mixed, "gy", 0, 0), axis=0)
    everyone = lax.all_to_all(jnp.broadcast_to(mixed[None], (nz, wr + gr, 128)), "gz", 0, 0)
    weight_sum = jnp.sum(everyone[:, :wr], axis=0)
    weight_all = lax.all_to_all(jnp.broadcast_to(weight_sum[None], (ny, wr, 128)), "gy", 0, 0)
    (factor_patch,) = call(
        lambda *refs: finish_gram(1.0 / cells, *refs),
        [((432, 432), F32)],
        [pltpu.VMEM((432, 432), F32), pltpu.VMEM((256, 256), F32), pltpu.VMEM((4, 432, 128), F32)],
        (everyone[:, wr:].reshape(512, 128),),
    )
    grad_weight, factor_grad = call(
        lambda *refs: finish_weight(1.0 / math.sqrt(cells), 1.0 / cells, *refs),
        [((16, 432), F32), ((16, 16), F32)],
        [pltpu.VMEM((16, 512), F32)],
        (weight_all.reshape(64, 128),),
    )
    return (grad_field, grad_feat.reshape(16, 4, 8, 128), grad_weight, factor_patch, factor_grad)


def solution(mesh):
    placed = (
        P(None, "gz", "gy", None),
        P("gz", "gy", None),
        P(None, "gz", "gy", None),
        P(),
        P("gz", "gy", None),
    )
    return jax.shard_map(
        body,
        mesh=mesh,
        in_specs=placed,
        out_specs=(P("gz", "gy", None), P(None, "gz", "gy", None), P(), P(), P()),
        check_vma=False,
    )
```

```python
import math

import jax
import jax.numpy as jnp
from jax import lax
from jax.experimental import pallas as pl
from jax.experimental.pallas import tpu as pltpu
from jax.sharding import PartitionSpec as P

H = 0.15
BASE = (2.0 / 60.0, -13.0 / 60.0, 47.0 / 60.0, 27.0 / 60.0, -3.0 / 60.0)
F32 = jnp.float32
BF16 = jnp.bfloat16
NT = (((1,), (1,)), ((), ()))

ROWS_IN = 19
ROWS_OUT = 17
PREV = 5
NEXT = 6

_HBM = pl.BlockSpec(memory_space=pltpu.HBM)


def call(kernel, outs, scratch, args, flops=1e6, follows=()):
    n_in, n_out = len(args), len(outs)

    def run(*refs):
        source, refs = refs[:n_in], refs[n_in + len(follows) :]
        target = refs[:n_out]
        refs = (None,) * n_in + tuple(refs)
        arrived, left = refs[n_in + n_out : n_in + n_out + 2]
        held = refs[n_in + n_out + 2 :]
        here, there = held[:n_in], held[n_in : n_in + n_out]
        coming = {i: pltpu.make_async_copy(source[i], here[i], arrived.at[i]) for i in range(n_in)}
        going = {i: pltpu.make_async_copy(there[i], target[i], left.at[i]) for i in range(n_out)}
        sent = []
        for i in range(n_in):
            coming[i].start()

        def need(*which):
            for i in which:
                coming.pop(i).wait()

        def done(*which):
            for i in which:
                going[i].start()
                sent.append(i)

        kernel(need, done, *held)
        need(*list(coming))
        done(*[i for i in range(n_out) if i not in sent])
        for i in range(n_out):
            going[i].wait()

    return pl.pallas_call(
        run,
        out_shape=[jax.ShapeDtypeStruct(s, t) for s, t in outs],
        in_specs=[_HBM] * (n_in + len(follows)),
        out_specs=[_HBM] * n_out,
        scratch_shapes=[pltpu.SemaphoreType.DMA((n_in,)), pltpu.SemaphoreType.DMA((n_out,))]
        + [pltpu.VMEM(a.shape, a.dtype) for a in args]
        + [pltpu.VMEM(s, t) for s, t in outs]
        + scratch,
        compiler_params=pltpu.CompilerParams(vmem_limit_bytes=64 * 1024 * 1024),
        cost_estimate=pl.CostEstimate(flops=int(flops), bytes_accessed=4000000, transcendentals=0),
    )(*args, *follows)


def call_small(kernel, outs, scratch, args):
    return pl.pallas_call(
        kernel,
        out_shape=[jax.ShapeDtypeStruct(s, t) for s, t in outs],
        in_specs=[pl.BlockSpec(memory_space=pltpu.VMEM)] * len(args),
        out_specs=[pl.BlockSpec(memory_space=pltpu.VMEM)] * len(outs),
        scratch_shapes=scratch,
        compiler_params=pltpu.CompilerParams(vmem_limit_bytes=16 * 1024 * 1024),
        cost_estimate=pl.CostEstimate(flops=1000000, bytes_accessed=4000000, transcendentals=0),
    )(*args)


def shift_both():
    i = lax.broadcasted_iota(jnp.int32, (128, 256), 0)
    j = lax.broadcasted_iota(jnp.int32, (128, 256), 1)
    source = jnp.where(j < 128, j + 127, j + 1) % 128
    return jnp.where(i == source, 1.0, 0.0).astype(BF16)


def roll(value, shift, axis):
    shift %= value.shape[axis]
    return value if shift == 0 else pltpu.roll(value, shift, axis)


def split(plane):
    lead = plane.astype(BF16).astype(F32)
    return jnp.concatenate([lead, plane - lead], axis=0).astype(BF16)


def join(tile):
    both = tile.astype(F32)
    return both[:8] + both[8:]


ORDER = [
    ("l", 3), (0, 3), (1, 3), (2, 3), ("u", 3), ("u", 1), ("u", 2), ("u", 0), ("l", 0), ("l", 1),
    (0, 0), (1, 0), (2, 0), ("l", 2), (0, 1), (0, 2), (1, 1), (1, 2), (2, 1), (2, 2),
]
UP, DOWN = (0, 7), (5, 13)


def pack_y(
    need, done, feat, field, vel, cot, own_feat, own_fields, to_next, to_prev, turn
):
    need(0)
    for c in range(16):
        turn[pl.ds(c, 32, stride=16), :] = feat[c].astype(F32)
    for zy in range(32):
        tile = turn[zy * 16 : (zy + 1) * 16, :].astype(BF16)
        own_feat[zy] = tile
        z, y = divmod(zy, 8)
        if y >= 8 - PREV:
            to_next[z * PREV + y - (8 - PREV)] = tile
        if y < NEXT:
            to_prev[z * NEXT + y] = tile
    need(1, 2, 3)
    for i, (kind, z) in enumerate(ORDER):
        tile = split(field[z] if kind == "u" else cot[z] if kind == "l" else vel[kind, z])
        own_fields[i] = tile
        to_next[4 * PREV + i] = tile
        to_prev[4 * NEXT + i] = tile


def pack_z(own_feat, own_fields, before, after, to_up, to_down, up, down, moved, left):
    copies = []

    def move(source, at, out, to, count):
        copies.append(
            pltpu.make_async_copy(
                source.at[at : at + count], out.at[to : to + count], moved.at[len(copies)]
            )
        )

    for out, z, (first, stop) in ((up, 3, UP), (down, 0, DOWN)):
        n = stop - first
        move(before, z * PREV, out, 0, PREV)
        move(own_feat, z * 8, out, PREV, 8)
        move(after, z * NEXT, out, PREV + 8, NEXT)
        move(before, 4 * PREV + first, out, ROWS_IN, n)
        move(own_fields, first, out, ROWS_IN + n, n)
        move(after, 4 * NEXT + first, out, ROWS_IN + 2 * n, n)
    for copy in copies:
        copy.start()
    out_up = pltpu.make_async_copy(up, to_up, left.at[0])
    out_down = pltpu.make_async_copy(down, to_down, left.at[1])
    for copy in copies[:6]:
        copy.wait()
    out_up.start()
    for copy in copies[6:]:
        copy.wait()
    out_down.start()
    out_up.wait()
    out_down.wait()


def fill_columns(columns, shifted, z, rows):
    for a in range(3):
        for b in range(3):
            at = pl.multiple_of(z * 144 + (a * 3 + b) * 16, 16)
            for y in range(rows):
                columns[pl.ds(at, 16), y * 128 : (y + 1) * 128] = shifted[
                    b, z, (y + a) * 16 : (y + a + 1) * 16, :
                ]


U0, LAM2, U1, LAM1, FACE = slice(0, 10), slice(10, 17), slice(35, 39), slice(39, 47), 47
VEL = (slice(17, 23), slice(23, 29), slice(29, 35))
FAR = [(2, 2), (3, 1), (3, 2), (1, -2), (0, -1), (0, -2)]


def stage_one(
    need, done, own_feat, before, after, below, above, field, vel, cot, w_rows,
    send_up, send_down, send_far, columns_own, coef, kept,
    shifted, columns,
):
    u0, lam2 = kept.at[U0], kept.at[LAM2]
    velx = [kept.at[v] for v in VEL]
    shift_value = shift_both()
    need(0, 1, 2, 3, 4)
    for z in range(6):
        if z == 0:
            tiles = below[0:ROWS_IN].reshape(ROWS_IN * 16, 128)
        elif z == 5:
            tiles = above[0:ROWS_IN].reshape(ROWS_IN * 16, 128)
        else:
            p = z - 1
            tiles = jnp.concatenate(
                [
                    before[p * PREV : (p + 1) * PREV].reshape(PREV * 16, 128),
                    own_feat[p * 8 : (p + 1) * 8].reshape(128, 128),
                    after[p * NEXT : (p + 1) * NEXT].reshape(NEXT * 16, 128),
                ],
                axis=0,
            )
        shifted[1, z] = tiles
        both = jnp.dot(tiles, shift_value, preferred_element_type=F32).astype(BF16)
        shifted[0, z] = both[:, :128]
        shifted[2, z] = both[:, 128:]

    need(5, 6, 7)

    def extended(kind, z, own):
        i = ORDER.index((kind, z))
        return jnp.concatenate(
            [join(before[4 * PREV + i]), own, join(after[4 * NEXT + i])], axis=0
        )

    def received(source, part, kind, z):
        n = part[1] - part[0]
        at = ROWS_IN + ORDER.index((kind, z)) - part[0]
        return jnp.concatenate([join(source[at + n * j]) for j in range(3)], axis=0)

    for j in range(3):
        u0[j] = received(below, UP, "u", 1 + j)
        u0[7 + j] = received(above, DOWN, "u", j)
        velx[j][0] = received(below, UP, j, 3)
        velx[j][5] = received(above, DOWN, j, 0)
    lam2[0] = received(below, UP, "l", 3)
    lam2[5] = received(above, DOWN, "l", 0)
    lam2[6] = received(above, DOWN, "l", 1)
    for z in range(4):
        u0[3 + z] = extended("u", z, field[z])
        lam2[1 + z] = extended("l", z, cot[z])
        for d in range(3):
            velx[d][1 + z] = extended(d, z, vel[d, z])

    def fill(z, carry):
        fill_columns(columns, shifted, z, ROWS_OUT)
        return carry

    lax.fori_loop(0, 6, fill, 0)

    columns_own[...] = columns[:, 512:1536]
    done(3)
    need(8)
    w_value = w_rows[...]
    for p in range(4):
        plane = jnp.dot(
            w_value, columns[p * 144 : p * 144 + 432, :], preferred_element_type=F32
        )
        for y in range(ROWS_OUT):
            coef[p, (4 + y) * 16 : (5 + y) * 16, :] = plane[:, y * 128 : (y + 1) * 128]

    done(4)

    def a(p, k):
        value = coef[p, pl.ds(k, 24, stride=16), :]
        return value + BASE[k % 5]

    pushed = [None] * 8

    def push(slot, value):
        pushed[slot] = value if pushed[slot] is None else pushed[slot] + value

    faces_z = []
    states = []
    carried = {}
    for p in range(4):
        rate = 1.0 + H * coef[p, pl.ds(15, 24, stride=16), :]
        u = u0[3 + p]
        lam = lam2[1 + p]
        state = u * rate
        push(p + 2, lam * rate)
        for d in range(3):
            beyond = lam2[2 + p] if d == 0 else roll(lam, -1, d - 1)
            drive = (-H) * (lam - beyond) * velx[d][1 + p]
            face = None
            for s in range(-2, 3):
                weight = a(p, 5 * d + s + 2)
                term = weight * (u0[3 + p + s] if d == 0 else roll(u, -s, d - 1))
                face = term if face is None else face + term
                back = drive * weight
                if d == 0:
                    push(p + 2 + s, back)
                    if (p, s) in FAR:
                        carried[p, s] = velx[0][1 + p] * weight
                else:
                    push(p + 2, roll(back, s, d - 1))
            face = (H * velx[d][1 + p]) * face
            if d == 0:
                faces_z.append(face)
                state = state - (face if p == 0 else face - faces_z[p - 1])
            else:
                state = state - (face - roll(face, 1, d - 1))
        states.append(state)
    u1_part, lam_part = kept.at[U1], kept.at[LAM1]
    for p in range(4):
        u1_part[p] = states[p]
    for j in range(8):
        lam_part[j] = pushed[j]
    kept[FACE] = faces_z[3]
    ups = [states[1], states[2], states[3], faces_z[3], pushed[5], pushed[6], pushed[7], pushed[4]]
    downs = [states[0], states[1], states[2], pushed[2], pushed[3], pushed[0], pushed[1], pushed[4]]
    for j in range(8):
        send_up[j] = ups[j][4:20]
        send_down[j] = downs[j][4:20]
    for out, keys in ((send_up, FAR[:3]), (send_down, FAR[3:])):
        out[8, 0:8, :] = carried[keys[0]][8:16]
        out[8, 8:16, :] = carried[keys[1]][8:16]
        out[9, 0:8, :] = carried[keys[2]][8:16]
        out[9, 8:16, :] = carried[keys[2]][8:16]
    send_far[...] = pushed[0][8:16]


def patch_gram(need, done, columns_own, gram):
    need(0)
    total = None
    for p in range(4):
        part = lax.dot_general(
            columns_own[p * 144 : (p + 1) * 144, :],
            columns_own[p * 144 + 48 : p * 144 + 432, :],
            NT,
            preferred_element_type=F32,
        )
        total = part if total is None else total + part
    for t in range(3):
        gram[t * 144 : (t + 1) * 144, :] = total[:, t * 128 : (t + 1) * 128]
    gram[432:, :] = jnp.zeros((gram.shape[0] - 432, 128), F32)


def stage_two(
    need, done, below, above, far, state, coef, columns_own,
    grad_w, tiles, lam0,
    u1, lam1, turn, row,
):
    u0, lam2, u1_part, lam_part = state.at[U0], state.at[LAM2], state.at[U1], state.at[LAM1]
    velx = [state.at[v] for v in VEL]
    need(0, 1, 2, 3, 4)

    def padded(value):
        zero = jnp.zeros((4, 128), F32)
        return jnp.concatenate([zero, value, zero], axis=0)

    low = [padded(below[j]) for j in range(8)]
    high = [padded(above[j]) for j in range(8)]
    for j in range(3):
        u1[j] = low[j]
        u1[7 + j] = high[j] + (state[FACE] if j == 0 else 0.0)
        u1[4 + j] = u1_part[1 + j]
    u1[3] = u1_part[0] + low[3]
    lam1[0] = low[4] + lam_part[1]
    lam1[1] = lam_part[2] + low[5]
    lam1[2] = lam_part[3] + low[6]
    lam1[3] = lam_part[4] + high[5]
    lam1[4] = lam_part[5] + high[6]
    lam1[5] = high[3] + lam_part[6]
    lam1[6] = high[4] + lam_part[7]

    pushed = [None] * 8

    def push(slot, value):
        pushed[slot] = value if pushed[slot] is None else pushed[slot] + value

    own_rows = slice(8, 16)
    lowest = lam_part[0][own_rows] + low[7][own_rows]
    highest = high[7][own_rows] + far[...]
    fall = [lowest, lam1[0, own_rows], lam1[1, own_rows]]
    rise = [lam1[5, own_rows], lam1[6, own_rows], highest]
    outer = [(-H) * (fall[0] - fall[1]), (-H) * (fall[1] - fall[2])]
    inner = [(-H) * (rise[0] - rise[1]), (-H) * (rise[1] - rise[2])]
    edge = [
        outer[0] * below[8, 0:8, :] + outer[1] * below[8, 8:16, :],
        outer[1] * below[9, 0:8, :],
        inner[0] * above[9, 0:8, :],
        inner[0] * above[8, 8:16, :] + inner[1] * above[8, 0:8, :],
    ]

    for z in range(6):
        later, first = lam2[z], lam1[z]
        v, u = u1[z + 2], u0[z + 2]
        own = 1 <= z <= 4
        p = z - 1
        if own:
            push(z + 1, first * (1.0 + H * coef[p, pl.ds(15, 24, stride=16), :]))
        for d in range(3):
            speed = velx[d][z]
            beyond_later = lam2[z + 1] if d == 0 else roll(later, -1, d - 1)
            beyond_first = lam1[z + 1] if d == 0 else roll(first, -1, d - 1)
            drive_later = (-H) * (later - beyond_later) * speed
            drive_first = (-H) * (first - beyond_first) * speed
            for s in range(-2, 3):
                k = 5 * d + s + 2
                there_later = u1[z + 2 + s] if d == 0 else roll(v, -s, d - 1)
                there_first = u0[z + 2 + s] if d == 0 else roll(u, -s, d - 1)
                turn[z, pl.ds(k, 24, stride=16), :] = (
                    drive_later * there_later + drive_first * there_first
                )
                if own:
                    back = drive_first * (coef[p, pl.ds(k, 24, stride=16), :] + BASE[s + 2])
                    if d == 0:
                        push(z + 1 + s, back)
                    else:
                        push(z + 1, roll(back, s, d - 1))
        turn[z, pl.ds(15, 24, stride=16), :] = H * later * v + H * first * u
    for p in range(4):
        lam0[p] = pushed[2 + p][own_rows] + edge[p]
    done(2)

    for z in range(6):
        tiles[z] = turn[z, 7 * 16 : 17 * 16, :].astype(BF16)
    done(1)
    need(5)
    sum_w = None
    sum_g = None
    for p in range(4):
        mine = jnp.concatenate(
            [tiles[p + 1, (y + 1) * 16 : (y + 2) * 16, :] for y in range(8)], axis=1
        )
        part_w = lax.dot_general(
            mine, columns_own[p * 144 : p * 144 + 432, :], NT, preferred_element_type=F32
        )
        part_g = lax.dot_general(mine, mine, NT, preferred_element_type=F32)
        sum_w = part_w if sum_w is None else sum_w + part_w
        sum_g = part_g if sum_g is None else sum_g + part_g
    row[...] = jnp.zeros((16, 512), F32)
    row[:, 0:432] = sum_w
    row[:, 432:448] = sum_g
    for t in range(4):
        grad_w[t * 16 : (t + 1) * 16, :] = row[:, t * 128 : (t + 1) * 128]


def stage_three(need, done, tiles, w_back, grad_feat, shifted, columns, turn_out):
    need(0)
    shift_value = shift_both()
    for z in range(6):
        shifted[1, z] = tiles[z]
        both = jnp.dot(tiles[z], shift_value, preferred_element_type=F32).astype(BF16)
        shifted[0, z] = both[:, :128]
        shifted[2, z] = both[:, 128:]

    def fill(z, carry):
        fill_columns(columns, shifted, z, 8)
        return carry

    lax.fori_loop(0, 6, fill, 0)
    need(1)
    w_value = w_back[...]
    for p in range(4):
        plane = jnp.dot(
            w_value, columns[p * 144 : p * 144 + 432, :], preferred_element_type=F32
        )
        for y in range(8):
            turn_out[pl.ds(p * 8 + y, 16, stride=32), :] = plane[:, y * 128 : (y + 1) * 128]
    for c in range(16):
        grad_feat[c] = turn_out[c * 32 : (c + 1) * 32, :].astype(BF16)


def pieces(value):
    one = value.astype(BF16)
    rest = value - one.astype(F32)
    two = rest.astype(BF16)
    three = (rest - two.astype(F32)).astype(BF16)
    return one, two, three


def to_channel_major(value):
    i = lax.broadcasted_iota(jnp.int32, (432, 432), 0)
    j = lax.broadcasted_iota(jnp.int32, (432, 432), 1)
    place = jnp.where((i % 16) * 27 + i // 16 == j, 1.0, 0.0).astype(BF16)
    parts = [jnp.dot(v, place, preferred_element_type=F32) for v in pieces(value)]
    return parts[2] + parts[1] + parts[0]


def finish_gram(scale, chunks, out, square, block, turn):
    for t in range(3):
        square[0:144, 48 + t * 128 : 48 + (t + 1) * 128] = chunks[t * 144 : (t + 1) * 144, :] * scale
    square[0:48, 0:48] = square[48:96, 48:96]
    block[...] = jnp.zeros((256, 256), F32)
    block[0:48, 0:96] = square[0:48, 48:144]
    square[48:144, 0:48] = jnp.transpose(block[...])[0:96, 0:48]
    square[144:288, 144:432] = square[0:144, 0:288]
    square[288:432, 288:432] = square[0:144, 0:144]
    block[0:144, 0:144] = square[0:144, 144:288]
    turned = jnp.transpose(block[...])[0:144, 0:144]
    square[144:288, 0:144] = turned
    square[288:432, 144:288] = turned
    block[0:144, 0:144] = square[0:144, 288:432]
    square[288:432, 0:144] = jnp.transpose(block[...])[0:144, 0:144]
    ready = to_channel_major(square[...])
    for t in range(4):
        wide = min(128, 432 - t * 128)
        for o in range(27):
            turn[t, pl.ds(o, 16, stride=27), 0:wide] = ready[
                o * 16 : (o + 1) * 16, t * 128 : t * 128 + wide
            ]
        out[:, t * 128 : t * 128 + wide] = turn[t, :, 0:wide]


def finish_weight(scale_w, scale_g, chunks, out_w, out_g, row):
    for t in range(4):
        row[:, t * 128 : (t + 1) * 128] = chunks[t * 16 : (t + 1) * 16, :]
    out_w[...] = to_channel_major(row[:, 0:432] * scale_w)
    out_g[...] = row[:, 432:448] * scale_g


def neighbours(to_next, to_prev, axis):
    size = lax.axis_size(axis)
    up = [(i, (i + 1) % size) for i in range(size)]
    down = [(j, i) for i, j in up]
    return lax.ppermute(to_next, axis, up), lax.ppermute(to_prev, axis, down)


def body(features, field, velocity, weight, cotangent):
    nz, ny = lax.axis_size("gz"), lax.axis_size("gy")
    cells = float(4096 * nz * ny)
    by_offset = weight.reshape(16, 16, 27)
    w_rows = by_offset.transpose(0, 2, 1).reshape(16, 432)
    w_back = by_offset.transpose(1, 2, 0)[:, ::-1, :].reshape(16, 432)
    tile = (16, 128)
    own_feat, own_fields, to_next, to_prev = call(
        pack_y,
        [((32,) + tile, BF16), ((20,) + tile, BF16), ((4 * PREV + 20,) + tile, BF16),
         ((4 * NEXT + 20,) + tile, BF16)],
        [pltpu.VMEM((512, 128), F32)],
        (features.reshape(16, 32, 128), field, velocity, cotangent),
    )
    before, after = neighbours(to_next, to_prev, "gy")
    to_up, to_down = pl.pallas_call(
        pack_z,
        out_shape=[
            jax.ShapeDtypeStruct((ROWS_IN + 3 * (stop - first),) + tile, BF16)
            for first, stop in (UP, DOWN)
        ],
        in_specs=[_HBM] * 4,
        out_specs=[_HBM] * 2,
        scratch_shapes=[
            pltpu.VMEM((ROWS_IN + 3 * (stop - first),) + tile, BF16) for first, stop in (UP, DOWN)
        ]
        + [pltpu.SemaphoreType.DMA((12,)), pltpu.SemaphoreType.DMA((2,))],
        compiler_params=pltpu.CompilerParams(vmem_limit_bytes=64 * 1024 * 1024),
    )(own_feat, own_fields, before, after)
    below, above = neighbours(to_up, to_down, "gz")
    send_up, send_down, send_far, columns_own, coef, state = call(
        stage_one,
        [((10, 16, 128), F32), ((10, 16, 128), F32), ((8, 128), F32), ((864, 1024), BF16),
         ((4, 384, 128), F32), ((48, 24, 128), F32)],
        [pltpu.VMEM((3, 6, ROWS_IN * 16, 128), BF16), pltpu.VMEM((864, ROWS_OUT * 128), BF16)],
        (own_feat, before, after, below, above, field, velocity, cotangent, w_rows),
    )
    below1, above1 = neighbours(send_up, send_down, "gz")
    far = lax.ppermute(send_far, "gz", [((i + 2) % nz, i) for i in range(nz)])
    (gram,) = call(patch_gram, [((512, 128), F32)], [], (columns_own,), 5e8)
    gram_parts = lax.all_to_all(gram.reshape(nz, 512 // nz, 128), "gz", 0, 0)
    gram_sum = jnp.sum(gram_parts, axis=0)
    grad_w, tiles, grad_field = call(
        stage_two,
        [((64, 128), F32), ((6, 160, 128), BF16), ((4, 8, 128), F32)],
        [pltpu.VMEM((10, 24, 128), F32), pltpu.VMEM((7, 24, 128), F32),
         pltpu.VMEM((6, 384, 128), F32), pltpu.VMEM((16, 512), F32)],
        (below1, above1, far, state, coef, columns_own),
    )
    wr, gr = 64 // ny, 512 // nz
    mixed = jnp.concatenate(
        [grad_w.reshape(ny, wr, 128), jnp.broadcast_to(gram_sum[None], (ny, gr, 128))], axis=1
    )
    (grad_feat,) = call(
        stage_three,
        [((16, 32, 128), BF16)],
        [pltpu.VMEM((3, 6, 160, 128), BF16), pltpu.VMEM((864, 1024), BF16), pltpu.VMEM((512, 128), F32)],
        (tiles, w_back),
        1e8,
        (mixed,),
    )
    mixed = jnp.sum(lax.all_to_all(mixed, "gy", 0, 0), axis=0)
    everyone = lax.all_to_all(jnp.broadcast_to(mixed[None], (nz, wr + gr, 128)), "gz", 0, 0)
    weight_sum = jnp.sum(everyone[:, :wr], axis=0)
    weight_all = lax.all_to_all(jnp.broadcast_to(weight_sum[None], (ny, wr, 128)), "gy", 0, 0)
    (factor_patch,) = call_small(
        lambda *refs: finish_gram(1.0 / cells, *refs),
        [((432, 432), F32)],
        [pltpu.VMEM((432, 432), F32), pltpu.VMEM((256, 256), F32), pltpu.VMEM((4, 432, 128), F32)],
        (everyone[:, wr:].reshape(512, 128),),
    )
    grad_weight, factor_grad = call_small(
        lambda *refs: finish_weight(1.0 / math.sqrt(cells), 1.0 / cells, *refs),
        [((16, 432), F32), ((16, 16), F32)],
        [pltpu.VMEM((16, 512), F32)],
        (weight_all.reshape(64, 128),),
    )
    return (grad_field, grad_feat.reshape(16, 4, 8, 128), grad_weight, factor_patch, factor_grad)


def solution(mesh):
    placed = (
        P(None, "gz", "gy", None),
        P("gz", "gy", None),
        P(None, "gz", "gy", None),
        P(),
        P("gz", "gy", None),
    )
    return jax.shard_map(
        body,
        mesh=mesh,
        in_specs=placed,
        out_specs=(P("gz", "gy", None), P(None, "gz", "gy", None), P(), P(), P()),
        check_vma=False,
    )
```

```python
import math

import jax
import jax.numpy as jnp
from jax import lax
from jax.experimental import pallas as pl
from jax.experimental.pallas import tpu as pltpu
from jax.sharding import PartitionSpec as P

H = 0.15
BASE = (2.0 / 60.0, -13.0 / 60.0, 47.0 / 60.0, 27.0 / 60.0, -3.0 / 60.0)
F32 = jnp.float32
BF16 = jnp.bfloat16
NT = (((1,), (1,)), ((), ()))

ROWS_IN = 19
ROWS_OUT = 17
PREV = 5
NEXT = 6

_HBM = pl.BlockSpec(memory_space=pltpu.HBM)


def call(kernel, outs, scratch, args, flops=1e6, follows=()):
    n_in, n_out = len(args), len(outs)

    def run(*refs):
        source, refs = refs[:n_in], refs[n_in + len(follows) :]
        target = refs[:n_out]
        refs = (None,) * n_in + tuple(refs)
        arrived, left = refs[n_in + n_out : n_in + n_out + 2]
        held = refs[n_in + n_out + 2 :]
        here, there = held[:n_in], held[n_in : n_in + n_out]
        coming = {i: pltpu.make_async_copy(source[i], here[i], arrived.at[i]) for i in range(n_in)}
        going = {i: pltpu.make_async_copy(there[i], target[i], left.at[i]) for i in range(n_out)}
        sent = []
        for i in range(n_in):
            coming[i].start()

        def need(*which):
            for i in which:
                coming.pop(i).wait()

        def done(*which):
            for i in which:
                going[i].start()
                sent.append(i)

        kernel(need, done, *held)
        need(*list(coming))
        done(*[i for i in range(n_out) if i not in sent])
        for i in range(n_out):
            going[i].wait()

    return pl.pallas_call(
        run,
        out_shape=[jax.ShapeDtypeStruct(s, t) for s, t in outs],
        in_specs=[_HBM] * (n_in + len(follows)),
        out_specs=[_HBM] * n_out,
        scratch_shapes=[pltpu.SemaphoreType.DMA((n_in,)), pltpu.SemaphoreType.DMA((n_out,))]
        + [pltpu.VMEM(a.shape, a.dtype) for a in args]
        + [pltpu.VMEM(s, t) for s, t in outs]
        + scratch,
        compiler_params=pltpu.CompilerParams(vmem_limit_bytes=64 * 1024 * 1024),
        cost_estimate=pl.CostEstimate(flops=int(flops), bytes_accessed=4000000, transcendentals=0),
    )(*args, *follows)


def call_small(kernel, outs, scratch, args):
    return pl.pallas_call(
        kernel,
        out_shape=[jax.ShapeDtypeStruct(s, t) for s, t in outs],
        in_specs=[pl.BlockSpec(memory_space=pltpu.VMEM)] * len(args),
        out_specs=[pl.BlockSpec(memory_space=pltpu.VMEM)] * len(outs),
        scratch_shapes=scratch,
        compiler_params=pltpu.CompilerParams(vmem_limit_bytes=16 * 1024 * 1024),
        cost_estimate=pl.CostEstimate(flops=1000000, bytes_accessed=4000000, transcendentals=0),
    )(*args)


def shift_both():
    i = lax.broadcasted_iota(jnp.int32, (128, 256), 0)
    j = lax.broadcasted_iota(jnp.int32, (128, 256), 1)
    source = jnp.where(j < 128, j + 127, j + 1) % 128
    return jnp.where(i == source, 1.0, 0.0).astype(BF16)


def roll(value, shift, axis):
    shift %= value.shape[axis]
    return value if shift == 0 else pltpu.roll(value, shift, axis)


def split(plane):
    lead = plane.astype(BF16).astype(F32)
    return jnp.concatenate([lead, plane - lead], axis=0).astype(BF16)


def join(tile):
    both = tile.astype(F32)
    return both[:8] + both[8:]


ORDER = [
    ("l", 3), (0, 3), (1, 3), (2, 3), ("u", 3), ("u", 1), ("u", 2), ("u", 0), ("l", 0), ("l", 1),
    (0, 0), (1, 0), (2, 0), ("l", 2), (0, 1), (0, 2), (1, 1), (1, 2), (2, 1), (2, 2),
]
UP, DOWN = (0, 7), (5, 13)


def pack_y(
    need, done, feat, field, vel, cot, own_feat, own_fields, to_next, to_prev, turn
):
    need(0)
    for c in range(16):
        turn[pl.ds(c, 32, stride=16), :] = feat[c].astype(F32)
    for zy in range(32):
        tile = turn[zy * 16 : (zy + 1) * 16, :].astype(BF16)
        own_feat[zy] = tile
        z, y = divmod(zy, 8)
        if y >= 8 - PREV:
            to_next[z * PREV + y - (8 - PREV)] = tile
        if y < NEXT:
            to_prev[z * NEXT + y] = tile
    need(1, 2, 3)
    for i, (kind, z) in enumerate(ORDER):
        tile = split(field[z] if kind == "u" else cot[z] if kind == "l" else vel[kind, z])
        own_fields[i] = tile
        to_next[4 * PREV + i] = tile
        to_prev[4 * NEXT + i] = tile


def pack_z(own_feat, own_fields, before, after, to_up, to_down, up, down, moved, left):
    copies = []

    def move(source, at, out, to, count):
        copies.append(
            pltpu.make_async_copy(
                source.at[at : at + count], out.at[to : to + count], moved.at[len(copies)]
            )
        )

    for out, z, (first, stop) in ((up, 3, UP), (down, 0, DOWN)):
        n = stop - first
        move(before, z * PREV, out, 0, PREV)
        move(own_feat, z * 8, out, PREV, 8)
        move(after, z * NEXT, out, PREV + 8, NEXT)
        move(before, 4 * PREV + first, out, ROWS_IN, n)
        move(own_fields, first, out, ROWS_IN + n, n)
        move(after, 4 * NEXT + first, out, ROWS_IN + 2 * n, n)
    for copy in copies:
        copy.start()
    out_up = pltpu.make_async_copy(up, to_up, left.at[0])
    out_down = pltpu.make_async_copy(down, to_down, left.at[1])
    for copy in copies[:6]:
        copy.wait()
    out_up.start()
    for copy in copies[6:]:
        copy.wait()
    out_down.start()
    out_up.wait()
    out_down.wait()


def fill_columns(columns, shifted, z, rows):
    for a in range(3):
        for b in range(3):
            at = pl.multiple_of(z * 144 + (a * 3 + b) * 16, 16)
            for y in range(rows):
                columns[pl.ds(at, 16), y * 128 : (y + 1) * 128] = shifted[
                    b, z, (y + a) * 16 : (y + a + 1) * 16, :
                ]


U0, LAM2, U1, LAM1, FACE = slice(0, 10), slice(10, 17), slice(35, 39), slice(39, 47), 47
VEL = (slice(17, 23), slice(23, 29), slice(29, 35))
FAR = [(2, 2), (3, 1), (3, 2), (1, -2), (0, -1), (0, -2)]


def stage_one(
    need, done, own_feat, before, after, below, above, field, vel, cot, w_rows,
    send_up, send_down, send_far, columns_own, coef, kept,
    shifted, columns,
):
    u0, lam2 = kept.at[U0], kept.at[LAM2]
    velx = [kept.at[v] for v in VEL]
    shift_value = shift_both()
    need(0, 1, 2, 3, 4)
    for z in range(6):
        if z == 0:
            tiles = below[0:ROWS_IN].reshape(ROWS_IN * 16, 128)
        elif z == 5:
            tiles = above[0:ROWS_IN].reshape(ROWS_IN * 16, 128)
        else:
            p = z - 1
            tiles = jnp.concatenate(
                [
                    before[p * PREV : (p + 1) * PREV].reshape(PREV * 16, 128),
                    own_feat[p * 8 : (p + 1) * 8].reshape(128, 128),
                    after[p * NEXT : (p + 1) * NEXT].reshape(NEXT * 16, 128),
                ],
                axis=0,
            )
        shifted[1, z] = tiles
        both = jnp.dot(tiles, shift_value, preferred_element_type=F32).astype(BF16)
        shifted[0, z] = both[:, :128]
        shifted[2, z] = both[:, 128:]

    need(5, 6, 7)

    def extended(kind, z, own):
        i = ORDER.index((kind, z))
        return jnp.concatenate(
            [join(before[4 * PREV + i]), own, join(after[4 * NEXT + i])], axis=0
        )

    def received(source, part, kind, z):
        n = part[1] - part[0]
        at = ROWS_IN + ORDER.index((kind, z)) - part[0]
        return jnp.concatenate([join(source[at + n * j]) for j in range(3)], axis=0)

    for j in range(3):
        u0[j] = received(below, UP, "u", 1 + j)
        u0[7 + j] = received(above, DOWN, "u", j)
        velx[j][0] = received(below, UP, j, 3)
        velx[j][5] = received(above, DOWN, j, 0)
    lam2[0] = received(below, UP, "l", 3)
    lam2[5] = received(above, DOWN, "l", 0)
    lam2[6] = received(above, DOWN, "l", 1)
    for z in range(4):
        u0[3 + z] = extended("u", z, field[z])
        lam2[1 + z] = extended("l", z, cot[z])
        for d in range(3):
            velx[d][1 + z] = extended(d, z, vel[d, z])

    def fill(z, carry):
        fill_columns(columns, shifted, z, ROWS_OUT)
        return carry

    lax.fori_loop(0, 6, fill, 0)

    columns_own[...] = columns[:, 512:1536]
    done(3)
    need(8)
    w_value = w_rows[...]
    for p in range(4):
        plane = jnp.dot(
            w_value, columns[p * 144 : p * 144 + 432, :], preferred_element_type=F32
        )
        for y in range(ROWS_OUT):
            coef[p, (4 + y) * 16 : (5 + y) * 16, :] = plane[:, y * 128 : (y + 1) * 128]

    done(4)

    def a(p, k):
        value = coef[p, pl.ds(k, 24, stride=16), :]
        return value + BASE[k % 5]

    pushed = [None] * 8

    def push(slot, value):
        pushed[slot] = value if pushed[slot] is None else pushed[slot] + value

    faces_z = []
    states = []
    carried = {}
    for p in range(4):
        rate = 1.0 + H * coef[p, pl.ds(15, 24, stride=16), :]
        u = u0[3 + p]
        lam = lam2[1 + p]
        state = u * rate
        push(p + 2, lam * rate)
        for d in range(3):
            beyond = lam2[2 + p] if d == 0 else roll(lam, -1, d - 1)
            drive = (-H) * (lam - beyond) * velx[d][1 + p]
            face = None
            for s in range(-2, 3):
                weight = a(p, 5 * d + s + 2)
                term = weight * (u0[3 + p + s] if d == 0 else roll(u, -s, d - 1))
                face = term if face is None else face + term
                back = drive * weight
                if d == 0:
                    push(p + 2 + s, back)
                    if (p, s) in FAR:
                        carried[p, s] = velx[0][1 + p] * weight
                else:
                    push(p + 2, roll(back, s, d - 1))
            face = (H * velx[d][1 + p]) * face
            if d == 0:
                faces_z.append(face)
                state = state - (face if p == 0 else face - faces_z[p - 1])
            else:
                state = state - (face - roll(face, 1, d - 1))
        states.append(state)
    u1_part, lam_part = kept.at[U1], kept.at[LAM1]
    for p in range(4):
        u1_part[p] = states[p]
    for j in range(8):
        lam_part[j] = pushed[j]
    kept[FACE] = faces_z[3]
    ups = [states[1], states[2], states[3], faces_z[3], pushed[5], pushed[6], pushed[7], pushed[4]]
    downs = [states[0], states[1], states[2], pushed[2], pushed[3], pushed[0], pushed[1], pushed[4]]
    for j in range(8):
        send_up[j] = ups[j][4:20]
        send_down[j] = downs[j][4:20]
    for out, keys in ((send_up, FAR[:3]), (send_down, FAR[3:])):
        out[8, 0:8, :] = carried[keys[0]][8:16]
        out[8, 8:16, :] = carried[keys[1]][8:16]
        out[9, 0:8, :] = carried[keys[2]][8:16]
        out[9, 8:16, :] = carried[keys[2]][8:16]
    send_far[...] = pushed[0][8:16]


def patch_gram(need, done, columns_own, gram, full, line):
    need(0)
    total = None
    for p in range(4):
        part = lax.dot_general(
            columns_own[p * 144 : (p + 1) * 144, :],
            columns_own[p * 144 : p * 144 + 432, :],
            NT,
            preferred_element_type=F32,
        )
        total = part if total is None else total + part
    full[:, 0:432] = total
    line[...] = jnp.zeros((16, 1280), F32)

    def put(dz, dy, dx, count, a, b, a_other):
        to = dz * 400 + (dy + 2) * 80 + (dx + 2) * 16
        at = dz * 144 + a_other * 48
        group = (a * 3 + b) * 16
        line[:, to : to + 16 * count] = full[group : group + 16, at : at + 16 * count]

    for dz in range(3):
        for a in range(3):
            put(dz, a, 0, 3, 0, 0, a)
            for b in (1, 2):
                put(dz, a, -b, 1, 0, b, a)
        for a in (1, 2):
            put(dz, -a, 0, 3, a, 0, 0)
            for b in (1, 2):
                put(dz, -a, -b, 1, a, b, 0)
    for t in range(10):
        gram[t * 16 : (t + 1) * 16, :] = line[:, t * 128 : (t + 1) * 128]
    gram[160:192, :] = jnp.zeros((32, 128), F32)


def stage_two(
    need, done, below, above, far, state, coef, columns_own, gram,
    mixed, tiles, lam0,
    u1, lam1, turn, row,
):
    u0, lam2, u1_part, lam_part = state.at[U0], state.at[LAM2], state.at[U1], state.at[LAM1]
    velx = [state.at[v] for v in VEL]
    need(0, 1, 2, 3, 4)

    def padded(value):
        zero = jnp.zeros((4, 128), F32)
        return jnp.concatenate([zero, value, zero], axis=0)

    low = [padded(below[j]) for j in range(8)]
    high = [padded(above[j]) for j in range(8)]
    for j in range(3):
        u1[j] = low[j]
        u1[7 + j] = high[j] + (state[FACE] if j == 0 else 0.0)
        u1[4 + j] = u1_part[1 + j]
    u1[3] = u1_part[0] + low[3]
    lam1[0] = low[4] + lam_part[1]
    lam1[1] = lam_part[2] + low[5]
    lam1[2] = lam_part[3] + low[6]
    lam1[3] = lam_part[4] + high[5]
    lam1[4] = lam_part[5] + high[6]
    lam1[5] = high[3] + lam_part[6]
    lam1[6] = high[4] + lam_part[7]

    pushed = [None] * 8

    def push(slot, value):
        pushed[slot] = value if pushed[slot] is None else pushed[slot] + value

    own_rows = slice(8, 16)
    lowest = lam_part[0][own_rows] + low[7][own_rows]
    highest = high[7][own_rows] + far[...]
    fall = [lowest, lam1[0, own_rows], lam1[1, own_rows]]
    rise = [lam1[5, own_rows], lam1[6, own_rows], highest]
    outer = [(-H) * (fall[0] - fall[1]), (-H) * (fall[1] - fall[2])]
    inner = [(-H) * (rise[0] - rise[1]), (-H) * (rise[1] - rise[2])]
    edge = [
        outer[0] * below[8, 0:8, :] + outer[1] * below[8, 8:16, :],
        outer[1] * below[9, 0:8, :],
        inner[0] * above[9, 0:8, :],
        inner[0] * above[8, 8:16, :] + inner[1] * above[8, 0:8, :],
    ]

    for z in range(6):
        later, first = lam2[z], lam1[z]
        v, u = u1[z + 2], u0[z + 2]
        own = 1 <= z <= 4
        p = z - 1
        if own:
            push(z + 1, first * (1.0 + H * coef[p, pl.ds(15, 24, stride=16), :]))
        for d in range(3):
            speed = velx[d][z]
            beyond_later = lam2[z + 1] if d == 0 else roll(later, -1, d - 1)
            beyond_first = lam1[z + 1] if d == 0 else roll(first, -1, d - 1)
            drive_later = (-H) * (later - beyond_later) * speed
            drive_first = (-H) * (first - beyond_first) * speed
            for s in range(-2, 3):
                k = 5 * d + s + 2
                there_later = u1[z + 2 + s] if d == 0 else roll(v, -s, d - 1)
                there_first = u0[z + 2 + s] if d == 0 else roll(u, -s, d - 1)
                turn[z, pl.ds(k, 24, stride=16), :] = (
                    drive_later * there_later + drive_first * there_first
                )
                if own:
                    back = drive_first * (coef[p, pl.ds(k, 24, stride=16), :] + BASE[s + 2])
                    if d == 0:
                        push(z + 1 + s, back)
                    else:
                        push(z + 1, roll(back, s, d - 1))
        turn[z, pl.ds(15, 24, stride=16), :] = H * later * v + H * first * u
    for p in range(4):
        lam0[p] = pushed[2 + p][own_rows] + edge[p]
    done(2)

    for z in range(6):
        tiles[z] = turn[z, 7 * 16 : 17 * 16, :].astype(BF16)
    done(1)
    need(5)
    sum_w = None
    sum_g = None
    for p in range(4):
        mine = jnp.concatenate(
            [tiles[p + 1, (y + 1) * 16 : (y + 2) * 16, :] for y in range(8)], axis=1
        )
        part_w = lax.dot_general(
            mine, columns_own[p * 144 : p * 144 + 432, :], NT, preferred_element_type=F32
        )
        part_g = lax.dot_general(mine, mine, NT, preferred_element_type=F32)
        sum_w = part_w if sum_w is None else sum_w + part_w
        sum_g = part_g if sum_g is None else sum_g + part_g
    row[...] = jnp.zeros((16, 512), F32)
    row[:, 0:432] = sum_w
    row[:, 432:448] = sum_g
    parts = mixed.shape[0]
    wr, gr = 64 // parts, 192 // parts
    for r in range(0, 64, 8):
        t, half = divmod(r, 16)
        mixed[r // wr, r % wr : r % wr + 8, :] = row[half : half + 8, t * 128 : (t + 1) * 128]
    need(6)
    for n in range(parts):
        mixed[n, wr : wr + gr, :] = gram[n * gr : (n + 1) * gr, :]


def stage_three(need, done, tiles, w_back, grad_feat, shifted, columns, turn_out):
    need(0)
    shift_value = shift_both()
    for z in range(6):
        shifted[1, z] = tiles[z]
        both = jnp.dot(tiles[z], shift_value, preferred_element_type=F32).astype(BF16)
        shifted[0, z] = both[:, :128]
        shifted[2, z] = both[:, 128:]

    def fill(z, carry):
        fill_columns(columns, shifted, z, 8)
        return carry

    lax.fori_loop(0, 6, fill, 0)
    need(1)
    w_value = w_back[...]
    for p in range(4):
        plane = jnp.dot(
            w_value, columns[p * 144 : p * 144 + 432, :], preferred_element_type=F32
        )
        for y in range(8):
            turn_out[pl.ds(p * 8 + y, 16, stride=32), :] = plane[:, y * 128 : (y + 1) * 128]
    for c in range(16):
        grad_feat[c] = turn_out[c * 32 : (c + 1) * 32, :].astype(BF16)


def pieces(value):
    one = value.astype(BF16)
    rest = value - one.astype(F32)
    two = rest.astype(BF16)
    three = (rest - two.astype(F32)).astype(BF16)
    return one, two, three


def to_channel_major(value):
    i = lax.broadcasted_iota(jnp.int32, (432, 432), 0)
    j = lax.broadcasted_iota(jnp.int32, (432, 432), 1)
    place = jnp.where((i % 16) * 27 + i // 16 == j, 1.0, 0.0).astype(BF16)
    parts = [jnp.dot(v, place, preferred_element_type=F32) for v in pieces(value)]
    return parts[2] + parts[1] + parts[0]


def total_to_all(parts, out):
    total = parts[0]
    for n in range(1, parts.shape[0]):
        total = total + parts[n]
    for n in range(out.shape[0]):
        out[n] = total


def finish(cells, chunks, out_w, out_p, out_g, line, row, square, block, turn):
    parts = chunks.shape[0]
    wr, gr = 64 // parts, 192 // parts
    for r in range(0, 64, 8):
        t, half = divmod(r, 16)
        row[half : half + 8, t * 128 : (t + 1) * 128] = chunks[r // wr, r % wr : r % wr + 8, :]
    for r in range(0, 160, 8):
        t, half = divmod(r, 16)
        line[half : half + 8, t * 128 : (t + 1) * 128] = chunks[
            r // gr, wr + r % gr : wr + r % gr + 8, :
        ] * (1.0 / cells)
    out_g[...] = row[:, 432:448] * (1.0 / cells)
    for dz in range(3):
        for a in range(3):
            for b in range(3):
                group = (a * 3 + b) * 16
                for a_other in range(3):
                    to = dz * 144 + a_other * 48
                    at = dz * 400 + (a_other - a + 2) * 80 + (2 - b) * 16
                    square[group : group + 16, to : to + 48] = line[:, at : at + 48]
    square[144:288, 144:432] = square[0:144, 0:288]
    square[288:432, 288:432] = square[0:144, 0:144]
    block[...] = jnp.zeros((256, 256), F32)
    block[0:144, 0:144] = square[0:144, 144:288]
    turned = jnp.transpose(block[...])[0:144, 0:144]
    square[144:288, 0:144] = turned
    square[288:432, 144:288] = turned
    block[0:144, 0:144] = square[0:144, 288:432]
    square[288:432, 0:144] = jnp.transpose(block[...])[0:144, 0:144]
    square[432:448, :] = row[:, 0:432] * (1.0 / math.sqrt(cells))
    ready = to_channel_major(square[...])
    out_w[...] = ready[432:448, :]
    for t in range(4):
        wide = min(128, 432 - t * 128)
        for o in range(27):
            turn[t, pl.ds(o, 16, stride=27), 0:wide] = ready[
                o * 16 : (o + 1) * 16, t * 128 : t * 128 + wide
            ]
        out_p[:, t * 128 : t * 128 + wide] = turn[t, :, 0:wide]


def neighbours(to_next, to_prev, axis):
    size = lax.axis_size(axis)
    up = [(i, (i + 1) % size) for i in range(size)]
    down = [(j, i) for i, j in up]
    return lax.ppermute(to_next, axis, up), lax.ppermute(to_prev, axis, down)


def body(features, field, velocity, weight, cotangent):
    nz, ny = lax.axis_size("gz"), lax.axis_size("gy")
    cells = float(4096 * nz * ny)
    by_offset = weight.reshape(16, 16, 27)
    w_rows = by_offset.transpose(0, 2, 1).reshape(16, 432)
    w_back = by_offset.transpose(1, 2, 0)[:, ::-1, :].reshape(16, 432)
    tile = (16, 128)
    own_feat, own_fields, to_next, to_prev = call(
        pack_y,
        [((32,) + tile, BF16), ((20,) + tile, BF16), ((4 * PREV + 20,) + tile, BF16),
         ((4 * NEXT + 20,) + tile, BF16)],
        [pltpu.VMEM((512, 128), F32)],
        (features.reshape(16, 32, 128), field, velocity, cotangent),
    )
    before, after = neighbours(to_next, to_prev, "gy")
    to_up, to_down = pl.pallas_call(
        pack_z,
        out_shape=[
            jax.ShapeDtypeStruct((ROWS_IN + 3 * (stop - first),) + tile, BF16)
            for first, stop in (UP, DOWN)
        ],
        in_specs=[_HBM] * 4,
        out_specs=[_HBM] * 2,
        scratch_shapes=[
            pltpu.VMEM((ROWS_IN + 3 * (stop - first),) + tile, BF16) for first, stop in (UP, DOWN)
        ]
        + [pltpu.SemaphoreType.DMA((12,)), pltpu.SemaphoreType.DMA((2,))],
        compiler_params=pltpu.CompilerParams(vmem_limit_bytes=64 * 1024 * 1024),
    )(own_feat, own_fields, before, after)
    below, above = neighbours(to_up, to_down, "gz")
    send_up, send_down, send_far, columns_own, coef, state = call(
        stage_one,
        [((10, 16, 128), F32), ((10, 16, 128), F32), ((8, 128), F32), ((864, 1024), BF16),
         ((4, 384, 128), F32), ((48, 24, 128), F32)],
        [pltpu.VMEM((3, 6, ROWS_IN * 16, 128), BF16), pltpu.VMEM((864, ROWS_OUT * 128), BF16)],
        (own_feat, before, after, below, above, field, velocity, cotangent, w_rows),
    )
    below1, above1 = neighbours(send_up, send_down, "gz")
    far = lax.ppermute(send_far, "gz", [((i + 2) % nz, i) for i in range(nz)])
    (gram,) = call(
        patch_gram,
        [((192, 128), F32)],
        [pltpu.VMEM((144, 512), F32), pltpu.VMEM((16, 1280), F32)],
        (columns_own,),
        5e8,
    )
    rows = 256 // ny
    mixed, tiles, grad_field = call(
        stage_two,
        [((ny, rows, 128), F32), ((6, 160, 128), BF16), ((4, 8, 128), F32)],
        [pltpu.VMEM((10, 24, 128), F32), pltpu.VMEM((7, 24, 128), F32),
         pltpu.VMEM((6, 384, 128), F32), pltpu.VMEM((16, 512), F32)],
        (below1, above1, far, state, coef, columns_own, gram),
    )
    (grad_feat,) = call(
        stage_three,
        [((16, 32, 128), BF16)],
        [pltpu.VMEM((3, 6, 160, 128), BF16), pltpu.VMEM((864, 1024), BF16), pltpu.VMEM((512, 128), F32)],
        (tiles, w_back),
        1e8,
        (mixed,),
    )
    parts = lax.all_to_all(mixed, "gy", 0, 0)
    (parts,) = call_small(total_to_all, [((nz, rows, 128), F32)], [], (parts,))
    parts = lax.all_to_all(parts, "gz", 0, 0)
    (parts,) = call_small(total_to_all, [((ny, rows, 128), F32)], [], (parts,))
    parts = lax.all_to_all(parts, "gy", 0, 0)
    grad_weight, factor_patch, factor_grad = call_small(
        lambda *refs: finish(cells, *refs),
        [((16, 432), F32), ((432, 432), F32), ((16, 16), F32)],
        [pltpu.VMEM((16, 1280), F32), pltpu.VMEM((16, 512), F32), pltpu.VMEM((448, 432), F32),
         pltpu.VMEM((256, 256), F32), pltpu.VMEM((4, 432, 128), F32)],
        (parts,),
    )
    return (grad_field, grad_feat.reshape(16, 4, 8, 128), grad_weight, factor_patch, factor_grad)


def solution(mesh):
    placed = (
        P(None, "gz", "gy", None),
        P("gz", "gy", None),
        P(None, "gz", "gy", None),
        P(),
        P("gz", "gy", None),
    )
    return jax.shard_map(
        body,
        mesh=mesh,
        in_specs=placed,
        out_specs=(P("gz", "gy", None), P(None, "gz", "gy", None), P(), P(), P()),
        check_vma=False,
    )
```

```python
import math

import jax
import jax.numpy as jnp
from jax import lax
from jax.experimental import pallas as pl
from jax.experimental.pallas import tpu as pltpu
from jax.sharding import PartitionSpec as P

H = 0.15
BASE = (2.0 / 60.0, -13.0 / 60.0, 47.0 / 60.0, 27.0 / 60.0, -3.0 / 60.0)
F32 = jnp.float32
BF16 = jnp.bfloat16
NT = (((1,), (1,)), ((), ()))

ROWS_IN = 19
ROWS_OUT = 17
PREV = 5
NEXT = 6

_HBM = pl.BlockSpec(memory_space=pltpu.HBM)


def call(kernel, outs, scratch, args, flops=1e6, follows=()):
    n_in, n_out = len(args), len(outs)

    def run(*refs):
        source, refs = refs[:n_in], refs[n_in + len(follows) :]
        target = refs[:n_out]
        refs = (None,) * n_in + tuple(refs)
        arrived, left = refs[n_in + n_out : n_in + n_out + 2]
        held = refs[n_in + n_out + 2 :]
        here, there = held[:n_in], held[n_in : n_in + n_out]
        coming = {i: pltpu.make_async_copy(source[i], here[i], arrived.at[i]) for i in range(n_in)}
        going = {i: pltpu.make_async_copy(there[i], target[i], left.at[i]) for i in range(n_out)}
        sent = []
        for i in range(n_in):
            coming[i].start()

        def need(*which):
            for i in which:
                coming.pop(i).wait()

        def done(*which):
            for i in which:
                going[i].start()
                sent.append(i)

        kernel(need, done, *held)
        need(*list(coming))
        done(*[i for i in range(n_out) if i not in sent])
        for i in range(n_out):
            going[i].wait()

    return pl.pallas_call(
        run,
        out_shape=[jax.ShapeDtypeStruct(s, t) for s, t in outs],
        in_specs=[_HBM] * (n_in + len(follows)),
        out_specs=[_HBM] * n_out,
        scratch_shapes=[pltpu.SemaphoreType.DMA((n_in,)), pltpu.SemaphoreType.DMA((n_out,))]
        + [pltpu.VMEM(a.shape, a.dtype) for a in args]
        + [pltpu.VMEM(s, t) for s, t in outs]
        + scratch,
        compiler_params=pltpu.CompilerParams(vmem_limit_bytes=64 * 1024 * 1024),
        cost_estimate=pl.CostEstimate(flops=int(flops), bytes_accessed=4000000, transcendentals=0),
    )(*args, *follows)


def call_small(kernel, outs, scratch, args):
    return pl.pallas_call(
        kernel,
        out_shape=[jax.ShapeDtypeStruct(s, t) for s, t in outs],
        in_specs=[pl.BlockSpec(memory_space=pltpu.VMEM)] * len(args),
        out_specs=[pl.BlockSpec(memory_space=pltpu.VMEM)] * len(outs),
        scratch_shapes=scratch,
        compiler_params=pltpu.CompilerParams(vmem_limit_bytes=16 * 1024 * 1024),
        cost_estimate=pl.CostEstimate(flops=1000000, bytes_accessed=4000000, transcendentals=0),
    )(*args)


def shift_both():
    i = lax.broadcasted_iota(jnp.int32, (128, 256), 0)
    j = lax.broadcasted_iota(jnp.int32, (128, 256), 1)
    source = jnp.where(j < 128, j + 127, j + 1) % 128
    return jnp.where(i == source, 1.0, 0.0).astype(BF16)


def roll(value, shift, axis):
    shift %= value.shape[axis]
    return value if shift == 0 else pltpu.roll(value, shift, axis)


def split(plane):
    lead = plane.astype(BF16).astype(F32)
    return jnp.concatenate([lead, plane - lead], axis=0).astype(BF16)


def join(tile):
    both = tile.astype(F32)
    return both[:8] + both[8:]


ORDER = [
    ("l", 3), (0, 3), (1, 3), (2, 3), ("u", 3), ("u", 1), ("u", 2), ("u", 0), ("l", 0), ("l", 1),
    (0, 0), (1, 0), (2, 0), ("l", 2), (0, 1), (0, 2), (1, 1), (1, 2), (2, 1), (2, 2),
]
UP, DOWN = (0, 7), (5, 13)


def pack_y(
    need, done, feat, field, vel, cot, own_feat, own_fields, to_next, to_prev, turn
):
    need(0)
    for c in range(16):
        turn[pl.ds(c, 32, stride=16), :] = feat[c].astype(F32)
    for zy in range(32):
        tile = turn[zy * 16 : (zy + 1) * 16, :].astype(BF16)
        own_feat[zy] = tile
        z, y = divmod(zy, 8)
        if y >= 8 - PREV:
            to_next[z * PREV + y - (8 - PREV)] = tile
        if y < NEXT:
            to_prev[z * NEXT + y] = tile
    need(1, 2, 3)
    for i, (kind, z) in enumerate(ORDER):
        tile = split(field[z] if kind == "u" else cot[z] if kind == "l" else vel[kind, z])
        own_fields[i] = tile
        to_next[4 * PREV + i] = tile
        to_prev[4 * NEXT + i] = tile


def pack_z(own_feat, own_fields, before, after, to_up, to_down, up, down, moved, left):
    copies = []

    def move(source, at, out, to, count):
        copies.append(
            pltpu.make_async_copy(
                source.at[at : at + count], out.at[to : to + count], moved.at[len(copies)]
            )
        )

    for out, z, (first, stop) in ((up, 3, UP), (down, 0, DOWN)):
        n = stop - first
        move(before, z * PREV, out, 0, PREV)
        move(own_feat, z * 8, out, PREV, 8)
        move(after, z * NEXT, out, PREV + 8, NEXT)
        move(before, 4 * PREV + first, out, ROWS_IN, n)
        move(own_fields, first, out, ROWS_IN + n, n)
        move(after, 4 * NEXT + first, out, ROWS_IN + 2 * n, n)
    for copy in copies:
        copy.start()
    out_up = pltpu.make_async_copy(up, to_up, left.at[0])
    out_down = pltpu.make_async_copy(down, to_down, left.at[1])
    for copy in copies[:6]:
        copy.wait()
    out_up.start()
    for copy in copies[6:]:
        copy.wait()
    out_down.start()
    out_up.wait()
    out_down.wait()


def fill_columns(columns, shifted, z, rows):
    for a in range(3):
        for b in range(3):
            at = pl.multiple_of(z * 144 + (a * 3 + b) * 16, 16)
            for y in range(rows):
                columns[pl.ds(at, 16), y * 128 : (y + 1) * 128] = shifted[
                    b, z, (y + a) * 16 : (y + a + 1) * 16, :
                ]


U0, LAM2, U1, LAM1, FACE = slice(0, 10), slice(10, 17), slice(35, 39), slice(39, 47), 47
VEL = (slice(17, 23), slice(23, 29), slice(29, 35))
FAR = [(2, 2), (3, 1), (3, 2), (1, -2), (0, -1), (0, -2)]


def stage_one(
    need, done, own_feat, before, after, below, above, field, vel, cot, w_rows,
    send_up, send_down, send_far, columns_own, coef, kept,
    shifted, columns,
):
    u0, lam2 = kept.at[U0], kept.at[LAM2]
    velx = [kept.at[v] for v in VEL]
    shift_value = shift_both()
    need(0, 1, 2, 3, 4)
    for z in range(6):
        if z == 0:
            tiles = below[0:ROWS_IN].reshape(ROWS_IN * 16, 128)
        elif z == 5:
            tiles = above[0:ROWS_IN].reshape(ROWS_IN * 16, 128)
        else:
            p = z - 1
            tiles = jnp.concatenate(
                [
                    before[p * PREV : (p + 1) * PREV].reshape(PREV * 16, 128),
                    own_feat[p * 8 : (p + 1) * 8].reshape(128, 128),
                    after[p * NEXT : (p + 1) * NEXT].reshape(NEXT * 16, 128),
                ],
                axis=0,
            )
        shifted[1, z] = tiles
        both = jnp.dot(tiles, shift_value, preferred_element_type=F32).astype(BF16)
        shifted[0, z] = both[:, :128]
        shifted[2, z] = both[:, 128:]

    need(5, 6, 7)

    def extended(kind, z, own):
        i = ORDER.index((kind, z))
        return jnp.concatenate(
            [join(before[4 * PREV + i]), own, join(after[4 * NEXT + i])], axis=0
        )

    def received(source, part, kind, z):
        n = part[1] - part[0]
        at = ROWS_IN + ORDER.index((kind, z)) - part[0]
        return jnp.concatenate([join(source[at + n * j]) for j in range(3)], axis=0)

    for j in range(3):
        u0[j] = received(below, UP, "u", 1 + j)
        u0[7 + j] = received(above, DOWN, "u", j)
        velx[j][0] = received(below, UP, j, 3)
        velx[j][5] = received(above, DOWN, j, 0)
    lam2[0] = received(below, UP, "l", 3)
    lam2[5] = received(above, DOWN, "l", 0)
    lam2[6] = received(above, DOWN, "l", 1)
    for z in range(4):
        u0[3 + z] = extended("u", z, field[z])
        lam2[1 + z] = extended("l", z, cot[z])
        for d in range(3):
            velx[d][1 + z] = extended(d, z, vel[d, z])

    def fill(z, carry):
        fill_columns(columns, shifted, z, ROWS_OUT)
        return carry

    lax.fori_loop(0, 6, fill, 0)

    columns_own[...] = columns[:, 512:1536]
    done(3)
    need(8)
    w_value = w_rows[...]
    for p in range(4):
        plane = jnp.dot(
            w_value, columns[p * 144 : p * 144 + 432, :], preferred_element_type=F32
        )
        for y in range(ROWS_OUT):
            coef[p, (4 + y) * 16 : (5 + y) * 16, :] = plane[:, y * 128 : (y + 1) * 128]

    done(4)

    def a(p, k):
        value = coef[p, pl.ds(k, 24, stride=16), :]
        return value + BASE[k % 5]

    pushed = [None] * 8

    def push(slot, value):
        pushed[slot] = value if pushed[slot] is None else pushed[slot] + value

    faces_z = []
    states = []
    carried = {}
    for p in range(4):
        rate = 1.0 + H * coef[p, pl.ds(15, 24, stride=16), :]
        u = u0[3 + p]
        lam = lam2[1 + p]
        state = u * rate
        push(p + 2, lam * rate)
        for d in range(3):
            beyond = lam2[2 + p] if d == 0 else roll(lam, -1, d - 1)
            drive = (-H) * (lam - beyond) * velx[d][1 + p]
            face = None
            for s in range(-2, 3):
                weight = a(p, 5 * d + s + 2)
                term = weight * (u0[3 + p + s] if d == 0 else roll(u, -s, d - 1))
                face = term if face is None else face + term
                back = drive * weight
                if d == 0:
                    push(p + 2 + s, back)
                    if (p, s) in FAR:
                        carried[p, s] = velx[0][1 + p] * weight
                else:
                    push(p + 2, roll(back, s, d - 1))
            face = (H * velx[d][1 + p]) * face
            if d == 0:
                faces_z.append(face)
                state = state - (face if p == 0 else face - faces_z[p - 1])
            else:
                state = state - (face - roll(face, 1, d - 1))
        states.append(state)
    u1_part, lam_part = kept.at[U1], kept.at[LAM1]
    for p in range(4):
        u1_part[p] = states[p]
    for j in range(8):
        lam_part[j] = pushed[j]
    kept[FACE] = faces_z[3]
    ups = [states[1], states[2], states[3], faces_z[3], pushed[5], pushed[6], pushed[7], pushed[4]]
    downs = [states[0], states[1], states[2], pushed[2], pushed[3], pushed[0], pushed[1], pushed[4]]
    for j in range(8):
        send_up[j] = ups[j][4:20]
        send_down[j] = downs[j][4:20]
    for out, keys in ((send_up, FAR[:3]), (send_down, FAR[3:])):
        out[8, 0:8, :] = carried[keys[0]][8:16]
        out[8, 8:16, :] = carried[keys[1]][8:16]
        out[9, 0:8, :] = carried[keys[2]][8:16]
        out[9, 8:16, :] = carried[keys[2]][8:16]
    send_far[...] = pushed[0][8:16]


def patch_gram(need, done, columns_own, gram, full, line):
    need(0)
    total = None
    for p in range(4):
        part = lax.dot_general(
            columns_own[p * 144 : (p + 1) * 144, :],
            columns_own[p * 144 : p * 144 + 432, :],
            NT,
            preferred_element_type=F32,
        )
        total = part if total is None else total + part
    full[:, 0:432] = total
    line[...] = jnp.zeros((16, 1280), F32)

    def put(dz, dy, dx, count, a, b, a_other):
        to = dz * 400 + (dy + 2) * 80 + (dx + 2) * 16
        at = dz * 144 + a_other * 48
        group = (a * 3 + b) * 16
        line[:, to : to + 16 * count] = full[group : group + 16, at : at + 16 * count]

    for dz in range(3):
        for a in range(3):
            put(dz, a, 0, 3, 0, 0, a)
            for b in (1, 2):
                put(dz, a, -b, 1, 0, b, a)
        for a in (1, 2):
            put(dz, -a, 0, 3, a, 0, 0)
            for b in (1, 2):
                put(dz, -a, -b, 1, a, b, 0)
    for t in range(10):
        gram[t * 16 : (t + 1) * 16, :] = line[:, t * 128 : (t + 1) * 128]
    gram[160:192, :] = jnp.zeros((32, 128), F32)


def stage_two(
    need, done, below, above, far, state, coef, columns_own, gram,
    mixed, tiles, lam0,
    u1, lam1, turn, row,
):
    u0, lam2, u1_part, lam_part = state.at[U0], state.at[LAM2], state.at[U1], state.at[LAM1]
    velx = [state.at[v] for v in VEL]
    need(0, 1, 2, 3, 4)

    def padded(value):
        zero = jnp.zeros((4, 128), F32)
        return jnp.concatenate([zero, value, zero], axis=0)

    low = [padded(below[j]) for j in range(8)]
    high = [padded(above[j]) for j in range(8)]
    for j in range(3):
        u1[j] = low[j]
        u1[7 + j] = high[j] + (state[FACE] if j == 0 else 0.0)
        u1[4 + j] = u1_part[1 + j]
    u1[3] = u1_part[0] + low[3]
    lam1[0] = low[4] + lam_part[1]
    lam1[1] = lam_part[2] + low[5]
    lam1[2] = lam_part[3] + low[6]
    lam1[3] = lam_part[4] + high[5]
    lam1[4] = lam_part[5] + high[6]
    lam1[5] = high[3] + lam_part[6]
    lam1[6] = high[4] + lam_part[7]

    pushed = [None] * 8

    def push(slot, value):
        pushed[slot] = value if pushed[slot] is None else pushed[slot] + value

    own_rows = slice(8, 16)
    lowest = lam_part[0][own_rows] + low[7][own_rows]
    highest = high[7][own_rows] + far[...]
    fall = [lowest, lam1[0, own_rows], lam1[1, own_rows]]
    rise = [lam1[5, own_rows], lam1[6, own_rows], highest]
    outer = [(-H) * (fall[0] - fall[1]), (-H) * (fall[1] - fall[2])]
    inner = [(-H) * (rise[0] - rise[1]), (-H) * (rise[1] - rise[2])]
    edge = [
        outer[0] * below[8, 0:8, :] + outer[1] * below[8, 8:16, :],
        outer[1] * below[9, 0:8, :],
        inner[0] * above[9, 0:8, :],
        inner[0] * above[8, 8:16, :] + inner[1] * above[8, 0:8, :],
    ]

    for z in range(6):
        later, first = lam2[z], lam1[z]
        v, u = u1[z + 2], u0[z + 2]
        own = 1 <= z <= 4
        p = z - 1
        if own:
            push(z + 1, first * (1.0 + H * coef[p, pl.ds(15, 24, stride=16), :]))
        for d in range(3):
            speed = velx[d][z]
            beyond_later = lam2[z + 1] if d == 0 else roll(later, -1, d - 1)
            beyond_first = lam1[z + 1] if d == 0 else roll(first, -1, d - 1)
            drive_later = (-H) * (later - beyond_later) * speed
            drive_first = (-H) * (first - beyond_first) * speed
            for s in range(-2, 3):
                k = 5 * d + s + 2
                there_later = u1[z + 2 + s] if d == 0 else roll(v, -s, d - 1)
                there_first = u0[z + 2 + s] if d == 0 else roll(u, -s, d - 1)
                turn[z, pl.ds(k, 24, stride=16), :] = (
                    drive_later * there_later + drive_first * there_first
                )
                if own:
                    back = drive_first * (coef[p, pl.ds(k, 24, stride=16), :] + BASE[s + 2])
                    if d == 0:
                        push(z + 1 + s, back)
                    else:
                        push(z + 1, roll(back, s, d - 1))
        turn[z, pl.ds(15, 24, stride=16), :] = H * later * v + H * first * u
    for p in range(4):
        lam0[p] = pushed[2 + p][own_rows] + edge[p]
    done(2)

    for z in range(6):
        tiles[z] = turn[z, 7 * 16 : 17 * 16, :].astype(BF16)
    done(1)
    need(5)
    sum_w = None
    sum_g = None
    for p in range(4):
        mine = jnp.concatenate(
            [tiles[p + 1, (y + 1) * 16 : (y + 2) * 16, :] for y in range(8)], axis=1
        )
        part_w = lax.dot_general(
            mine, columns_own[p * 144 : p * 144 + 432, :], NT, preferred_element_type=F32
        )
        part_g = lax.dot_general(mine, mine, NT, preferred_element_type=F32)
        sum_w = part_w if sum_w is None else sum_w + part_w
        sum_g = part_g if sum_g is None else sum_g + part_g
    row[...] = jnp.zeros((16, 512), F32)
    row[:, 0:432] = sum_w
    row[:, 432:448] = sum_g
    for t in range(4):
        mixed[t * 16 : (t + 1) * 16, :] = row[:, t * 128 : (t + 1) * 128]
    need(6)
    mixed[64:256, :] = gram[...]


def stage_three(need, done, tiles, w_back, grad_feat, shifted, columns, turn_out):
    need(0)
    shift_value = shift_both()
    for z in range(6):
        shifted[1, z] = tiles[z]
        both = jnp.dot(tiles[z], shift_value, preferred_element_type=F32).astype(BF16)
        shifted[0, z] = both[:, :128]
        shifted[2, z] = both[:, 128:]

    def fill(z, carry):
        fill_columns(columns, shifted, z, 8)
        return carry

    lax.fori_loop(0, 6, fill, 0)
    need(1)
    w_value = w_back[...]
    for p in range(4):
        plane = jnp.dot(
            w_value, columns[p * 144 : p * 144 + 432, :], preferred_element_type=F32
        )
        for y in range(8):
            turn_out[pl.ds(p * 8 + y, 16, stride=32), :] = plane[:, y * 128 : (y + 1) * 128]
    for c in range(16):
        grad_feat[c] = turn_out[c * 32 : (c + 1) * 32, :].astype(BF16)


def pieces(value):
    one = value.astype(BF16)
    rest = value - one.astype(F32)
    two = rest.astype(BF16)
    three = (rest - two.astype(F32)).astype(BF16)
    return one, two, three


def to_channel_major(value):
    i = lax.broadcasted_iota(jnp.int32, (432, 432), 0)
    j = lax.broadcasted_iota(jnp.int32, (432, 432), 1)
    place = jnp.where((i % 16) * 27 + i // 16 == j, 1.0, 0.0).astype(BF16)
    parts = [jnp.dot(v, place, preferred_element_type=F32) for v in pieces(value)]
    return parts[2] + parts[1] + parts[0]


def total_to_all(parts, out):
    total = parts[0]
    for n in range(1, parts.shape[0]):
        total = total + parts[n]
    for n in range(out.shape[0]):
        out[n] = total


def finish(cells, chunks, out_w, out_p, out_g, line, row, square, block, turn):
    for t in range(4):
        row[:, t * 128 : (t + 1) * 128] = chunks[t * 16 : (t + 1) * 16, :]
    for t in range(10):
        line[:, t * 128 : (t + 1) * 128] = chunks[64 + t * 16 : 80 + t * 16, :] * (1.0 / cells)
    out_g[...] = row[:, 432:448] * (1.0 / cells)
    for dz in range(3):
        for a in range(3):
            for b in range(3):
                group = (a * 3 + b) * 16
                for a_other in range(3):
                    to = dz * 144 + a_other * 48
                    at = dz * 400 + (a_other - a + 2) * 80 + (2 - b) * 16
                    square[group : group + 16, to : to + 48] = line[:, at : at + 48]
    square[144:288, 144:432] = square[0:144, 0:288]
    square[288:432, 288:432] = square[0:144, 0:144]
    block[...] = jnp.zeros((256, 256), F32)
    block[0:144, 0:144] = square[0:144, 144:288]
    turned = jnp.transpose(block[...])[0:144, 0:144]
    square[144:288, 0:144] = turned
    square[288:432, 144:288] = turned
    block[0:144, 0:144] = square[0:144, 288:432]
    square[288:432, 0:144] = jnp.transpose(block[...])[0:144, 0:144]
    square[432:448, :] = row[:, 0:432] * (1.0 / math.sqrt(cells))
    ready = to_channel_major(square[...])
    out_w[...] = ready[432:448, :]
    for t in range(4):
        wide = min(128, 432 - t * 128)
        for o in range(27):
            turn[t, pl.ds(o, 16, stride=27), 0:wide] = ready[
                o * 16 : (o + 1) * 16, t * 128 : t * 128 + wide
            ]
        out_p[:, t * 128 : t * 128 + wide] = turn[t, :, 0:wide]


def neighbours(to_next, to_prev, axis):
    size = lax.axis_size(axis)
    up = [(i, (i + 1) % size) for i in range(size)]
    down = [(j, i) for i, j in up]
    return lax.ppermute(to_next, axis, up), lax.ppermute(to_prev, axis, down)


def body(features, field, velocity, weight, cotangent):
    nz, ny = lax.axis_size("gz"), lax.axis_size("gy")
    cells = float(4096 * nz * ny)
    by_offset = weight.reshape(16, 16, 27)
    w_rows = by_offset.transpose(0, 2, 1).reshape(16, 432)
    w_back = by_offset.transpose(1, 2, 0)[:, ::-1, :].reshape(16, 432)
    tile = (16, 128)
    own_feat, own_fields, to_next, to_prev = call(
        pack_y,
        [((32,) + tile, BF16), ((20,) + tile, BF16), ((4 * PREV + 20,) + tile, BF16),
         ((4 * NEXT + 20,) + tile, BF16)],
        [pltpu.VMEM((512, 128), F32)],
        (features.reshape(16, 32, 128), field, velocity, cotangent),
    )
    before, after = neighbours(to_next, to_prev, "gy")
    to_up, to_down = pl.pallas_call(
        pack_z,
        out_shape=[
            jax.ShapeDtypeStruct((ROWS_IN + 3 * (stop - first),) + tile, BF16)
            for first, stop in (UP, DOWN)
        ],
        in_specs=[_HBM] * 4,
        out_specs=[_HBM] * 2,
        scratch_shapes=[
            pltpu.VMEM((ROWS_IN + 3 * (stop - first),) + tile, BF16) for first, stop in (UP, DOWN)
        ]
        + [pltpu.SemaphoreType.DMA((12,)), pltpu.SemaphoreType.DMA((2,))],
        compiler_params=pltpu.CompilerParams(vmem_limit_bytes=64 * 1024 * 1024),
    )(own_feat, own_fields, before, after)
    below, above = neighbours(to_up, to_down, "gz")
    send_up, send_down, send_far, columns_own, coef, state = call(
        stage_one,
        [((10, 16, 128), F32), ((10, 16, 128), F32), ((8, 128), F32), ((864, 1024), BF16),
         ((4, 384, 128), F32), ((48, 24, 128), F32)],
        [pltpu.VMEM((3, 6, ROWS_IN * 16, 128), BF16), pltpu.VMEM((864, ROWS_OUT * 128), BF16)],
        (own_feat, before, after, below, above, field, velocity, cotangent, w_rows),
    )
    below1, above1 = neighbours(send_up, send_down, "gz")
    far = lax.ppermute(send_far, "gz", [((i + 2) % nz, i) for i in range(nz)])
    (gram,) = call(
        patch_gram,
        [((192, 128), F32)],
        [pltpu.VMEM((144, 512), F32), pltpu.VMEM((16, 1280), F32)],
        (columns_own,),
        5e8,
    )
    mixed, tiles, grad_field = call(
        stage_two,
        [((256, 128), F32), ((6, 160, 128), BF16), ((4, 8, 128), F32)],
        [pltpu.VMEM((10, 24, 128), F32), pltpu.VMEM((7, 24, 128), F32),
         pltpu.VMEM((6, 384, 128), F32), pltpu.VMEM((16, 512), F32)],
        (below1, above1, far, state, coef, columns_own, gram),
    )
    (grad_feat,) = call(
        stage_three,
        [((16, 32, 128), BF16)],
        [pltpu.VMEM((3, 6, 160, 128), BF16), pltpu.VMEM((864, 1024), BF16), pltpu.VMEM((512, 128), F32)],
        (tiles, w_back),
        1e8,
        (mixed,),
    )
    half = nz // 2
    line = [[(h * half + i) * ny + j for h in range(2) for j in range(ny)] for i in range(half)]
    plane = [[(h * half + i) * ny + j for i in range(half)] for h in range(2) for j in range(ny)]
    rows = 256 // len(line[0])
    axes = ("gz", "gy")
    parts = mixed.reshape(2 * ny, rows, 128)
    parts = lax.all_to_all(parts, axes, 0, 0, axis_index_groups=line)
    (parts,) = call_small(total_to_all, [((half, rows, 128), F32)], [], (parts,))
    parts = lax.all_to_all(parts, axes, 0, 0, axis_index_groups=plane)
    (parts,) = call_small(total_to_all, [((2 * ny, rows, 128), F32)], [], (parts,))
    parts = lax.all_to_all(parts, axes, 0, 0, axis_index_groups=line).reshape(256, 128)
    grad_weight, factor_patch, factor_grad = call_small(
        lambda *refs: finish(cells, *refs),
        [((16, 432), F32), ((432, 432), F32), ((16, 16), F32)],
        [pltpu.VMEM((16, 1280), F32), pltpu.VMEM((16, 512), F32), pltpu.VMEM((448, 432), F32),
         pltpu.VMEM((256, 256), F32), pltpu.VMEM((4, 432, 128), F32)],
        (parts,),
    )
    return (grad_field, grad_feat.reshape(16, 4, 8, 128), grad_weight, factor_patch, factor_grad)


def solution(mesh):
    placed = (
        P(None, "gz", "gy", None),
        P("gz", "gy", None),
        P(None, "gz", "gy", None),
        P(),
        P("gz", "gy", None),
    )
    return jax.shard_map(
        body,
        mesh=mesh,
        in_specs=placed,
        out_specs=(P("gz", "gy", None), P(None, "gz", "gy", None), P(), P(), P()),
        check_vma=False,
    )
```

```python
import math

import jax
import jax.numpy as jnp
from jax import lax
from jax.experimental import pallas as pl
from jax.experimental.pallas import tpu as pltpu
from jax.sharding import PartitionSpec as P

H = 0.15
BASE = (2.0 / 60.0, -13.0 / 60.0, 47.0 / 60.0, 27.0 / 60.0, -3.0 / 60.0)
F32 = jnp.float32
BF16 = jnp.bfloat16
NT = (((1,), (1,)), ((), ()))

ROWS_IN = 19
ROWS_OUT = 17
PREV = 5
NEXT = 6

_HBM = pl.BlockSpec(memory_space=pltpu.HBM)


def call(kernel, outs, scratch, args, flops=1e6, follows=()):
    n_in, n_out = len(args), len(outs)

    def run(*refs):
        source, refs = refs[:n_in], refs[n_in + len(follows) :]
        target = refs[:n_out]
        refs = (None,) * n_in + tuple(refs)
        arrived, left = refs[n_in + n_out : n_in + n_out + 2]
        held = refs[n_in + n_out + 2 :]
        here, there = held[:n_in], held[n_in : n_in + n_out]
        coming = {i: pltpu.make_async_copy(source[i], here[i], arrived.at[i]) for i in range(n_in)}
        going = {i: pltpu.make_async_copy(there[i], target[i], left.at[i]) for i in range(n_out)}
        sent = []
        for i in range(n_in):
            coming[i].start()

        def need(*which):
            for i in which:
                coming.pop(i).wait()

        def done(*which):
            for i in which:
                going[i].start()
                sent.append(i)

        kernel(need, done, *held)
        need(*list(coming))
        done(*[i for i in range(n_out) if i not in sent])
        for i in range(n_out):
            going[i].wait()

    return pl.pallas_call(
        run,
        out_shape=[jax.ShapeDtypeStruct(s, t) for s, t in outs],
        in_specs=[_HBM] * (n_in + len(follows)),
        out_specs=[_HBM] * n_out,
        scratch_shapes=[pltpu.SemaphoreType.DMA((n_in,)), pltpu.SemaphoreType.DMA((n_out,))]
        + [pltpu.VMEM(a.shape, a.dtype) for a in args]
        + [pltpu.VMEM(s, t) for s, t in outs]
        + scratch,
        compiler_params=pltpu.CompilerParams(vmem_limit_bytes=64 * 1024 * 1024),
        cost_estimate=pl.CostEstimate(flops=int(flops), bytes_accessed=4000000, transcendentals=0),
    )(*args, *follows)


def call_small(kernel, outs, scratch, args):
    return pl.pallas_call(
        kernel,
        out_shape=[jax.ShapeDtypeStruct(s, t) for s, t in outs],
        in_specs=[pl.BlockSpec(memory_space=pltpu.VMEM)] * len(args),
        out_specs=[pl.BlockSpec(memory_space=pltpu.VMEM)] * len(outs),
        scratch_shapes=scratch,
        compiler_params=pltpu.CompilerParams(vmem_limit_bytes=16 * 1024 * 1024),
        cost_estimate=pl.CostEstimate(flops=1000000, bytes_accessed=4000000, transcendentals=0),
    )(*args)


def shift_both():
    i = lax.broadcasted_iota(jnp.int32, (128, 256), 0)
    j = lax.broadcasted_iota(jnp.int32, (128, 256), 1)
    source = jnp.where(j < 128, j + 127, j + 1) % 128
    return jnp.where(i == source, 1.0, 0.0).astype(BF16)


def roll(value, shift, axis):
    shift %= value.shape[axis]
    return value if shift == 0 else pltpu.roll(value, shift, axis)


def split(plane):
    lead = plane.astype(BF16).astype(F32)
    return jnp.concatenate([lead, plane - lead], axis=0).astype(BF16)


def join(tile):
    both = tile.astype(F32)
    return both[:8] + both[8:]


ORDER = [
    ("l", 3), (0, 3), (1, 3), (2, 3), ("u", 3), ("u", 1), ("u", 2), ("u", 0), ("l", 0), ("l", 1),
    (0, 0), (1, 0), (2, 0), ("l", 2), (0, 1), (0, 2), (1, 1), (1, 2), (2, 1), (2, 2),
]
UP, DOWN = (0, 7), (5, 13)


def pack_y(
    need, done, feat, field, vel, cot, own_feat, own_fields, to_next, to_prev, turn
):
    need(0)
    for c in range(16):
        turn[pl.ds(c, 32, stride=16), :] = feat[c].astype(F32)
    for zy in range(32):
        tile = turn[zy * 16 : (zy + 1) * 16, :].astype(BF16)
        own_feat[zy] = tile
        z, y = divmod(zy, 8)
        if y >= 8 - PREV:
            to_next[z * PREV + y - (8 - PREV)] = tile
        if y < NEXT:
            to_prev[z * NEXT + y] = tile
    need(1, 2, 3)
    for i, (kind, z) in enumerate(ORDER):
        tile = split(field[z] if kind == "u" else cot[z] if kind == "l" else vel[kind, z])
        own_fields[i] = tile
        to_next[4 * PREV + i] = tile
        to_prev[4 * NEXT + i] = tile


def pack_z(own_feat, own_fields, before, after, to_up, to_down, up, down, moved, left):
    copies = []

    def move(source, at, out, to, count):
        copies.append(
            pltpu.make_async_copy(
                source.at[at : at + count], out.at[to : to + count], moved.at[len(copies)]
            )
        )

    for out, z, (first, stop) in ((up, 3, UP), (down, 0, DOWN)):
        n = stop - first
        move(before, z * PREV, out, 0, PREV)
        move(own_feat, z * 8, out, PREV, 8)
        move(after, z * NEXT, out, PREV + 8, NEXT)
        move(before, 4 * PREV + first, out, ROWS_IN, n)
        move(own_fields, first, out, ROWS_IN + n, n)
        move(after, 4 * NEXT + first, out, ROWS_IN + 2 * n, n)
    second = ROWS_IN + 3 * (DOWN[1] - DOWN[0])
    move(before, 2 * PREV - 1, down, second, 1)
    move(own_feat, 8, down, second + 1, 8)
    move(after, NEXT, down, second + 9, 1)
    for copy in copies:
        copy.start()
    out_up = pltpu.make_async_copy(up, to_up, left.at[0])
    out_down = pltpu.make_async_copy(down, to_down, left.at[1])
    for copy in copies[:6]:
        copy.wait()
    out_up.start()
    for copy in copies[6:]:
        copy.wait()
    out_down.start()
    out_up.wait()
    out_down.wait()


def fill_columns(columns, shifted, z, rows):
    for a in range(3):
        for b in range(3):
            at = pl.multiple_of(z * 144 + (a * 3 + b) * 16, 16)
            for y in rows:
                columns[pl.ds(at, 16), y * 128 : (y + 1) * 128] = shifted[
                    b, z, (y + a) * 16 : (y + a + 1) * 16, :
                ]


U0, LAM2, U1, LAM1, FACE = slice(0, 10), slice(10, 17), slice(35, 39), slice(39, 47), 47
VEL = (slice(17, 23), slice(23, 29), slice(29, 35))
FAR = [(2, 2), (3, 1), (3, 2), (1, -2), (0, -1), (0, -2)]


def stage_one(
    need, done, own_feat, before, after, below, above, field, vel, cot, w_rows,
    send_up, send_down, columns_own, coef, kept,
    shifted, columns, coef_above,
):
    u0, lam2 = kept.at[U0], kept.at[LAM2]
    velx = [kept.at[v] for v in VEL]
    shift_value = shift_both()
    need(0, 1, 2, 3, 4)
    for z in range(6):
        if z == 0:
            tiles = below[0:ROWS_IN].reshape(ROWS_IN * 16, 128)
        elif z == 5:
            tiles = above[0:ROWS_IN].reshape(ROWS_IN * 16, 128)
        else:
            p = z - 1
            tiles = jnp.concatenate(
                [
                    before[p * PREV : (p + 1) * PREV].reshape(PREV * 16, 128),
                    own_feat[p * 8 : (p + 1) * 8].reshape(128, 128),
                    after[p * NEXT : (p + 1) * NEXT].reshape(NEXT * 16, 128),
                ],
                axis=0,
            )
        shifted[1, z] = tiles
        both = jnp.dot(tiles, shift_value, preferred_element_type=F32).astype(BF16)
        shifted[0, z] = both[:, :128]
        shifted[2, z] = both[:, 128:]
    second = ROWS_IN + 3 * (DOWN[1] - DOWN[0])
    tiles = above[second : second + 10].reshape(160, 128)
    both = jnp.dot(tiles, shift_value, preferred_element_type=F32).astype(BF16)
    shifted[0, 6, 64:224, :] = both[:, :128]
    shifted[1, 6, 64:224, :] = tiles
    shifted[2, 6, 64:224, :] = both[:, 128:]

    need(5, 6, 7)

    def extended(kind, z, own):
        i = ORDER.index((kind, z))
        return jnp.concatenate(
            [join(before[4 * PREV + i]), own, join(after[4 * NEXT + i])], axis=0
        )

    def received(source, part, kind, z):
        n = part[1] - part[0]
        at = ROWS_IN + ORDER.index((kind, z)) - part[0]
        return jnp.concatenate([join(source[at + n * j]) for j in range(3)], axis=0)

    for j in range(3):
        u0[j] = received(below, UP, "u", 1 + j)
        u0[7 + j] = received(above, DOWN, "u", j)
        velx[j][0] = received(below, UP, j, 3)
        velx[j][5] = received(above, DOWN, j, 0)
    lam2[0] = received(below, UP, "l", 3)
    lam2[5] = received(above, DOWN, "l", 0)
    lam2[6] = received(above, DOWN, "l", 1)
    for z in range(4):
        u0[3 + z] = extended("u", z, field[z])
        lam2[1 + z] = extended("l", z, cot[z])
        for d in range(3):
            velx[d][1 + z] = extended(d, z, vel[d, z])

    def fill(z, carry):
        fill_columns(columns, shifted, z, range(ROWS_OUT))
        return carry

    lax.fori_loop(0, 6, fill, 0)
    fill_columns(columns, shifted, 6, range(4, 12))

    columns_own[...] = columns[0:864, 512:1536]
    done(2)
    need(8)
    w_value = w_rows[...]
    for p in range(4):
        plane = jnp.dot(
            w_value, columns[p * 144 : p * 144 + 432, :], preferred_element_type=F32
        )
        for y in range(ROWS_OUT):
            coef[p, (4 + y) * 16 : (5 + y) * 16, :] = plane[:, y * 128 : (y + 1) * 128]

    done(3)
    plane = jnp.dot(w_value, columns[576:1008, 512:1536], preferred_element_type=F32)
    for y in range(8):
        coef_above[y * 16 : (y + 1) * 16, :] = plane[:, y * 128 : (y + 1) * 128]

    def a(p, k):
        value = coef[p, pl.ds(k, 24, stride=16), :]
        return value + BASE[k % 5]

    pushed = [None] * 8

    def push(slot, value):
        pushed[slot] = value if pushed[slot] is None else pushed[slot] + value

    faces_z = []
    states = []
    carried = {}
    for p in range(4):
        rate = 1.0 + H * coef[p, pl.ds(15, 24, stride=16), :]
        u = u0[3 + p]
        lam = lam2[1 + p]
        state = u * rate
        push(p + 2, lam * rate)
        for d in range(3):
            beyond = lam2[2 + p] if d == 0 else roll(lam, -1, d - 1)
            drive = (-H) * (lam - beyond) * velx[d][1 + p]
            face = None
            for s in range(-2, 3):
                weight = a(p, 5 * d + s + 2)
                term = weight * (u0[3 + p + s] if d == 0 else roll(u, -s, d - 1))
                face = term if face is None else face + term
                back = drive * weight
                if d == 0:
                    push(p + 2 + s, back)
                    if (p, s) in FAR:
                        carried[p, s] = velx[0][1 + p] * weight
                else:
                    push(p + 2, roll(back, s, d - 1))
            face = (H * velx[d][1 + p]) * face
            if d == 0:
                faces_z.append(face)
                state = state - (face if p == 0 else face - faces_z[p - 1])
            else:
                state = state - (face - roll(face, 1, d - 1))
        states.append(state)
    u1_part, lam_part = kept.at[U1], kept.at[LAM1]
    for p in range(4):
        u1_part[p] = states[p]
    for j in range(8):
        lam_part[j] = pushed[j]
    kept[FACE] = faces_z[3]
    ups = [states[1], states[2], states[3], faces_z[3], pushed[5], pushed[6], pushed[7], pushed[4]]
    downs = [states[0], states[1], states[2], pushed[2], pushed[3], pushed[0], pushed[1], pushed[4]]
    for j in range(8):
        send_up[j] = ups[j][4:20]
        send_down[j] = downs[j][4:20]
    for out, keys in ((send_up, FAR[:3]), (send_down, FAR[3:])):
        out[8, 0:8, :] = carried[keys[0]][8:16]
        out[8, 8:16, :] = carried[keys[1]][8:16]
        out[9, 0:8, :] = carried[keys[2]][8:16]
        out[9, 8:16, :] = carried[keys[2]][8:16]
    face = (-H) * (lam2[5, 8:16] - lam2[6, 8:16]) * velx[0][5, 8:16]
    face = face * (BASE[0] + coef_above[pl.ds(0, 8, stride=16), :])
    send_down[7, 4:12, :] = pushed[4][8:16] + face


def patch_gram(need, done, columns_own, gram, full, line):
    need(0)
    total = None
    for p in range(4):
        part = lax.dot_general(
            columns_own[p * 144 : (p + 1) * 144, :],
            columns_own[p * 144 : p * 144 + 432, :],
            NT,
            preferred_element_type=F32,
        )
        total = part if total is None else total + part
    full[:, 0:432] = total
    line[...] = jnp.zeros((16, 1280), F32)

    def put(dz, dy, dx, count, a, b, a_other):
        to = dz * 400 + (dy + 2) * 80 + (dx + 2) * 16
        at = dz * 144 + a_other * 48
        group = (a * 3 + b) * 16
        line[:, to : to + 16 * count] = full[group : group + 16, at : at + 16 * count]

    for dz in range(3):
        for a in range(3):
            put(dz, a, 0, 3, 0, 0, a)
            for b in (1, 2):
                put(dz, a, -b, 1, 0, b, a)
        for a in (1, 2):
            put(dz, -a, 0, 3, a, 0, 0)
            for b in (1, 2):
                put(dz, -a, -b, 1, a, b, 0)
    for t in range(10):
        gram[t * 16 : (t + 1) * 16, :] = line[:, t * 128 : (t + 1) * 128]
    gram[160:192, :] = jnp.zeros((32, 128), F32)


def stage_two(
    need, done, below, above, state, coef, columns_own, gram,
    mixed, tiles, lam0,
    u1, lam1, turn, row,
):
    u0, lam2, u1_part, lam_part = state.at[U0], state.at[LAM2], state.at[U1], state.at[LAM1]
    velx = [state.at[v] for v in VEL]
    need(0, 1, 2, 3)

    def padded(value):
        zero = jnp.zeros((4, 128), F32)
        return jnp.concatenate([zero, value, zero], axis=0)

    low = [padded(below[j]) for j in range(8)]
    high = [padded(above[j]) for j in range(8)]
    for j in range(3):
        u1[j] = low[j]
        u1[7 + j] = high[j] + (state[FACE] if j == 0 else 0.0)
        u1[4 + j] = u1_part[1 + j]
    u1[3] = u1_part[0] + low[3]
    lam1[0] = low[4] + lam_part[1]
    lam1[1] = lam_part[2] + low[5]
    lam1[2] = lam_part[3] + low[6]
    lam1[3] = lam_part[4] + high[5]
    lam1[4] = lam_part[5] + high[6]
    lam1[5] = high[3] + lam_part[6]
    lam1[6] = high[4] + lam_part[7]

    pushed = [None] * 8

    def push(slot, value):
        pushed[slot] = value if pushed[slot] is None else pushed[slot] + value

    own_rows = slice(8, 16)
    lowest = lam_part[0][own_rows] + low[7][own_rows]
    highest = high[7][own_rows]
    fall = [lowest, lam1[0, own_rows], lam1[1, own_rows]]
    rise = [lam1[5, own_rows], lam1[6, own_rows], highest]
    outer = [(-H) * (fall[0] - fall[1]), (-H) * (fall[1] - fall[2])]
    inner = [(-H) * (rise[0] - rise[1]), (-H) * (rise[1] - rise[2])]
    edge = [
        outer[0] * below[8, 0:8, :] + outer[1] * below[8, 8:16, :],
        outer[1] * below[9, 0:8, :],
        inner[0] * above[9, 0:8, :],
        inner[0] * above[8, 8:16, :] + inner[1] * above[8, 0:8, :],
    ]

    for z in range(6):
        later, first = lam2[z], lam1[z]
        v, u = u1[z + 2], u0[z + 2]
        own = 1 <= z <= 4
        p = z - 1
        if own:
            push(z + 1, first * (1.0 + H * coef[p, pl.ds(15, 24, stride=16), :]))
        for d in range(3):
            speed = velx[d][z]
            beyond_later = lam2[z + 1] if d == 0 else roll(later, -1, d - 1)
            beyond_first = lam1[z + 1] if d == 0 else roll(first, -1, d - 1)
            drive_later = (-H) * (later - beyond_later) * speed
            drive_first = (-H) * (first - beyond_first) * speed
            for s in range(-2, 3):
                k = 5 * d + s + 2
                there_later = u1[z + 2 + s] if d == 0 else roll(v, -s, d - 1)
                there_first = u0[z + 2 + s] if d == 0 else roll(u, -s, d - 1)
                turn[z, pl.ds(k, 24, stride=16), :] = (
                    drive_later * there_later + drive_first * there_first
                )
                if own:
                    back = drive_first * (coef[p, pl.ds(k, 24, stride=16), :] + BASE[s + 2])
                    if d == 0:
                        push(z + 1 + s, back)
                    else:
                        push(z + 1, roll(back, s, d - 1))
        turn[z, pl.ds(15, 24, stride=16), :] = H * later * v + H * first * u
    for p in range(4):
        lam0[p] = pushed[2 + p][own_rows] + edge[p]
    done(2)

    for z in range(6):
        tiles[z] = turn[z, 7 * 16 : 17 * 16, :].astype(BF16)
    done(1)
    need(4)
    sum_w = None
    sum_g = None
    for p in range(4):
        mine = jnp.concatenate(
            [tiles[p + 1, (y + 1) * 16 : (y + 2) * 16, :] for y in range(8)], axis=1
        )
        part_w = lax.dot_general(
            mine, columns_own[p * 144 : p * 144 + 432, :], NT, preferred_element_type=F32
        )
        part_g = lax.dot_general(mine, mine, NT, preferred_element_type=F32)
        sum_w = part_w if sum_w is None else sum_w + part_w
        sum_g = part_g if sum_g is None else sum_g + part_g
    row[...] = jnp.zeros((16, 512), F32)
    row[:, 0:432] = sum_w
    row[:, 432:448] = sum_g
    for t in range(4):
        mixed[t * 16 : (t + 1) * 16, :] = row[:, t * 128 : (t + 1) * 128]
    need(5)
    mixed[64:256, :] = gram[...]


def stage_three(need, done, tiles, w_back, grad_feat, shifted, columns, turn_out):
    need(0)
    shift_value = shift_both()
    for z in range(6):
        shifted[1, z] = tiles[z]
        both = jnp.dot(tiles[z], shift_value, preferred_element_type=F32).astype(BF16)
        shifted[0, z] = both[:, :128]
        shifted[2, z] = both[:, 128:]

    def fill(z, carry):
        fill_columns(columns, shifted, z, range(8))
        return carry

    lax.fori_loop(0, 6, fill, 0)
    need(1)
    w_value = w_back[...]
    for p in range(4):
        plane = jnp.dot(
            w_value, columns[p * 144 : p * 144 + 432, :], preferred_element_type=F32
        )
        for y in range(8):
            turn_out[pl.ds(p * 8 + y, 16, stride=32), :] = plane[:, y * 128 : (y + 1) * 128]
    for c in range(16):
        grad_feat[c] = turn_out[c * 32 : (c + 1) * 32, :].astype(BF16)


def pieces(value):
    one = value.astype(BF16)
    rest = value - one.astype(F32)
    two = rest.astype(BF16)
    three = (rest - two.astype(F32)).astype(BF16)
    return one, two, three


def to_channel_major(value):
    i = lax.broadcasted_iota(jnp.int32, (432, 432), 0)
    j = lax.broadcasted_iota(jnp.int32, (432, 432), 1)
    place = jnp.where((i % 16) * 27 + i // 16 == j, 1.0, 0.0).astype(BF16)
    parts = [jnp.dot(v, place, preferred_element_type=F32) for v in pieces(value)]
    return parts[2] + parts[1] + parts[0]


def total_to_all(parts, out):
    total = parts[0]
    for n in range(1, parts.shape[0]):
        total = total + parts[n]
    for n in range(out.shape[0]):
        out[n] = total


def finish(cells, chunks, out_w, out_p, out_g, line, row, square, block, turn):
    for t in range(4):
        row[:, t * 128 : (t + 1) * 128] = chunks[t * 16 : (t + 1) * 16, :]
    for t in range(10):
        line[:, t * 128 : (t + 1) * 128] = chunks[64 + t * 16 : 80 + t * 16, :] * (1.0 / cells)
    out_g[...] = row[:, 432:448] * (1.0 / cells)
    for dz in range(3):
        for a in range(3):
            for b in range(3):
                group = (a * 3 + b) * 16
                for a_other in range(3):
                    to = dz * 144 + a_other * 48
                    at = dz * 400 + (a_other - a + 2) * 80 + (2 - b) * 16
                    square[group : group + 16, to : to + 48] = line[:, at : at + 48]
    square[144:288, 144:432] = square[0:144, 0:288]
    square[288:432, 288:432] = square[0:144, 0:144]
    block[...] = jnp.zeros((256, 256), F32)
    block[0:144, 0:144] = square[0:144, 144:288]
    turned = jnp.transpose(block[...])[0:144, 0:144]
    square[144:288, 0:144] = turned
    square[288:432, 144:288] = turned
    block[0:144, 0:144] = square[0:144, 288:432]
    square[288:432, 0:144] = jnp.transpose(block[...])[0:144, 0:144]
    square[432:448, :] = row[:, 0:432] * (1.0 / math.sqrt(cells))
    ready = to_channel_major(square[...])
    out_w[...] = ready[432:448, :]
    for t in range(4):
        wide = min(128, 432 - t * 128)
        for o in range(27):
            turn[t, pl.ds(o, 16, stride=27), 0:wide] = ready[
                o * 16 : (o + 1) * 16, t * 128 : t * 128 + wide
            ]
        out_p[:, t * 128 : t * 128 + wide] = turn[t, :, 0:wide]


def neighbours(to_next, to_prev, axis):
    size = lax.axis_size(axis)
    up = [(i, (i + 1) % size) for i in range(size)]
    down = [(j, i) for i, j in up]
    return lax.ppermute(to_next, axis, up), lax.ppermute(to_prev, axis, down)


def body(features, field, velocity, weight, cotangent):
    nz, ny = lax.axis_size("gz"), lax.axis_size("gy")
    cells = float(4096 * nz * ny)
    by_offset = weight.reshape(16, 16, 27)
    w_rows = by_offset.transpose(0, 2, 1).reshape(16, 432)
    w_back = by_offset.transpose(1, 2, 0)[:, ::-1, :].reshape(16, 432)
    tile = (16, 128)
    own_feat, own_fields, to_next, to_prev = call(
        pack_y,
        [((32,) + tile, BF16), ((20,) + tile, BF16), ((4 * PREV + 20,) + tile, BF16),
         ((4 * NEXT + 20,) + tile, BF16)],
        [pltpu.VMEM((512, 128), F32)],
        (features.reshape(16, 32, 128), field, velocity, cotangent),
    )
    before, after = neighbours(to_next, to_prev, "gy")
    along_z = (ROWS_IN + 3 * (UP[1] - UP[0]), ROWS_IN + 3 * (DOWN[1] - DOWN[0]) + 10)
    to_up, to_down = pl.pallas_call(
        pack_z,
        out_shape=[jax.ShapeDtypeStruct((n,) + tile, BF16) for n in along_z],
        in_specs=[_HBM] * 4,
        out_specs=[_HBM] * 2,
        scratch_shapes=[pltpu.VMEM((n,) + tile, BF16) for n in along_z]
        + [pltpu.SemaphoreType.DMA((15,)), pltpu.SemaphoreType.DMA((2,))],
        compiler_params=pltpu.CompilerParams(vmem_limit_bytes=64 * 1024 * 1024),
    )(own_feat, own_fields, before, after)
    below, above = neighbours(to_up, to_down, "gz")
    send_up, send_down, columns_own, coef, state = call(
        stage_one,
        [((10, 16, 128), F32), ((10, 16, 128), F32), ((864, 1024), BF16),
         ((4, 384, 128), F32), ((48, 24, 128), F32)],
        [pltpu.VMEM((3, 7, ROWS_IN * 16, 128), BF16), pltpu.VMEM((1008, ROWS_OUT * 128), BF16),
         pltpu.VMEM((128, 128), F32)],
        (own_feat, before, after, below, above, field, velocity, cotangent, w_rows),
    )
    below1, above1 = neighbours(send_up, send_down, "gz")
    (gram,) = call(
        patch_gram,
        [((192, 128), F32)],
        [pltpu.VMEM((144, 512), F32), pltpu.VMEM((16, 1280), F32)],
        (columns_own,),
        5e8,
    )
    mixed, tiles, grad_field = call(
        stage_two,
        [((256, 128), F32), ((6, 160, 128), BF16), ((4, 8, 128), F32)],
        [pltpu.VMEM((10, 24, 128), F32), pltpu.VMEM((7, 24, 128), F32),
         pltpu.VMEM((6, 384, 128), F32), pltpu.VMEM((16, 512), F32)],
        (below1, above1, state, coef, columns_own, gram),
    )
    (grad_feat,) = call(
        stage_three,
        [((16, 32, 128), BF16)],
        [pltpu.VMEM((3, 6, 160, 128), BF16), pltpu.VMEM((864, 1024), BF16), pltpu.VMEM((512, 128), F32)],
        (tiles, w_back),
        1e8,
        (mixed,),
    )
    half = nz // 2
    line = [[(h * half + i) * ny + j for h in range(2) for j in range(ny)] for i in range(half)]
    plane = [[(h * half + i) * ny + j for i in range(half)] for h in range(2) for j in range(ny)]
    rows = 256 // len(line[0])
    axes = ("gz", "gy")
    parts = mixed.reshape(2 * ny, rows, 128)
    parts = lax.all_to_all(parts, axes, 0, 0, axis_index_groups=line)
    (parts,) = call_small(total_to_all, [((half, rows, 128), F32)], [], (parts,))
    parts = lax.all_to_all(parts, axes, 0, 0, axis_index_groups=plane)
    (parts,) = call_small(total_to_all, [((2 * ny, rows, 128), F32)], [], (parts,))
    parts = lax.all_to_all(parts, axes, 0, 0, axis_index_groups=line).reshape(256, 128)
    grad_weight, factor_patch, factor_grad = call_small(
        lambda *refs: finish(cells, *refs),
        [((16, 432), F32), ((432, 432), F32), ((16, 16), F32)],
        [pltpu.VMEM((16, 1280), F32), pltpu.VMEM((16, 512), F32), pltpu.VMEM((448, 432), F32),
         pltpu.VMEM((256, 256), F32), pltpu.VMEM((4, 432, 128), F32)],
        (parts,),
    )
    return (grad_field, grad_feat.reshape(16, 4, 8, 128), grad_weight, factor_patch, factor_grad)


def solution(mesh):
    placed = (
        P(None, "gz", "gy", None),
        P("gz", "gy", None),
        P(None, "gz", "gy", None),
        P(),
        P("gz", "gy", None),
    )
    return jax.shard_map(
        body,
        mesh=mesh,
        in_specs=placed,
        out_specs=(P("gz", "gy", None), P(None, "gz", "gy", None), P(), P(), P()),
        check_vma=False,
    )
```

```python
import math

import jax
import jax.numpy as jnp
from jax import lax
from jax.experimental import pallas as pl
from jax.experimental.pallas import tpu as pltpu
from jax.sharding import PartitionSpec as P

H = 0.15
BASE = (2.0 / 60.0, -13.0 / 60.0, 47.0 / 60.0, 27.0 / 60.0, -3.0 / 60.0)
F32 = jnp.float32
BF16 = jnp.bfloat16
NT = (((1,), (1,)), ((), ()))

ROWS_IN = 19
ROWS_OUT = 17
PREV = 5
NEXT = 6

_HBM = pl.BlockSpec(memory_space=pltpu.HBM)


def call(kernel, outs, scratch, args, flops=1e6, follows=()):
    n_in, n_out = len(args), len(outs)

    def run(*refs):
        source, refs = refs[:n_in], refs[n_in + len(follows) :]
        target = refs[:n_out]
        refs = (None,) * n_in + tuple(refs)
        arrived, left = refs[n_in + n_out : n_in + n_out + 2]
        held = refs[n_in + n_out + 2 :]
        here, there = held[:n_in], held[n_in : n_in + n_out]
        coming = {i: pltpu.make_async_copy(source[i], here[i], arrived.at[i]) for i in range(n_in)}
        going = {i: pltpu.make_async_copy(there[i], target[i], left.at[i]) for i in range(n_out)}
        sent = []
        for i in range(n_in):
            coming[i].start()

        def need(*which):
            for i in which:
                coming.pop(i).wait()

        def done(*which):
            for i in which:
                going[i].start()
                sent.append(i)

        kernel(need, done, *held)
        need(*list(coming))
        done(*[i for i in range(n_out) if i not in sent])
        for i in range(n_out):
            going[i].wait()

    return pl.pallas_call(
        run,
        out_shape=[jax.ShapeDtypeStruct(s, t) for s, t in outs],
        in_specs=[_HBM] * (n_in + len(follows)),
        out_specs=[_HBM] * n_out,
        scratch_shapes=[pltpu.SemaphoreType.DMA((n_in,)), pltpu.SemaphoreType.DMA((n_out,))]
        + [pltpu.VMEM(a.shape, a.dtype) for a in args]
        + [pltpu.VMEM(s, t) for s, t in outs]
        + scratch,
        compiler_params=pltpu.CompilerParams(vmem_limit_bytes=64 * 1024 * 1024),
        cost_estimate=pl.CostEstimate(flops=int(flops), bytes_accessed=4000000, transcendentals=0),
    )(*args, *follows)


def call_small(kernel, outs, scratch, args):
    return pl.pallas_call(
        kernel,
        out_shape=[jax.ShapeDtypeStruct(s, t) for s, t in outs],
        in_specs=[pl.BlockSpec(memory_space=pltpu.VMEM)] * len(args),
        out_specs=[pl.BlockSpec(memory_space=pltpu.VMEM)] * len(outs),
        scratch_shapes=scratch,
        compiler_params=pltpu.CompilerParams(vmem_limit_bytes=16 * 1024 * 1024),
        cost_estimate=pl.CostEstimate(flops=1000000, bytes_accessed=4000000, transcendentals=0),
    )(*args)


def shift_both():
    i = lax.broadcasted_iota(jnp.int32, (128, 256), 0)
    j = lax.broadcasted_iota(jnp.int32, (128, 256), 1)
    source = jnp.where(j < 128, j + 127, j + 1) % 128
    return jnp.where(i == source, 1.0, 0.0).astype(BF16)


def roll(value, shift, axis):
    shift %= value.shape[axis]
    return value if shift == 0 else pltpu.roll(value, shift, axis)


def split(plane):
    lead = plane.astype(BF16).astype(F32)
    return jnp.concatenate([lead, plane - lead], axis=0).astype(BF16)


def join(tile):
    both = tile.astype(F32)
    return both[:8] + both[8:]


ORDER = [
    ("l", 3), (0, 3), (1, 3), (2, 3), ("u", 3), ("u", 1), ("u", 2), ("u", 0), ("l", 0), ("l", 1),
    (0, 0), (1, 0), (2, 0), ("l", 2), (0, 1), (0, 2), (1, 1), (1, 2), (2, 1), (2, 2),
]
UP, DOWN = (0, 7), (5, 13)


def pack_y(
    need, done, feat, field, vel, cot, own_feat, own_fields, to_next, to_prev, turn
):
    need(0)
    for c in range(16):
        turn[pl.ds(c, 32, stride=16), :] = feat[c].astype(F32)
    for zy in range(32):
        tile = turn[zy * 16 : (zy + 1) * 16, :].astype(BF16)
        own_feat[zy] = tile
        z, y = divmod(zy, 8)
        if y >= 8 - PREV:
            to_next[z * PREV + y - (8 - PREV)] = tile
        if y < NEXT:
            to_prev[z * NEXT + y] = tile
    need(1, 2, 3)
    for i, (kind, z) in enumerate(ORDER):
        tile = split(field[z] if kind == "u" else cot[z] if kind == "l" else vel[kind, z])
        own_fields[i] = tile
        to_next[4 * PREV + i] = tile
        to_prev[4 * NEXT + i] = tile


def pack_z(own_feat, own_fields, before, after, to_up, to_down, up, down, moved, left):
    copies = []

    def move(source, at, out, to, count):
        copies.append(
            pltpu.make_async_copy(
                source.at[at : at + count], out.at[to : to + count], moved.at[len(copies)]
            )
        )

    for out, z, (first, stop) in ((up, 3, UP), (down, 0, DOWN)):
        n = stop - first
        move(before, z * PREV, out, 0, PREV)
        move(own_feat, z * 8, out, PREV, 8)
        move(after, z * NEXT, out, PREV + 8, NEXT)
        move(before, 4 * PREV + first, out, ROWS_IN, n)
        move(own_fields, first, out, ROWS_IN + n, n)
        move(after, 4 * NEXT + first, out, ROWS_IN + 2 * n, n)
    second = ROWS_IN + 3 * (DOWN[1] - DOWN[0])
    move(before, 2 * PREV - 1, down, second, 1)
    move(own_feat, 8, down, second + 1, 8)
    move(after, NEXT, down, second + 9, 1)
    for copy in copies:
        copy.start()
    out_up = pltpu.make_async_copy(up, to_up, left.at[0])
    out_down = pltpu.make_async_copy(down, to_down, left.at[1])
    for copy in copies[:6]:
        copy.wait()
    out_up.start()
    for copy in copies[6:]:
        copy.wait()
    out_down.start()
    out_up.wait()
    out_down.wait()


def fill_columns(columns, shifted, z, rows):
    for a in range(3):
        for b in range(3):
            at = pl.multiple_of(z * 144 + (a * 3 + b) * 16, 16)
            for y in rows:
                columns[pl.ds(at, 16), y * 128 : (y + 1) * 128] = shifted[
                    b, z, (y + a) * 16 : (y + a + 1) * 16, :
                ]


U0, LAM2, U1, LAM1, FACE = slice(0, 10), slice(10, 17), slice(35, 39), slice(39, 47), 47
VEL = (slice(17, 23), slice(23, 29), slice(29, 35))
FAR = [(2, 2), (3, 1), (3, 2), (1, -2), (0, -1), (0, -2)]


def stage_one(
    need, done, own_feat, before, after, below, above, field, vel, cot, w_rows,
    send_up, send_down, columns_own, coef, kept,
    shifted, columns, coef_above,
):
    u0, lam2 = kept.at[U0], kept.at[LAM2]
    velx = [kept.at[v] for v in VEL]
    shift_value = shift_both()
    need(0, 1, 2, 3, 4)
    for z in range(6):
        if z == 0:
            tiles = below[0:ROWS_IN].reshape(ROWS_IN * 16, 128)
        elif z == 5:
            tiles = above[0:ROWS_IN].reshape(ROWS_IN * 16, 128)
        else:
            p = z - 1
            tiles = jnp.concatenate(
                [
                    before[p * PREV : (p + 1) * PREV].reshape(PREV * 16, 128),
                    own_feat[p * 8 : (p + 1) * 8].reshape(128, 128),
                    after[p * NEXT : (p + 1) * NEXT].reshape(NEXT * 16, 128),
                ],
                axis=0,
            )
        shifted[1, z] = tiles
        both = jnp.dot(tiles, shift_value, preferred_element_type=F32).astype(BF16)
        shifted[0, z] = both[:, :128]
        shifted[2, z] = both[:, 128:]
    second = ROWS_IN + 3 * (DOWN[1] - DOWN[0])
    tiles = above[second : second + 10].reshape(160, 128)
    both = jnp.dot(tiles, shift_value, preferred_element_type=F32).astype(BF16)
    shifted[0, 6, 64:224, :] = both[:, :128]
    shifted[1, 6, 64:224, :] = tiles
    shifted[2, 6, 64:224, :] = both[:, 128:]

    need(5, 6, 7)

    def extended(kind, z, own):
        i = ORDER.index((kind, z))
        return jnp.concatenate(
            [join(before[4 * PREV + i]), own, join(after[4 * NEXT + i])], axis=0
        )

    def received(source, part, kind, z):
        n = part[1] - part[0]
        at = ROWS_IN + ORDER.index((kind, z)) - part[0]
        return jnp.concatenate([join(source[at + n * j]) for j in range(3)], axis=0)

    for j in range(3):
        u0[j] = received(below, UP, "u", 1 + j)
        u0[7 + j] = received(above, DOWN, "u", j)
        velx[j][0] = received(below, UP, j, 3)
        velx[j][5] = received(above, DOWN, j, 0)
    lam2[0] = received(below, UP, "l", 3)
    lam2[5] = received(above, DOWN, "l", 0)
    lam2[6] = received(above, DOWN, "l", 1)
    for z in range(4):
        u0[3 + z] = extended("u", z, field[z])
        lam2[1 + z] = extended("l", z, cot[z])
        for d in range(3):
            velx[d][1 + z] = extended(d, z, vel[d, z])

    def fill(z, carry):
        fill_columns(columns, shifted, z, range(ROWS_OUT))
        return carry

    lax.fori_loop(0, 6, fill, 0)
    fill_columns(columns, shifted, 6, range(4, 12))

    columns_own[...] = columns[0:864, 512:1536]
    done(2)
    need(8)
    w_value = w_rows[...]
    for p in range(4):
        plane = jnp.dot(
            w_value, columns[p * 144 : p * 144 + 432, :], preferred_element_type=F32
        )
        for y in range(ROWS_OUT):
            coef[p, (4 + y) * 16 : (5 + y) * 16, :] = plane[:, y * 128 : (y + 1) * 128]

    done(3)
    plane = jnp.dot(w_value, columns[576:1008, 512:1536], preferred_element_type=F32)
    for y in range(8):
        coef_above[y * 16 : (y + 1) * 16, :] = plane[:, y * 128 : (y + 1) * 128]

    def a(p, k):
        value = coef[p, pl.ds(k, 24, stride=16), :]
        return value + BASE[k % 5]

    pushed = [None] * 8

    def push(slot, value):
        pushed[slot] = value if pushed[slot] is None else pushed[slot] + value

    faces_z = []
    states = []
    carried = {}
    for p in range(4):
        rate = 1.0 + H * coef[p, pl.ds(15, 24, stride=16), :]
        u = u0[3 + p]
        lam = lam2[1 + p]
        state = u * rate
        push(p + 2, lam * rate)
        for d in range(3):
            beyond = lam2[2 + p] if d == 0 else roll(lam, -1, d - 1)
            drive = (-H) * (lam - beyond) * velx[d][1 + p]
            face = None
            for s in range(-2, 3):
                weight = a(p, 5 * d + s + 2)
                term = weight * (u0[3 + p + s] if d == 0 else roll(u, -s, d - 1))
                face = term if face is None else face + term
                back = drive * weight
                if d == 0:
                    push(p + 2 + s, back)
                    if (p, s) in FAR:
                        carried[p, s] = velx[0][1 + p] * weight
                else:
                    push(p + 2, roll(back, s, d - 1))
            face = (H * velx[d][1 + p]) * face
            if d == 0:
                faces_z.append(face)
                state = state - (face if p == 0 else face - faces_z[p - 1])
            else:
                state = state - (face - roll(face, 1, d - 1))
        states.append(state)
    u1_part, lam_part = kept.at[U1], kept.at[LAM1]
    for p in range(4):
        u1_part[p] = states[p]
    for j in range(8):
        lam_part[j] = pushed[j]
    kept[FACE] = faces_z[3]
    ups = [states[1], states[2], states[3], faces_z[3], pushed[5], pushed[6], pushed[7], pushed[4]]
    downs = [states[0], states[1], states[2], pushed[2], pushed[3], pushed[0], pushed[1], pushed[4]]
    for j in range(8):
        send_up[j] = ups[j][4:20]
        send_down[j] = downs[j][4:20]
    for out, keys in ((send_up, FAR[:3]), (send_down, FAR[3:])):
        out[8, 0:8, :] = carried[keys[0]][8:16]
        out[8, 8:16, :] = carried[keys[1]][8:16]
        out[9, 0:8, :] = carried[keys[2]][8:16]
        out[9, 8:16, :] = carried[keys[2]][8:16]
    face = (-H) * (lam2[5, 8:16] - lam2[6, 8:16]) * velx[0][5, 8:16]
    face = face * (BASE[0] + coef_above[pl.ds(0, 8, stride=16), :])
    send_down[7, 4:12, :] = pushed[4][8:16] + face


def patch_gram(need, done, columns_own, down, gram, down_out, full, line):
    need(1)
    down_out[...] = down[...]
    done(1)
    need(0)
    total = None
    for p in range(4):
        part = lax.dot_general(
            columns_own[p * 144 : (p + 1) * 144, :],
            columns_own[p * 144 : p * 144 + 432, :],
            NT,
            preferred_element_type=F32,
        )
        total = part if total is None else total + part
    full[:, 0:432] = total
    line[...] = jnp.zeros((16, 1280), F32)

    def put(dz, dy, dx, count, a, b, a_other):
        to = dz * 400 + (dy + 2) * 80 + (dx + 2) * 16
        at = dz * 144 + a_other * 48
        group = (a * 3 + b) * 16
        line[:, to : to + 16 * count] = full[group : group + 16, at : at + 16 * count]

    for dz in range(3):
        for a in range(3):
            put(dz, a, 0, 3, 0, 0, a)
            for b in (1, 2):
                put(dz, a, -b, 1, 0, b, a)
        for a in (1, 2):
            put(dz, -a, 0, 3, a, 0, 0)
            for b in (1, 2):
                put(dz, -a, -b, 1, a, b, 0)
    for t in range(10):
        gram[t * 16 : (t + 1) * 16, :] = line[:, t * 128 : (t + 1) * 128]
    gram[160:192, :] = jnp.zeros((32, 128), F32)


def stage_two(
    need, done, below, above, state, coef, columns_own, gram,
    mixed, tiles, lam0,
    u1, lam1, turn, row,
):
    u0, lam2, u1_part, lam_part = state.at[U0], state.at[LAM2], state.at[U1], state.at[LAM1]
    velx = [state.at[v] for v in VEL]
    need(0, 1, 2, 3)

    def padded(value):
        zero = jnp.zeros((4, 128), F32)
        return jnp.concatenate([zero, value, zero], axis=0)

    low = [padded(below[j]) for j in range(8)]
    high = [padded(above[j]) for j in range(8)]
    for j in range(3):
        u1[j] = low[j]
        u1[7 + j] = high[j] + (state[FACE] if j == 0 else 0.0)
        u1[4 + j] = u1_part[1 + j]
    u1[3] = u1_part[0] + low[3]
    lam1[0] = low[4] + lam_part[1]
    lam1[1] = lam_part[2] + low[5]
    lam1[2] = lam_part[3] + low[6]
    lam1[3] = lam_part[4] + high[5]
    lam1[4] = lam_part[5] + high[6]
    lam1[5] = high[3] + lam_part[6]
    lam1[6] = high[4] + lam_part[7]

    pushed = [None] * 8

    def push(slot, value):
        pushed[slot] = value if pushed[slot] is None else pushed[slot] + value

    own_rows = slice(8, 16)
    lowest = lam_part[0][own_rows] + low[7][own_rows]
    highest = high[7][own_rows]
    fall = [lowest, lam1[0, own_rows], lam1[1, own_rows]]
    rise = [lam1[5, own_rows], lam1[6, own_rows], highest]
    outer = [(-H) * (fall[0] - fall[1]), (-H) * (fall[1] - fall[2])]
    inner = [(-H) * (rise[0] - rise[1]), (-H) * (rise[1] - rise[2])]
    edge = [
        outer[0] * below[8, 0:8, :] + outer[1] * below[8, 8:16, :],
        outer[1] * below[9, 0:8, :],
        inner[0] * above[9, 0:8, :],
        inner[0] * above[8, 8:16, :] + inner[1] * above[8, 0:8, :],
    ]

    for z in range(6):
        later, first = lam2[z], lam1[z]
        v, u = u1[z + 2], u0[z + 2]
        own = 1 <= z <= 4
        p = z - 1
        if own:
            push(z + 1, first * (1.0 + H * coef[p, pl.ds(15, 24, stride=16), :]))
        for d in range(3):
            speed = velx[d][z]
            beyond_later = lam2[z + 1] if d == 0 else roll(later, -1, d - 1)
            beyond_first = lam1[z + 1] if d == 0 else roll(first, -1, d - 1)
            drive_later = (-H) * (later - beyond_later) * speed
            drive_first = (-H) * (first - beyond_first) * speed
            for s in range(-2, 3):
                k = 5 * d + s + 2
                there_later = u1[z + 2 + s] if d == 0 else roll(v, -s, d - 1)
                there_first = u0[z + 2 + s] if d == 0 else roll(u, -s, d - 1)
                turn[z, pl.ds(k, 24, stride=16), :] = (
                    drive_later * there_later + drive_first * there_first
                )
                if own:
                    back = drive_first * (coef[p, pl.ds(k, 24, stride=16), :] + BASE[s + 2])
                    if d == 0:
                        push(z + 1 + s, back)
                    else:
                        push(z + 1, roll(back, s, d - 1))
        turn[z, pl.ds(15, 24, stride=16), :] = H * later * v + H * first * u
    for p in range(4):
        lam0[p] = pushed[2 + p][own_rows] + edge[p]
    done(2)

    for z in range(6):
        tiles[z] = turn[z, 7 * 16 : 17 * 16, :].astype(BF16)
    done(1)
    need(4)
    sum_w = None
    sum_g = None
    for p in range(4):
        mine = jnp.concatenate(
            [tiles[p + 1, (y + 1) * 16 : (y + 2) * 16, :] for y in range(8)], axis=1
        )
        part_w = lax.dot_general(
            mine, columns_own[p * 144 : p * 144 + 432, :], NT, preferred_element_type=F32
        )
        part_g = lax.dot_general(mine, mine, NT, preferred_element_type=F32)
        sum_w = part_w if sum_w is None else sum_w + part_w
        sum_g = part_g if sum_g is None else sum_g + part_g
    row[...] = jnp.zeros((16, 512), F32)
    row[:, 0:432] = sum_w
    row[:, 432:448] = sum_g
    for t in range(4):
        mixed[t * 16 : (t + 1) * 16, :] = row[:, t * 128 : (t + 1) * 128]
    need(5)
    mixed[64:256, :] = gram[...]


def stage_three(need, done, tiles, w_back, grad_feat, shifted, columns, turn_out):
    need(0)
    shift_value = shift_both()
    for z in range(6):
        shifted[1, z] = tiles[z]
        both = jnp.dot(tiles[z], shift_value, preferred_element_type=F32).astype(BF16)
        shifted[0, z] = both[:, :128]
        shifted[2, z] = both[:, 128:]

    def fill(z, carry):
        fill_columns(columns, shifted, z, range(8))
        return carry

    lax.fori_loop(0, 6, fill, 0)
    need(1)
    w_value = w_back[...]
    for p in range(4):
        plane = jnp.dot(
            w_value, columns[p * 144 : p * 144 + 432, :], preferred_element_type=F32
        )
        for y in range(8):
            turn_out[pl.ds(p * 8 + y, 16, stride=32), :] = plane[:, y * 128 : (y + 1) * 128]
    for c in range(16):
        grad_feat[c] = turn_out[c * 32 : (c + 1) * 32, :].astype(BF16)


def pieces(value):
    one = value.astype(BF16)
    rest = value - one.astype(F32)
    two = rest.astype(BF16)
    return one, two


def to_channel_major(value):
    i = lax.broadcasted_iota(jnp.int32, (432, 432), 0)
    j = lax.broadcasted_iota(jnp.int32, (432, 432), 1)
    place = jnp.where((i % 16) * 27 + i // 16 == j, 1.0, 0.0).astype(BF16)
    parts = [jnp.dot(v, place, preferred_element_type=F32) for v in pieces(value)]
    return parts[1] + parts[0]


def total_to_all(parts, out):
    total = parts[0]
    for n in range(1, parts.shape[0]):
        total = total + parts[n]
    for n in range(out.shape[0]):
        out[n] = total


def finish(cells, chunks, out_w, out_p, out_g, line, row, square, block, turn):
    for t in range(4):
        row[:, t * 128 : (t + 1) * 128] = chunks[t * 16 : (t + 1) * 16, :]
    for t in range(10):
        line[:, t * 128 : (t + 1) * 128] = chunks[64 + t * 16 : 80 + t * 16, :] * (1.0 / cells)
    out_g[...] = row[:, 432:448] * (1.0 / cells)
    for dz in range(3):
        for a in range(3):
            for b in range(3):
                group = (a * 3 + b) * 16
                for a_other in range(3):
                    to = dz * 144 + a_other * 48
                    at = dz * 400 + (a_other - a + 2) * 80 + (2 - b) * 16
                    square[group : group + 16, to : to + 48] = line[:, at : at + 48]
    square[144:288, 144:432] = square[0:144, 0:288]
    square[288:432, 288:432] = square[0:144, 0:144]
    block[...] = jnp.zeros((256, 256), F32)
    block[0:144, 0:144] = square[0:144, 144:288]
    turned = jnp.transpose(block[...])[0:144, 0:144]
    square[144:288, 0:144] = turned
    square[288:432, 144:288] = turned
    block[0:144, 0:144] = square[0:144, 288:432]
    square[288:432, 0:144] = jnp.transpose(block[...])[0:144, 0:144]
    square[432:448, :] = row[:, 0:432] * (1.0 / math.sqrt(cells))
    ready = to_channel_major(square[...])
    out_w[...] = ready[432:448, :]
    for t in range(4):
        wide = min(128, 432 - t * 128)
        for o in range(27):
            turn[t, pl.ds(o, 16, stride=27), 0:wide] = ready[
                o * 16 : (o + 1) * 16, t * 128 : t * 128 + wide
            ]
        out_p[:, t * 128 : t * 128 + wide] = turn[t, :, 0:wide]


def neighbours(to_next, to_prev, axis):
    size = lax.axis_size(axis)
    up = [(i, (i + 1) % size) for i in range(size)]
    down = [(j, i) for i, j in up]
    return lax.ppermute(to_next, axis, up), lax.ppermute(to_prev, axis, down)


def body(features, field, velocity, weight, cotangent):
    nz, ny = lax.axis_size("gz"), lax.axis_size("gy")
    cells = float(4096 * nz * ny)
    by_offset = weight.reshape(16, 16, 27)
    w_rows = by_offset.transpose(0, 2, 1).reshape(16, 432)
    w_back = by_offset.transpose(1, 2, 0)[:, ::-1, :].reshape(16, 432)
    tile = (16, 128)
    own_feat, own_fields, to_next, to_prev = call(
        pack_y,
        [((32,) + tile, BF16), ((20,) + tile, BF16), ((4 * PREV + 20,) + tile, BF16),
         ((4 * NEXT + 20,) + tile, BF16)],
        [pltpu.VMEM((512, 128), F32)],
        (features.reshape(16, 32, 128), field, velocity, cotangent),
    )
    before, after = neighbours(to_next, to_prev, "gy")
    along_z = (ROWS_IN + 3 * (UP[1] - UP[0]), ROWS_IN + 3 * (DOWN[1] - DOWN[0]) + 10)
    to_up, to_down = pl.pallas_call(
        pack_z,
        out_shape=[jax.ShapeDtypeStruct((n,) + tile, BF16) for n in along_z],
        in_specs=[_HBM] * 4,
        out_specs=[_HBM] * 2,
        scratch_shapes=[pltpu.VMEM((n,) + tile, BF16) for n in along_z]
        + [pltpu.SemaphoreType.DMA((15,)), pltpu.SemaphoreType.DMA((2,))],
        compiler_params=pltpu.CompilerParams(vmem_limit_bytes=64 * 1024 * 1024),
    )(own_feat, own_fields, before, after)
    below, above = neighbours(to_up, to_down, "gz")
    send_up, send_down, columns_own, coef, state = call(
        stage_one,
        [((10, 16, 128), F32), ((10, 16, 128), F32), ((864, 1024), BF16),
         ((4, 384, 128), F32), ((48, 24, 128), F32)],
        [pltpu.VMEM((3, 7, ROWS_IN * 16, 128), BF16), pltpu.VMEM((1008, ROWS_OUT * 128), BF16),
         pltpu.VMEM((128, 128), F32)],
        (own_feat, before, after, below, above, field, velocity, cotangent, w_rows),
    )
    gram, send_down = call(
        patch_gram,
        [((192, 128), F32), ((10, 16, 128), F32)],
        [pltpu.VMEM((144, 512), F32), pltpu.VMEM((16, 1280), F32)],
        (columns_own, send_down),
        5e8,
    )
    below1, above1 = neighbours(send_up, send_down, "gz")
    mixed, tiles, grad_field = call(
        stage_two,
        [((256, 128), F32), ((6, 160, 128), BF16), ((4, 8, 128), F32)],
        [pltpu.VMEM((10, 24, 128), F32), pltpu.VMEM((7, 24, 128), F32),
         pltpu.VMEM((6, 384, 128), F32), pltpu.VMEM((16, 512), F32)],
        (below1, above1, state, coef, columns_own, gram),
    )
    (grad_feat,) = call(
        stage_three,
        [((16, 32, 128), BF16)],
        [pltpu.VMEM((3, 6, 160, 128), BF16), pltpu.VMEM((864, 1024), BF16), pltpu.VMEM((512, 128), F32)],
        (tiles, w_back),
        1e8,
        (mixed,),
    )
    half = nz // 2
    line = [[(h * half + i) * ny + j for h in range(2) for j in range(ny)] for i in range(half)]
    plane = [[(h * half + i) * ny + j for i in range(half)] for h in range(2) for j in range(ny)]
    rows = 256 // len(line[0])
    axes = ("gz", "gy")
    parts = mixed.reshape(2 * ny, rows, 128)
    parts = lax.all_to_all(parts, axes, 0, 0, axis_index_groups=line)
    (parts,) = call_small(total_to_all, [((half, rows, 128), F32)], [], (parts,))
    parts = lax.all_to_all(parts, axes, 0, 0, axis_index_groups=plane)
    (parts,) = call_small(total_to_all, [((2 * ny, rows, 128), F32)], [], (parts,))
    parts = lax.all_to_all(parts, axes, 0, 0, axis_index_groups=line).reshape(256, 128)
    grad_weight, factor_patch, factor_grad = call_small(
        lambda *refs: finish(cells, *refs),
        [((16, 432), F32), ((432, 432), F32), ((16, 16), F32)],
        [pltpu.VMEM((16, 1280), F32), pltpu.VMEM((16, 512), F32), pltpu.VMEM((448, 432), F32),
         pltpu.VMEM((256, 256), F32), pltpu.VMEM((4, 432, 128), F32)],
        (parts,),
    )
    return (grad_field, grad_feat.reshape(16, 4, 8, 128), grad_weight, factor_patch, factor_grad)


def solution(mesh):
    placed = (
        P(None, "gz", "gy", None),
        P("gz", "gy", None),
        P(None, "gz", "gy", None),
        P(),
        P("gz", "gy", None),
    )
    return jax.shard_map(
        body,
        mesh=mesh,
        in_specs=placed,
        out_specs=(P("gz", "gy", None), P(None, "gz", "gy", None), P(), P(), P()),
        check_vma=False,
    )
```

```python
import math

import jax
import jax.numpy as jnp
from jax import lax
from jax.experimental import pallas as pl
from jax.experimental.pallas import tpu as pltpu
from jax.sharding import PartitionSpec as P

H = 0.15
BASE = (2.0 / 60.0, -13.0 / 60.0, 47.0 / 60.0, 27.0 / 60.0, -3.0 / 60.0)
F32 = jnp.float32
BF16 = jnp.bfloat16
NT = (((1,), (1,)), ((), ()))

ROWS_IN = 19
ROWS_OUT = 17
PREV = 5
NEXT = 6

_HBM = pl.BlockSpec(memory_space=pltpu.HBM)


def call(kernel, outs, scratch, args, flops=1e6, follows=()):
    n_in, n_out = len(args), len(outs)

    def run(*refs):
        source, refs = refs[:n_in], refs[n_in + len(follows) :]
        target = refs[:n_out]
        refs = (None,) * n_in + tuple(refs)
        arrived, left = refs[n_in + n_out : n_in + n_out + 2]
        held = refs[n_in + n_out + 2 :]
        here, there = held[:n_in], held[n_in : n_in + n_out]
        coming = {i: pltpu.make_async_copy(source[i], here[i], arrived.at[i]) for i in range(n_in)}
        going = {i: pltpu.make_async_copy(there[i], target[i], left.at[i]) for i in range(n_out)}
        sent = []
        for i in range(n_in):
            coming[i].start()

        def need(*which):
            for i in which:
                coming.pop(i).wait()

        def done(*which):
            for i in which:
                going[i].start()
                sent.append(i)

        kernel(need, done, *held)
        need(*list(coming))
        done(*[i for i in range(n_out) if i not in sent])
        for i in range(n_out):
            going[i].wait()

    return pl.pallas_call(
        run,
        out_shape=[jax.ShapeDtypeStruct(s, t) for s, t in outs],
        in_specs=[_HBM] * (n_in + len(follows)),
        out_specs=[_HBM] * n_out,
        scratch_shapes=[pltpu.SemaphoreType.DMA((n_in,)), pltpu.SemaphoreType.DMA((n_out,))]
        + [pltpu.VMEM(a.shape, a.dtype) for a in args]
        + [pltpu.VMEM(s, t) for s, t in outs]
        + scratch,
        compiler_params=pltpu.CompilerParams(vmem_limit_bytes=64 * 1024 * 1024),
        cost_estimate=pl.CostEstimate(flops=int(flops), bytes_accessed=4000000, transcendentals=0),
    )(*args, *follows)


def call_small(kernel, outs, scratch, args):
    return pl.pallas_call(
        kernel,
        out_shape=[jax.ShapeDtypeStruct(s, t) for s, t in outs],
        in_specs=[pl.BlockSpec(memory_space=pltpu.VMEM)] * len(args),
        out_specs=[pl.BlockSpec(memory_space=pltpu.VMEM)] * len(outs),
        scratch_shapes=scratch,
        compiler_params=pltpu.CompilerParams(vmem_limit_bytes=16 * 1024 * 1024),
        cost_estimate=pl.CostEstimate(flops=1000000, bytes_accessed=4000000, transcendentals=0),
    )(*args)


def shift_both():
    i = lax.broadcasted_iota(jnp.int32, (128, 256), 0)
    j = lax.broadcasted_iota(jnp.int32, (128, 256), 1)
    source = jnp.where(j < 128, j + 127, j + 1) % 128
    return jnp.where(i == source, 1.0, 0.0).astype(BF16)


def roll(value, shift, axis):
    shift %= value.shape[axis]
    return value if shift == 0 else pltpu.roll(value, shift, axis)


def split(plane):
    lead = plane.astype(BF16).astype(F32)
    return jnp.concatenate([lead, plane - lead], axis=0).astype(BF16)


def join(tile):
    both = tile.astype(F32)
    return both[:8] + both[8:]


ORDER = [
    ("l", 3), (0, 3), (1, 3), (2, 3), ("u", 3), ("u", 1), ("u", 2), ("u", 0), ("l", 0), ("l", 1),
    (0, 0), (1, 0), (2, 0), ("l", 2), (0, 1), (0, 2), (1, 1), (1, 2), (2, 1), (2, 2),
]
UP, DOWN = (0, 7), (5, 13)


def pack_y(
    need, done, feat, field, vel, cot, own_feat, own_fields, to_next, to_prev, turn
):
    need(0)
    for c in range(16):
        turn[pl.ds(c, 32, stride=16), :] = feat[c].astype(F32)
    for zy in range(32):
        tile = turn[zy * 16 : (zy + 1) * 16, :].astype(BF16)
        own_feat[zy] = tile
        z, y = divmod(zy, 8)
        if y >= 8 - PREV:
            to_next[z * PREV + y - (8 - PREV)] = tile
        if y < NEXT:
            to_prev[z * NEXT + y] = tile
    need(1, 2, 3)
    for i, (kind, z) in enumerate(ORDER):
        tile = split(field[z] if kind == "u" else cot[z] if kind == "l" else vel[kind, z])
        own_fields[i] = tile
        to_next[4 * PREV + i] = tile
        to_prev[4 * NEXT + i] = tile


def pack_z(own_feat, own_fields, before, after, to_up, to_down, up, down, moved, left):
    copies = []

    def move(source, at, out, to, count):
        copies.append(
            pltpu.make_async_copy(
                source.at[at : at + count], out.at[to : to + count], moved.at[len(copies)]
            )
        )

    for out, z, (first, stop) in ((up, 3, UP), (down, 0, DOWN)):
        n = stop - first
        move(before, z * PREV, out, 0, PREV)
        move(own_feat, z * 8, out, PREV, 8)
        move(after, z * NEXT, out, PREV + 8, NEXT)
        move(before, 4 * PREV + first, out, ROWS_IN, n)
        move(own_fields, first, out, ROWS_IN + n, n)
        move(after, 4 * NEXT + first, out, ROWS_IN + 2 * n, n)
    second = ROWS_IN + 3 * (DOWN[1] - DOWN[0])
    move(before, 2 * PREV - 1, down, second, 1)
    move(own_feat, 8, down, second + 1, 8)
    move(after, NEXT, down, second + 9, 1)
    for copy in copies:
        copy.start()
    out_up = pltpu.make_async_copy(up, to_up, left.at[0])
    out_down = pltpu.make_async_copy(down, to_down, left.at[1])
    for copy in copies[:6]:
        copy.wait()
    out_up.start()
    for copy in copies[6:]:
        copy.wait()
    out_down.start()
    out_up.wait()
    out_down.wait()


def fill_columns(columns, shifted, z, rows):
    for a in range(3):
        for b in range(3):
            at = pl.multiple_of(z * 144 + (a * 3 + b) * 16, 16)
            for y in rows:
                columns[pl.ds(at, 16), y * 128 : (y + 1) * 128] = shifted[
                    b, z, (y + a) * 16 : (y + a + 1) * 16, :
                ]


U0, LAM2, U1, LAM1, FACE = slice(0, 10), slice(10, 17), slice(35, 39), slice(39, 47), 47
VEL = (slice(17, 23), slice(23, 29), slice(29, 35))
FAR = [(2, 2), (3, 1), (3, 2), (1, -2), (0, -1), (0, -2)]


def stage_one(
    need, done, own_feat, before, after, below, above, field, vel, cot, w_rows,
    send_up, send_down, columns_own, coef, kept,
    shifted, columns, coef_above,
):
    u0, lam2 = kept.at[U0], kept.at[LAM2]
    velx = [kept.at[v] for v in VEL]
    shift_value = shift_both()
    need(0, 1, 2, 3, 4)
    for z in range(6):
        if z == 0:
            tiles = below[0:ROWS_IN].reshape(ROWS_IN * 16, 128)
        elif z == 5:
            tiles = above[0:ROWS_IN].reshape(ROWS_IN * 16, 128)
        else:
            p = z - 1
            tiles = jnp.concatenate(
                [
                    before[p * PREV : (p + 1) * PREV].reshape(PREV * 16, 128),
                    own_feat[p * 8 : (p + 1) * 8].reshape(128, 128),
                    after[p * NEXT : (p + 1) * NEXT].reshape(NEXT * 16, 128),
                ],
                axis=0,
            )
        shifted[1, z] = tiles
        both = jnp.dot(tiles, shift_value, preferred_element_type=F32).astype(BF16)
        shifted[0, z] = both[:, :128]
        shifted[2, z] = both[:, 128:]
    second = ROWS_IN + 3 * (DOWN[1] - DOWN[0])
    tiles = above[second : second + 10].reshape(160, 128)
    both = jnp.dot(tiles, shift_value, preferred_element_type=F32).astype(BF16)
    shifted[0, 6, 64:224, :] = both[:, :128]
    shifted[1, 6, 64:224, :] = tiles
    shifted[2, 6, 64:224, :] = both[:, 128:]

    need(5, 6, 7)

    def extended(kind, z, own):
        i = ORDER.index((kind, z))
        return jnp.concatenate(
            [join(before[4 * PREV + i]), own, join(after[4 * NEXT + i])], axis=0
        )

    def received(source, part, kind, z):
        n = part[1] - part[0]
        at = ROWS_IN + ORDER.index((kind, z)) - part[0]
        return jnp.concatenate([join(source[at + n * j]) for j in range(3)], axis=0)

    for j in range(3):
        u0[j] = received(below, UP, "u", 1 + j)
        u0[7 + j] = received(above, DOWN, "u", j)
        velx[j][0] = received(below, UP, j, 3)
        velx[j][5] = received(above, DOWN, j, 0)
    lam2[0] = received(below, UP, "l", 3)
    lam2[5] = received(above, DOWN, "l", 0)
    lam2[6] = received(above, DOWN, "l", 1)
    for z in range(4):
        u0[3 + z] = extended("u", z, field[z])
        lam2[1 + z] = extended("l", z, cot[z])
        for d in range(3):
            velx[d][1 + z] = extended(d, z, vel[d, z])

    def fill(z, carry):
        fill_columns(columns, shifted, z, range(ROWS_OUT))
        return carry

    lax.fori_loop(0, 6, fill, 0)
    fill_columns(columns, shifted, 6, range(4, 12))

    columns_own[...] = columns[0:864, 512:1536]
    done(2)
    need(8)
    w_value = w_rows[...]
    for p in range(4):
        plane = jnp.dot(
            w_value, columns[p * 144 : p * 144 + 432, :], preferred_element_type=F32
        )
        for y in range(ROWS_OUT):
            coef[p, (4 + y) * 16 : (5 + y) * 16, :] = plane[:, y * 128 : (y + 1) * 128]

    done(3)
    plane = jnp.dot(w_value, columns[576:1008, 512:1536], preferred_element_type=F32)
    for y in range(8):
        coef_above[y * 16 : (y + 1) * 16, :] = plane[:, y * 128 : (y + 1) * 128]

    def a(p, k):
        value = coef[p, pl.ds(k, 24, stride=16), :]
        return value + BASE[k % 5]

    pushed = [None] * 8

    def push(slot, value):
        pushed[slot] = value if pushed[slot] is None else pushed[slot] + value

    faces_z = []
    states = []
    carried = {}
    for p in range(4):
        rate = 1.0 + H * coef[p, pl.ds(15, 24, stride=16), :]
        u = u0[3 + p]
        lam = lam2[1 + p]
        state = u * rate
        push(p + 2, lam * rate)
        for d in range(3):
            beyond = lam2[2 + p] if d == 0 else roll(lam, -1, d - 1)
            drive = (-H) * (lam - beyond) * velx[d][1 + p]
            face = None
            for s in range(-2, 3):
                weight = a(p, 5 * d + s + 2)
                term = weight * (u0[3 + p + s] if d == 0 else roll(u, -s, d - 1))
                face = term if face is None else face + term
                back = drive * weight
                if d == 0:
                    push(p + 2 + s, back)
                    if (p, s) in FAR:
                        carried[p, s] = velx[0][1 + p] * weight
                else:
                    push(p + 2, roll(back, s, d - 1))
            face = (H * velx[d][1 + p]) * face
            if d == 0:
                faces_z.append(face)
                state = state - (face if p == 0 else face - faces_z[p - 1])
            else:
                state = state - (face - roll(face, 1, d - 1))
        states.append(state)
    u1_part, lam_part = kept.at[U1], kept.at[LAM1]
    for p in range(4):
        u1_part[p] = states[p]
    for j in range(8):
        lam_part[j] = pushed[j]
    kept[FACE] = faces_z[3]
    ups = [states[1], states[2], states[3], faces_z[3], pushed[5], pushed[6], pushed[7], pushed[4]]
    downs = [states[0], states[1], states[2], pushed[2], pushed[3], pushed[0], pushed[1], pushed[4]]
    for j in range(8):
        send_up[j] = ups[j][4:20]
        send_down[j] = downs[j][4:20]
    for out, keys in ((send_up, FAR[:3]), (send_down, FAR[3:])):
        out[8, 0:8, :] = carried[keys[0]][8:16]
        out[8, 8:16, :] = carried[keys[1]][8:16]
        out[9, 0:8, :] = carried[keys[2]][8:16]
        out[9, 8:16, :] = carried[keys[2]][8:16]
    face = (-H) * (lam2[5, 8:16] - lam2[6, 8:16]) * velx[0][5, 8:16]
    face = face * (BASE[0] + coef_above[pl.ds(0, 8, stride=16), :])
    send_down[7, 4:12, :] = pushed[4][8:16] + face


def patch_gram(need, done, columns_own, gram, full, line):
    need(0)
    total = None
    for p in range(4):
        part = lax.dot_general(
            columns_own[p * 144 : (p + 1) * 144, :],
            columns_own[p * 144 : p * 144 + 432, :],
            NT,
            preferred_element_type=F32,
        )
        total = part if total is None else total + part
    full[:, 0:432] = total
    line[...] = jnp.zeros((16, 1280), F32)

    def put(dz, dy, dx, count, a, b, a_other):
        to = dz * 400 + (dy + 2) * 80 + (dx + 2) * 16
        at = dz * 144 + a_other * 48
        group = (a * 3 + b) * 16
        line[:, to : to + 16 * count] = full[group : group + 16, at : at + 16 * count]

    for dz in range(3):
        for a in range(3):
            put(dz, a, 0, 3, 0, 0, a)
            for b in (1, 2):
                put(dz, a, -b, 1, 0, b, a)
        for a in (1, 2):
            put(dz, -a, 0, 3, a, 0, 0)
            for b in (1, 2):
                put(dz, -a, -b, 1, a, b, 0)
    for t in range(10):
        gram[t * 16 : (t + 1) * 16, :] = line[:, t * 128 : (t + 1) * 128]
    gram[160:192, :] = jnp.zeros((32, 128), F32)


def stage_two(
    need, done, below, above, state, coef, columns_own, gram,
    mixed, tiles, lam0,
    u1, lam1, turn, row,
):
    u0, lam2, u1_part, lam_part = state.at[U0], state.at[LAM2], state.at[U1], state.at[LAM1]
    velx = [state.at[v] for v in VEL]
    need(0, 1, 2, 3)

    def padded(value):
        zero = jnp.zeros((4, 128), F32)
        return jnp.concatenate([zero, value, zero], axis=0)

    low = [padded(below[j]) for j in range(8)]
    high = [padded(above[j]) for j in range(8)]
    for j in range(3):
        u1[j] = low[j]
        u1[7 + j] = high[j] + (state[FACE] if j == 0 else 0.0)
        u1[4 + j] = u1_part[1 + j]
    u1[3] = u1_part[0] + low[3]
    lam1[0] = low[4] + lam_part[1]
    lam1[1] = lam_part[2] + low[5]
    lam1[2] = lam_part[3] + low[6]
    lam1[3] = lam_part[4] + high[5]
    lam1[4] = lam_part[5] + high[6]
    lam1[5] = high[3] + lam_part[6]
    lam1[6] = high[4] + lam_part[7]

    pushed = [None] * 8

    def push(slot, value):
        pushed[slot] = value if pushed[slot] is None else pushed[slot] + value

    own_rows = slice(8, 16)
    lowest = lam_part[0][own_rows] + low[7][own_rows]
    highest = high[7][own_rows]
    fall = [lowest, lam1[0, own_rows], lam1[1, own_rows]]
    rise = [lam1[5, own_rows], lam1[6, own_rows], highest]
    outer = [(-H) * (fall[0] - fall[1]), (-H) * (fall[1] - fall[2])]
    inner = [(-H) * (rise[0] - rise[1]), (-H) * (rise[1] - rise[2])]
    edge = [
        outer[0] * below[8, 0:8, :] + outer[1] * below[8, 8:16, :],
        outer[1] * below[9, 0:8, :],
        inner[0] * above[9, 0:8, :],
        inner[0] * above[8, 8:16, :] + inner[1] * above[8, 0:8, :],
    ]

    for z in range(6):
        later, first = lam2[z], lam1[z]
        v, u = u1[z + 2], u0[z + 2]
        own = 1 <= z <= 4
        p = z - 1
        if own:
            push(z + 1, first * (1.0 + H * coef[p, pl.ds(15, 24, stride=16), :]))
        for d in range(3):
            speed = velx[d][z]
            beyond_later = lam2[z + 1] if d == 0 else roll(later, -1, d - 1)
            beyond_first = lam1[z + 1] if d == 0 else roll(first, -1, d - 1)
            drive_later = (-H) * (later - beyond_later) * speed
            drive_first = (-H) * (first - beyond_first) * speed
            for s in range(-2, 3):
                k = 5 * d + s + 2
                there_later = u1[z + 2 + s] if d == 0 else roll(v, -s, d - 1)
                there_first = u0[z + 2 + s] if d == 0 else roll(u, -s, d - 1)
                turn[z, pl.ds(k, 24, stride=16), :] = (
                    drive_later * there_later + drive_first * there_first
                )
                if own:
                    back = drive_first * (coef[p, pl.ds(k, 24, stride=16), :] + BASE[s + 2])
                    if d == 0:
                        push(z + 1 + s, back)
                    else:
                        push(z + 1, roll(back, s, d - 1))
        turn[z, pl.ds(15, 24, stride=16), :] = H * later * v + H * first * u
    for p in range(4):
        lam0[p] = pushed[2 + p][own_rows] + edge[p]
    done(2)

    for z in range(6):
        tiles[z] = turn[z, 7 * 16 : 17 * 16, :].astype(BF16)
    done(1)
    need(4)
    sum_w = None
    sum_g = None
    for p in range(4):
        mine = jnp.concatenate(
            [tiles[p + 1, (y + 1) * 16 : (y + 2) * 16, :] for y in range(8)], axis=1
        )
        part_w = lax.dot_general(
            mine, columns_own[p * 144 : p * 144 + 432, :], NT, preferred_element_type=F32
        )
        part_g = lax.dot_general(mine, mine, NT, preferred_element_type=F32)
        sum_w = part_w if sum_w is None else sum_w + part_w
        sum_g = part_g if sum_g is None else sum_g + part_g
    row[...] = jnp.zeros((16, 512), F32)
    row[:, 0:432] = sum_w
    row[:, 432:448] = sum_g
    for t in range(4):
        mixed[t * 16 : (t + 1) * 16, :] = row[:, t * 128 : (t + 1) * 128]
    need(5)
    mixed[64:256, :] = gram[...]


def stage_three(need, done, tiles, w_back, grad_feat, shifted, columns, turn_out):
    need(0)
    shift_value = shift_both()
    for z in range(6):
        shifted[1, z] = tiles[z]
        both = jnp.dot(tiles[z], shift_value, preferred_element_type=F32).astype(BF16)
        shifted[0, z] = both[:, :128]
        shifted[2, z] = both[:, 128:]

    def fill(z, carry):
        fill_columns(columns, shifted, z, range(8))
        return carry

    lax.fori_loop(0, 6, fill, 0)
    need(1)
    w_value = w_back[...]
    for p in range(4):
        plane = jnp.dot(
            w_value, columns[p * 144 : p * 144 + 432, :], preferred_element_type=F32
        )
        for y in range(8):
            turn_out[pl.ds(p * 8 + y, 16, stride=32), :] = plane[:, y * 128 : (y + 1) * 128]
    for c in range(16):
        grad_feat[c] = turn_out[c * 32 : (c + 1) * 32, :].astype(BF16)


def pieces(value):
    one = value.astype(BF16)
    rest = value - one.astype(F32)
    two = rest.astype(BF16)
    return one, two


def to_channel_major(value):
    i = lax.broadcasted_iota(jnp.int32, (432, 432), 0)
    j = lax.broadcasted_iota(jnp.int32, (432, 432), 1)
    place = jnp.where((i % 16) * 27 + i // 16 == j, 1.0, 0.0).astype(BF16)
    parts = [jnp.dot(v, place, preferred_element_type=F32) for v in pieces(value)]
    return parts[1] + parts[0]


def total_to_all(parts, out):
    total = parts[0]
    for n in range(1, parts.shape[0]):
        total = total + parts[n]
    for n in range(out.shape[0]):
        out[n] = total


def finish(cells, chunks, out_w, out_p, out_g, line, row, square, block, turn):
    for t in range(4):
        row[:, t * 128 : (t + 1) * 128] = chunks[t * 16 : (t + 1) * 16, :]
    for t in range(10):
        line[:, t * 128 : (t + 1) * 128] = chunks[64 + t * 16 : 80 + t * 16, :] * (1.0 / cells)
    out_g[...] = row[:, 432:448] * (1.0 / cells)
    for dz in range(3):
        for a in range(3):
            for b in range(3):
                group = (a * 3 + b) * 16
                for a_other in range(3):
                    to = dz * 144 + a_other * 48
                    at = dz * 400 + (a_other - a + 2) * 80 + (2 - b) * 16
                    square[group : group + 16, to : to + 48] = line[:, at : at + 48]
    square[144:288, 144:432] = square[0:144, 0:288]
    square[288:432, 288:432] = square[0:144, 0:144]
    block[...] = jnp.zeros((256, 256), F32)
    block[0:144, 0:144] = square[0:144, 144:288]
    turned = jnp.transpose(block[...])[0:144, 0:144]
    square[144:288, 0:144] = turned
    square[288:432, 144:288] = turned
    block[0:144, 0:144] = square[0:144, 288:432]
    square[288:432, 0:144] = jnp.transpose(block[...])[0:144, 0:144]
    square[432:448, :] = row[:, 0:432] * (1.0 / math.sqrt(cells))
    ready = to_channel_major(square[...])
    out_w[...] = ready[432:448, :]
    for t in range(4):
        wide = min(128, 432 - t * 128)
        for o in range(27):
            turn[t, pl.ds(o, 16, stride=27), 0:wide] = ready[
                o * 16 : (o + 1) * 16, t * 128 : t * 128 + wide
            ]
        out_p[:, t * 128 : t * 128 + wide] = turn[t, :, 0:wide]


def neighbours(to_next, to_prev, axis):
    size = lax.axis_size(axis)
    up = [(i, (i + 1) % size) for i in range(size)]
    down = [(j, i) for i, j in up]
    return lax.ppermute(to_next, axis, up), lax.ppermute(to_prev, axis, down)


def body(features, field, velocity, weight, cotangent):
    nz, ny = lax.axis_size("gz"), lax.axis_size("gy")
    cells = float(4096 * nz * ny)
    by_offset = weight.reshape(16, 16, 27)
    w_rows = by_offset.transpose(0, 2, 1).reshape(16, 432)
    w_back = by_offset.transpose(1, 2, 0)[:, ::-1, :].reshape(16, 432)
    tile = (16, 128)
    own_feat, own_fields, to_next, to_prev = call(
        pack_y,
        [((32,) + tile, BF16), ((20,) + tile, BF16), ((4 * NEXT + 20,) + tile, BF16),
         ((4 * NEXT + 20,) + tile, BF16)],
        [pltpu.VMEM((512, 128), F32)],
        (features.reshape(16, 32, 128), field, velocity, cotangent),
    )
    before, after = neighbours(to_next, to_prev, "gy")
    along_z = (ROWS_IN + 3 * (DOWN[1] - DOWN[0]) + 10,) * 2
    to_up, to_down = pl.pallas_call(
        pack_z,
        out_shape=[jax.ShapeDtypeStruct((n,) + tile, BF16) for n in along_z],
        in_specs=[_HBM] * 4,
        out_specs=[_HBM] * 2,
        scratch_shapes=[pltpu.VMEM((n,) + tile, BF16) for n in along_z]
        + [pltpu.SemaphoreType.DMA((15,)), pltpu.SemaphoreType.DMA((2,))],
        compiler_params=pltpu.CompilerParams(vmem_limit_bytes=64 * 1024 * 1024),
    )(own_feat, own_fields, before, after)
    below, above = neighbours(to_up, to_down, "gz")
    send_up, send_down, columns_own, coef, state = call(
        stage_one,
        [((10, 16, 128), F32), ((10, 16, 128), F32), ((864, 1024), BF16),
         ((4, 384, 128), F32), ((48, 24, 128), F32)],
        [pltpu.VMEM((3, 7, ROWS_IN * 16, 128), BF16), pltpu.VMEM((1008, ROWS_OUT * 128), BF16),
         pltpu.VMEM((128, 128), F32)],
        (own_feat, before, after, below, above, field, velocity, cotangent, w_rows),
    )
    below1, above1 = neighbours(send_up, send_down, "gz")
    (gram,) = call(
        patch_gram,
        [((192, 128), F32)],
        [pltpu.VMEM((144, 512), F32), pltpu.VMEM((16, 1280), F32)],
        (columns_own,),
        5e8,
    )
    mixed, tiles, grad_field = call(
        stage_two,
        [((256, 128), F32), ((6, 160, 128), BF16), ((4, 8, 128), F32)],
        [pltpu.VMEM((10, 24, 128), F32), pltpu.VMEM((7, 24, 128), F32),
         pltpu.VMEM((6, 384, 128), F32), pltpu.VMEM((16, 512), F32)],
        (below1, above1, state, coef, columns_own, gram),
    )
    (grad_feat,) = call(
        stage_three,
        [((16, 32, 128), BF16)],
        [pltpu.VMEM((3, 6, 160, 128), BF16), pltpu.VMEM((864, 1024), BF16), pltpu.VMEM((512, 128), F32)],
        (tiles, w_back),
        1e8,
        (mixed,),
    )
    half = nz // 2
    line = [
        [(h * half + 2 * m + q) * ny + j for h in range(2) for q in range(2) for j in range(ny)]
        for m in range(half // 2)
    ]
    plane = [
        [(h * half + 2 * m + q) * ny + j for m in range(half // 2)]
        for h in range(2) for q in range(2) for j in range(ny)
    ]
    near, far = len(line[0]), len(plane[0])
    rows = 256 // near
    axes = ("gz", "gy")
    parts = mixed.reshape(near, rows, 128)
    parts = lax.all_to_all(parts, axes, 0, 0, axis_index_groups=line)
    (parts,) = call_small(total_to_all, [((far, rows, 128), F32)], [], (parts,))
    parts = lax.all_to_all(parts, axes, 0, 0, axis_index_groups=plane)
    (parts,) = call_small(total_to_all, [((near, rows, 128), F32)], [], (parts,))
    parts = lax.all_to_all(parts, axes, 0, 0, axis_index_groups=line).reshape(256, 128)
    grad_weight, factor_patch, factor_grad = call_small(
        lambda *refs: finish(cells, *refs),
        [((16, 432), F32), ((432, 432), F32), ((16, 16), F32)],
        [pltpu.VMEM((16, 1280), F32), pltpu.VMEM((16, 512), F32), pltpu.VMEM((448, 432), F32),
         pltpu.VMEM((256, 256), F32), pltpu.VMEM((4, 432, 128), F32)],
        (parts,),
    )
    return (grad_field, grad_feat.reshape(16, 4, 8, 128), grad_weight, factor_patch, factor_grad)


def solution(mesh):
    placed = (
        P(None, "gz", "gy", None),
        P("gz", "gy", None),
        P(None, "gz", "gy", None),
        P(),
        P("gz", "gy", None),
    )
    return jax.shard_map(
        body,
        mesh=mesh,
        in_specs=placed,
        out_specs=(P("gz", "gy", None), P(None, "gz", "gy", None), P(), P(), P()),
        check_vma=False,
    )
```

```python
import math

import jax
import jax.numpy as jnp
from jax import lax
from jax.experimental import pallas as pl
from jax.experimental.pallas import tpu as pltpu
from jax.sharding import PartitionSpec as P

H = 0.15
BASE = (2.0 / 60.0, -13.0 / 60.0, 47.0 / 60.0, 27.0 / 60.0, -3.0 / 60.0)
F32 = jnp.float32
BF16 = jnp.bfloat16
NT = (((1,), (1,)), ((), ()))

ROWS_IN = 19
ROWS_OUT = 17
PREV = 5
NEXT = 6

_HBM = pl.BlockSpec(memory_space=pltpu.HBM)


def call(kernel, outs, scratch, args, flops=1e6, follows=()):
    n_in, n_out = len(args), len(outs)

    def run(*refs):
        source, refs = refs[:n_in], refs[n_in + len(follows) :]
        target = refs[:n_out]
        refs = (None,) * n_in + tuple(refs)
        arrived, left = refs[n_in + n_out : n_in + n_out + 2]
        held = refs[n_in + n_out + 2 :]
        here, there = held[:n_in], held[n_in : n_in + n_out]
        coming = {i: pltpu.make_async_copy(source[i], here[i], arrived.at[i]) for i in range(n_in)}
        going = {i: pltpu.make_async_copy(there[i], target[i], left.at[i]) for i in range(n_out)}
        sent = []
        for i in range(n_in):
            coming[i].start()

        def need(*which):
            for i in which:
                coming.pop(i).wait()

        def done(*which):
            for i in which:
                going[i].start()
                sent.append(i)

        kernel(need, done, *held)
        need(*list(coming))
        done(*[i for i in range(n_out) if i not in sent])
        for i in range(n_out):
            going[i].wait()

    return pl.pallas_call(
        run,
        out_shape=[jax.ShapeDtypeStruct(s, t) for s, t in outs],
        in_specs=[_HBM] * (n_in + len(follows)),
        out_specs=[_HBM] * n_out,
        scratch_shapes=[pltpu.SemaphoreType.DMA((n_in,)), pltpu.SemaphoreType.DMA((n_out,))]
        + [pltpu.VMEM(a.shape, a.dtype) for a in args]
        + [pltpu.VMEM(s, t) for s, t in outs]
        + scratch,
        compiler_params=pltpu.CompilerParams(vmem_limit_bytes=64 * 1024 * 1024),
        cost_estimate=pl.CostEstimate(flops=int(flops), bytes_accessed=4000000, transcendentals=0),
    )(*args, *follows)


def call_small(kernel, outs, scratch, args):
    return pl.pallas_call(
        kernel,
        out_shape=[jax.ShapeDtypeStruct(s, t) for s, t in outs],
        in_specs=[pl.BlockSpec(memory_space=pltpu.VMEM)] * len(args),
        out_specs=[pl.BlockSpec(memory_space=pltpu.VMEM)] * len(outs),
        scratch_shapes=scratch,
        compiler_params=pltpu.CompilerParams(vmem_limit_bytes=16 * 1024 * 1024),
        cost_estimate=pl.CostEstimate(flops=1000000, bytes_accessed=4000000, transcendentals=0),
    )(*args)


def shift_both():
    i = lax.broadcasted_iota(jnp.int32, (128, 256), 0)
    j = lax.broadcasted_iota(jnp.int32, (128, 256), 1)
    source = jnp.where(j < 128, j + 127, j + 1) % 128
    return jnp.where(i == source, 1.0, 0.0).astype(BF16)


def roll(value, shift, axis):
    shift %= value.shape[axis]
    return value if shift == 0 else pltpu.roll(value, shift, axis)


def split(plane):
    lead = plane.astype(BF16).astype(F32)
    return jnp.concatenate([lead, plane - lead], axis=0).astype(BF16)


def join(tile):
    both = tile.astype(F32)
    return both[:8] + both[8:]


ORDER = [
    ("l", 3), (0, 3), (1, 3), (2, 3), ("u", 3), ("u", 1), ("u", 2), ("u", 0), ("l", 0), ("l", 1),
    (0, 0), (1, 0), (2, 0), ("l", 2), (0, 1), (0, 2), (1, 1), (1, 2), (2, 1), (2, 2),
]
UP, DOWN = (0, 7), (5, 13)


def pack_y(
    need, done, feat, field, vel, cot, own_feat, own_fields, to_next, to_prev, turn
):
    need(0)
    for c in range(16):
        turn[pl.ds(c, 32, stride=16), :] = feat[c].astype(F32)
    for zy in range(32):
        tile = turn[zy * 16 : (zy + 1) * 16, :].astype(BF16)
        own_feat[zy] = tile
        z, y = divmod(zy, 8)
        if y >= 8 - PREV:
            to_next[z * PREV + y - (8 - PREV)] = tile
        if y < NEXT:
            to_prev[z * NEXT + y] = tile
    need(1, 2, 3)
    for i, (kind, z) in enumerate(ORDER):
        tile = split(field[z] if kind == "u" else cot[z] if kind == "l" else vel[kind, z])
        own_fields[i] = tile
        to_next[4 * PREV + i] = tile
        to_prev[4 * NEXT + i] = tile


def pack_z(own_feat, own_fields, before, after, to_up, to_down, up, down, moved, left):
    copies = []

    def move(source, at, out, to, count):
        copies.append(
            pltpu.make_async_copy(
                source.at[at : at + count], out.at[to : to + count], moved.at[len(copies)]
            )
        )

    for out, z, (first, stop) in ((up, 3, UP), (down, 0, DOWN)):
        n = stop - first
        move(before, z * PREV, out, 0, PREV)
        move(own_feat, z * 8, out, PREV, 8)
        move(after, z * NEXT, out, PREV + 8, NEXT)
        move(before, 4 * PREV + first, out, ROWS_IN, n)
        move(own_fields, first, out, ROWS_IN + n, n)
        move(after, 4 * NEXT + first, out, ROWS_IN + 2 * n, n)
    second = ROWS_IN + 3 * (DOWN[1] - DOWN[0])
    move(before, 2 * PREV - 1, down, second, 1)
    move(own_feat, 8, down, second + 1, 8)
    move(after, NEXT, down, second + 9, 1)
    for copy in copies:
        copy.start()
    out_up = pltpu.make_async_copy(up, to_up, left.at[0])
    out_down = pltpu.make_async_copy(down, to_down, left.at[1])
    for copy in copies[:6]:
        copy.wait()
    out_up.start()
    for copy in copies[6:]:
        copy.wait()
    out_down.start()
    out_up.wait()
    out_down.wait()


def fill_columns(columns, shifted, z, rows):
    for a in range(3):
        for b in range(3):
            at = pl.multiple_of(z * 144 + (a * 3 + b) * 16, 16)
            for y in rows:
                columns[pl.ds(at, 16), y * 128 : (y + 1) * 128] = shifted[
                    b, z, (y + a) * 16 : (y + a + 1) * 16, :
                ]


U0, LAM2, U1, LAM1, FACE = slice(0, 10), slice(10, 17), slice(35, 39), slice(39, 47), 47
VEL = (slice(17, 23), slice(23, 29), slice(29, 35))
FAR = [(2, 2), (3, 1), (3, 2), (1, -2), (0, -1), (0, -2)]


def stage_one(
    need, done, own_feat, before, after, below, above, field, vel, cot, w_rows,
    send_up, send_down, columns_own, coef, kept,
    shifted, columns, coef_above,
):
    u0, lam2 = kept.at[U0], kept.at[LAM2]
    velx = [kept.at[v] for v in VEL]
    shift_value = shift_both()
    need(0, 1, 2, 3, 4)
    for z in range(6):
        if z == 0:
            tiles = below[0:ROWS_IN].reshape(ROWS_IN * 16, 128)
        elif z == 5:
            tiles = above[0:ROWS_IN].reshape(ROWS_IN * 16, 128)
        else:
            p = z - 1
            tiles = jnp.concatenate(
                [
                    before[p * PREV : (p + 1) * PREV].reshape(PREV * 16, 128),
                    own_feat[p * 8 : (p + 1) * 8].reshape(128, 128),
                    after[p * NEXT : (p + 1) * NEXT].reshape(NEXT * 16, 128),
                ],
                axis=0,
            )
        shifted[1, z] = tiles
        both = jnp.dot(tiles, shift_value, preferred_element_type=F32).astype(BF16)
        shifted[0, z] = both[:, :128]
        shifted[2, z] = both[:, 128:]
    second = ROWS_IN + 3 * (DOWN[1] - DOWN[0])
    tiles = above[second : second + 10].reshape(160, 128)
    both = jnp.dot(tiles, shift_value, preferred_element_type=F32).astype(BF16)
    shifted[0, 6, 64:224, :] = both[:, :128]
    shifted[1, 6, 64:224, :] = tiles
    shifted[2, 6, 64:224, :] = both[:, 128:]

    need(5, 6, 7)

    def extended(kind, z, own):
        i = ORDER.index((kind, z))
        return jnp.concatenate(
            [join(before[4 * PREV + i]), own, join(after[4 * NEXT + i])], axis=0
        )

    def received(source, part, kind, z):
        n = part[1] - part[0]
        at = ROWS_IN + ORDER.index((kind, z)) - part[0]
        return jnp.concatenate([join(source[at + n * j]) for j in range(3)], axis=0)

    for j in range(3):
        u0[j] = received(below, UP, "u", 1 + j)
        u0[7 + j] = received(above, DOWN, "u", j)
        velx[j][0] = received(below, UP, j, 3)
        velx[j][5] = received(above, DOWN, j, 0)
    lam2[0] = received(below, UP, "l", 3)
    lam2[5] = received(above, DOWN, "l", 0)
    lam2[6] = received(above, DOWN, "l", 1)
    for z in range(4):
        u0[3 + z] = extended("u", z, field[z])
        lam2[1 + z] = extended("l", z, cot[z])
        for d in range(3):
            velx[d][1 + z] = extended(d, z, vel[d, z])

    def fill(z, carry):
        fill_columns(columns, shifted, z, range(ROWS_OUT))
        return carry

    lax.fori_loop(0, 6, fill, 0)
    fill_columns(columns, shifted, 6, range(4, 12))

    columns_own[...] = columns[0:864, 512:1536]
    done(2)
    need(8)
    w_value = w_rows[...]
    for p in range(4):
        plane = jnp.dot(
            w_value, columns[p * 144 : p * 144 + 432, :], preferred_element_type=F32
        )
        for y in range(ROWS_OUT):
            coef[p, (4 + y) * 16 : (5 + y) * 16, :] = plane[:, y * 128 : (y + 1) * 128]

    done(3)
    plane = jnp.dot(w_value, columns[576:1008, 512:1536], preferred_element_type=F32)
    for y in range(8):
        coef_above[y * 16 : (y + 1) * 16, :] = plane[:, y * 128 : (y + 1) * 128]

    def a(p, k):
        value = coef[p, pl.ds(k, 24, stride=16), :]
        return value + BASE[k % 5]

    pushed = [None] * 8

    def push(slot, value):
        pushed[slot] = value if pushed[slot] is None else pushed[slot] + value

    faces_z = []
    states = []
    carried = {}
    for p in range(4):
        rate = 1.0 + H * coef[p, pl.ds(15, 24, stride=16), :]
        u = u0[3 + p]
        lam = lam2[1 + p]
        state = u * rate
        push(p + 2, lam * rate)
        for d in range(3):
            beyond = lam2[2 + p] if d == 0 else roll(lam, -1, d - 1)
            drive = (-H) * (lam - beyond) * velx[d][1 + p]
            face = None
            for s in range(-2, 3):
                weight = a(p, 5 * d + s + 2)
                term = weight * (u0[3 + p + s] if d == 0 else roll(u, -s, d - 1))
                face = term if face is None else face + term
                back = drive * weight
                if d == 0:
                    push(p + 2 + s, back)
                    if (p, s) in FAR:
                        carried[p, s] = velx[0][1 + p] * weight
                else:
                    push(p + 2, roll(back, s, d - 1))
            face = (H * velx[d][1 + p]) * face
            if d == 0:
                faces_z.append(face)
                state = state - (face if p == 0 else face - faces_z[p - 1])
            else:
                state = state - (face - roll(face, 1, d - 1))
        states.append(state)
    u1_part, lam_part = kept.at[U1], kept.at[LAM1]
    for p in range(4):
        u1_part[p] = states[p]
    for j in range(8):
        lam_part[j] = pushed[j]
    kept[FACE] = faces_z[3]
    ups = [states[1], states[2], states[3], faces_z[3], pushed[5], pushed[6], pushed[7], pushed[4]]
    downs = [states[0], states[1], states[2], pushed[2], pushed[3], pushed[0], pushed[1], pushed[4]]
    for j in range(8):
        send_up[j] = ups[j][4:20]
        send_down[j] = downs[j][4:20]
    for out, keys in ((send_up, FAR[:3]), (send_down, FAR[3:])):
        out[8, 0:8, :] = carried[keys[0]][8:16]
        out[8, 8:16, :] = carried[keys[1]][8:16]
        out[9, 0:8, :] = carried[keys[2]][8:16]
        out[9, 8:16, :] = carried[keys[2]][8:16]
    face = (-H) * (lam2[5, 8:16] - lam2[6, 8:16]) * velx[0][5, 8:16]
    face = face * (BASE[0] + coef_above[pl.ds(0, 8, stride=16), :])
    send_down[7, 4:12, :] = pushed[4][8:16] + face


def patch_gram(need, done, columns_own, gram, full, line):
    need(0)
    total = None
    for p in range(4):
        part = lax.dot_general(
            columns_own[p * 144 : (p + 1) * 144, :],
            columns_own[p * 144 : p * 144 + 432, :],
            NT,
            preferred_element_type=F32,
        )
        total = part if total is None else total + part
    full[:, 0:432] = total
    line[...] = jnp.zeros((16, 1280), F32)

    def put(dz, dy, dx, count, a, b, a_other):
        to = dz * 400 + (dy + 2) * 80 + (dx + 2) * 16
        at = dz * 144 + a_other * 48
        group = (a * 3 + b) * 16
        line[:, to : to + 16 * count] = full[group : group + 16, at : at + 16 * count]

    for dz in range(3):
        for a in range(3):
            put(dz, a, 0, 3, 0, 0, a)
            for b in (1, 2):
                put(dz, a, -b, 1, 0, b, a)
        for a in (1, 2):
            put(dz, -a, 0, 3, a, 0, 0)
            for b in (1, 2):
                put(dz, -a, -b, 1, a, b, 0)
    for t in range(10):
        gram[t * 16 : (t + 1) * 16, :] = line[:, t * 128 : (t + 1) * 128]
    gram[160:192, :] = jnp.zeros((32, 128), F32)


def stage_two(
    need, done, below, above, state, coef, columns_own, gram,
    mixed, tiles, lam0,
    u1, lam1, turn, row,
):
    u0, lam2, u1_part, lam_part = state.at[U0], state.at[LAM2], state.at[U1], state.at[LAM1]
    velx = [state.at[v] for v in VEL]
    need(0, 1, 2, 3)

    def padded(value):
        zero = jnp.zeros((4, 128), F32)
        return jnp.concatenate([zero, value, zero], axis=0)

    low = [padded(below[j]) for j in range(8)]
    high = [padded(above[j]) for j in range(8)]
    for j in range(3):
        u1[j] = low[j]
        u1[7 + j] = high[j] + (state[FACE] if j == 0 else 0.0)
        u1[4 + j] = u1_part[1 + j]
    u1[3] = u1_part[0] + low[3]
    lam1[0] = low[4] + lam_part[1]
    lam1[1] = lam_part[2] + low[5]
    lam1[2] = lam_part[3] + low[6]
    lam1[3] = lam_part[4] + high[5]
    lam1[4] = lam_part[5] + high[6]
    lam1[5] = high[3] + lam_part[6]
    lam1[6] = high[4] + lam_part[7]

    pushed = [None] * 8

    def push(slot, value):
        pushed[slot] = value if pushed[slot] is None else pushed[slot] + value

    own_rows = slice(8, 16)
    lowest = lam_part[0][own_rows] + low[7][own_rows]
    highest = high[7][own_rows]
    fall = [lowest, lam1[0, own_rows], lam1[1, own_rows]]
    rise = [lam1[5, own_rows], lam1[6, own_rows], highest]
    outer = [(-H) * (fall[0] - fall[1]), (-H) * (fall[1] - fall[2])]
    inner = [(-H) * (rise[0] - rise[1]), (-H) * (rise[1] - rise[2])]
    edge = [
        outer[0] * below[8, 0:8, :] + outer[1] * below[8, 8:16, :],
        outer[1] * below[9, 0:8, :],
        inner[0] * above[9, 0:8, :],
        inner[0] * above[8, 8:16, :] + inner[1] * above[8, 0:8, :],
    ]

    for z in range(6):
        later, first = lam2[z], lam1[z]
        v, u = u1[z + 2], u0[z + 2]
        own = 1 <= z <= 4
        p = z - 1
        if own:
            push(z + 1, first * (1.0 + H * coef[p, pl.ds(15, 24, stride=16), :]))
        for d in range(3):
            speed = velx[d][z]
            beyond_later = lam2[z + 1] if d == 0 else roll(later, -1, d - 1)
            beyond_first = lam1[z + 1] if d == 0 else roll(first, -1, d - 1)
            drive_later = (-H) * (later - beyond_later) * speed
            drive_first = (-H) * (first - beyond_first) * speed
            for s in range(-2, 3):
                k = 5 * d + s + 2
                there_later = u1[z + 2 + s] if d == 0 else roll(v, -s, d - 1)
                there_first = u0[z + 2 + s] if d == 0 else roll(u, -s, d - 1)
                turn[z, pl.ds(k, 24, stride=16), :] = (
                    drive_later * there_later + drive_first * there_first
                )
                if own:
                    back = drive_first * (coef[p, pl.ds(k, 24, stride=16), :] + BASE[s + 2])
                    if d == 0:
                        push(z + 1 + s, back)
                    else:
                        push(z + 1, roll(back, s, d - 1))
        turn[z, pl.ds(15, 24, stride=16), :] = H * later * v + H * first * u
    for p in range(4):
        lam0[p] = pushed[2 + p][own_rows] + edge[p]
    done(2)

    for z in range(6):
        tiles[z] = turn[z, 7 * 16 : 17 * 16, :].astype(BF16)
    done(1)
    need(4)
    sum_w = None
    sum_g = None
    for p in range(4):
        mine = jnp.concatenate(
            [tiles[p + 1, (y + 1) * 16 : (y + 2) * 16, :] for y in range(8)], axis=1
        )
        part_w = lax.dot_general(
            mine, columns_own[p * 144 : p * 144 + 432, :], NT, preferred_element_type=F32
        )
        part_g = lax.dot_general(mine, mine, NT, preferred_element_type=F32)
        sum_w = part_w if sum_w is None else sum_w + part_w
        sum_g = part_g if sum_g is None else sum_g + part_g
    row[...] = jnp.zeros((16, 512), F32)
    row[:, 0:432] = sum_w
    row[:, 432:448] = sum_g
    for t in range(4):
        mixed[t * 16 : (t + 1) * 16, :] = row[:, t * 128 : (t + 1) * 128]
    need(5)
    mixed[64:256, :] = gram[...]


def stage_three(need, done, tiles, w_back, grad_feat, shifted, columns, turn_out):
    need(0)
    shift_value = shift_both()
    for z in range(6):
        shifted[1, z] = tiles[z]
        both = jnp.dot(tiles[z], shift_value, preferred_element_type=F32).astype(BF16)
        shifted[0, z] = both[:, :128]
        shifted[2, z] = both[:, 128:]

    def fill(z, carry):
        fill_columns(columns, shifted, z, range(8))
        return carry

    lax.fori_loop(0, 6, fill, 0)
    need(1)
    w_value = w_back[...]
    for p in range(4):
        plane = jnp.dot(
            w_value, columns[p * 144 : p * 144 + 432, :], preferred_element_type=F32
        )
        for y in range(8):
            turn_out[pl.ds(p * 8 + y, 16, stride=32), :] = plane[:, y * 128 : (y + 1) * 128]
    for c in range(16):
        grad_feat[c] = turn_out[c * 32 : (c + 1) * 32, :].astype(BF16)


def pieces(value):
    one = value.astype(BF16)
    rest = value - one.astype(F32)
    two = rest.astype(BF16)
    return one, two


def to_channel_major(value):
    i = lax.broadcasted_iota(jnp.int32, (432, 432), 0)
    j = lax.broadcasted_iota(jnp.int32, (432, 432), 1)
    place = jnp.where((i % 16) * 27 + i // 16 == j, 1.0, 0.0).astype(BF16)
    parts = [jnp.dot(v, place, preferred_element_type=F32) for v in pieces(value)]
    return parts[1] + parts[0]


def total_to_all(parts, out):
    total = parts[0]
    for n in range(1, parts.shape[0]):
        total = total + parts[n]
    for n in range(out.shape[0]):
        out[n] = total


def finish(cells, chunks, out_w, out_p, out_g, line, row, square, block, turn):
    for t in range(4):
        row[:, t * 128 : (t + 1) * 128] = chunks[t * 16 : (t + 1) * 16, :]
    for t in range(10):
        line[:, t * 128 : (t + 1) * 128] = chunks[64 + t * 16 : 80 + t * 16, :] * (1.0 / cells)
    out_g[...] = row[:, 432:448] * (1.0 / cells)
    for dz in range(3):
        for a in range(3):
            for b in range(3):
                group = (a * 3 + b) * 16
                for a_other in range(3):
                    to = dz * 144 + a_other * 48
                    at = dz * 400 + (a_other - a + 2) * 80 + (2 - b) * 16
                    square[group : group + 16, to : to + 48] = line[:, at : at + 48]
    square[144:288, 144:432] = square[0:144, 0:288]
    square[288:432, 288:432] = square[0:144, 0:144]
    block[...] = jnp.zeros((256, 256), F32)
    block[0:144, 0:144] = square[0:144, 144:288]
    turned = jnp.transpose(block[...])[0:144, 0:144]
    square[144:288, 0:144] = turned
    square[288:432, 144:288] = turned
    block[0:144, 0:144] = square[0:144, 288:432]
    square[288:432, 0:144] = jnp.transpose(block[...])[0:144, 0:144]
    square[432:448, :] = row[:, 0:432] * (1.0 / math.sqrt(cells))
    ready = to_channel_major(square[...])
    out_w[...] = ready[432:448, :]
    for t in range(4):
        wide = min(128, 432 - t * 128)
        for o in range(27):
            turn[t, pl.ds(o, 16, stride=27), 0:wide] = ready[
                o * 16 : (o + 1) * 16, t * 128 : t * 128 + wide
            ]
        out_p[:, t * 128 : t * 128 + wide] = turn[t, :, 0:wide]


def neighbours(to_next, to_prev, axis):
    size = lax.axis_size(axis)
    up = [(i, (i + 1) % size) for i in range(size)]
    down = [(j, i) for i, j in up]
    return lax.ppermute(to_next, axis, up), lax.ppermute(to_prev, axis, down)


def body(features, field, velocity, weight, cotangent):
    nz, ny = lax.axis_size("gz"), lax.axis_size("gy")
    cells = float(4096 * nz * ny)
    by_offset = weight.reshape(16, 16, 27)
    w_rows = by_offset.transpose(0, 2, 1).reshape(16, 432)
    w_back = by_offset.transpose(1, 2, 0)[:, ::-1, :].reshape(16, 432)
    tile = (16, 128)
    own_feat, own_fields, to_next, to_prev = call(
        pack_y,
        [((32,) + tile, BF16), ((20,) + tile, BF16), ((4 * NEXT + 20,) + tile, BF16),
         ((4 * NEXT + 20,) + tile, BF16)],
        [pltpu.VMEM((512, 128), F32)],
        (features.reshape(16, 32, 128), field, velocity, cotangent),
    )
    before, after = neighbours(to_next, to_prev, "gy")
    along_z = (ROWS_IN + 3 * (DOWN[1] - DOWN[0]) + 10,) * 2
    to_up, to_down = pl.pallas_call(
        pack_z,
        out_shape=[jax.ShapeDtypeStruct((n,) + tile, BF16) for n in along_z],
        in_specs=[_HBM] * 4,
        out_specs=[_HBM] * 2,
        scratch_shapes=[pltpu.VMEM((n,) + tile, BF16) for n in along_z]
        + [pltpu.SemaphoreType.DMA((15,)), pltpu.SemaphoreType.DMA((2,))],
        compiler_params=pltpu.CompilerParams(vmem_limit_bytes=64 * 1024 * 1024),
    )(own_feat, own_fields, before, after)
    below, above = neighbours(to_up, to_down, "gz")
    send_up, send_down, columns_own, coef, state = call(
        stage_one,
        [((10, 16, 128), F32), ((10, 16, 128), F32), ((864, 1024), BF16),
         ((4, 384, 128), F32), ((48, 24, 128), F32)],
        [pltpu.VMEM((3, 7, ROWS_IN * 16, 128), BF16), pltpu.VMEM((1008, ROWS_OUT * 128), BF16),
         pltpu.VMEM((128, 128), F32)],
        (own_feat, before, after, below, above, field, velocity, cotangent, w_rows),
    )
    below1, above1 = neighbours(send_up, send_down, "gz")
    (gram,) = call(
        patch_gram,
        [((192, 128), F32)],
        [pltpu.VMEM((144, 512), F32), pltpu.VMEM((16, 1280), F32)],
        (columns_own,),
        5e8,
    )
    mixed, tiles, grad_field = call(
        stage_two,
        [((256, 128), F32), ((6, 160, 128), BF16), ((4, 8, 128), F32)],
        [pltpu.VMEM((10, 24, 128), F32), pltpu.VMEM((7, 24, 128), F32),
         pltpu.VMEM((6, 384, 128), F32), pltpu.VMEM((16, 512), F32)],
        (below1, above1, state, coef, columns_own, gram),
    )
    (grad_feat,) = call(
        stage_three,
        [((16, 32, 128), BF16)],
        [pltpu.VMEM((3, 6, 160, 128), BF16), pltpu.VMEM((864, 1024), BF16), pltpu.VMEM((512, 128), F32)],
        (tiles, w_back),
        1e8,
        (mixed,),
    )
    half = nz // 2
    line = [
        [(h * half + 4 * m + q) * ny + j for h in range(2) for q in range(4) for j in range(ny)]
        for m in range(half // 4)
    ]
    plane = [
        [(h * half + 4 * m + q) * ny + j for m in range(half // 4)]
        for h in range(2) for q in range(4) for j in range(ny)
    ]
    near, far = len(line[0]), len(plane[0])
    rows = 256 // near
    axes = ("gz", "gy")
    parts = mixed.reshape(near, rows, 128)
    parts = lax.all_to_all(parts, axes, 0, 0, axis_index_groups=line)
    (parts,) = call_small(total_to_all, [((far, rows, 128), F32)], [], (parts,))
    parts = lax.all_to_all(parts, axes, 0, 0, axis_index_groups=plane)
    (parts,) = call_small(total_to_all, [((near, rows, 128), F32)], [], (parts,))
    parts = lax.all_to_all(parts, axes, 0, 0, axis_index_groups=line).reshape(256, 128)
    grad_weight, factor_patch, factor_grad = call_small(
        lambda *refs: finish(cells, *refs),
        [((16, 432), F32), ((432, 432), F32), ((16, 16), F32)],
        [pltpu.VMEM((16, 1280), F32), pltpu.VMEM((16, 512), F32), pltpu.VMEM((448, 432), F32),
         pltpu.VMEM((256, 256), F32), pltpu.VMEM((4, 432, 128), F32)],
        (parts,),
    )
    return (grad_field, grad_feat.reshape(16, 4, 8, 128), grad_weight, factor_patch, factor_grad)


def solution(mesh):
    placed = (
        P(None, "gz", "gy", None),
        P("gz", "gy", None),
        P(None, "gz", "gy", None),
        P(),
        P("gz", "gy", None),
    )
    return jax.shard_map(
        body,
        mesh=mesh,
        in_specs=placed,
        out_specs=(P("gz", "gy", None), P(None, "gz", "gy", None), P(), P(), P()),
        check_vma=False,
    )
```

```python
import math

import jax
import jax.numpy as jnp
from jax import lax
from jax.experimental import pallas as pl
from jax.experimental.pallas import tpu as pltpu
from jax.sharding import PartitionSpec as P

H = 0.15
BASE = (2.0 / 60.0, -13.0 / 60.0, 47.0 / 60.0, 27.0 / 60.0, -3.0 / 60.0)
F32 = jnp.float32
BF16 = jnp.bfloat16
NT = (((1,), (1,)), ((), ()))

ROWS_IN = 19
ROWS_OUT = 17
PREV = 5
NEXT = 6

_HBM = pl.BlockSpec(memory_space=pltpu.HBM)


def call(kernel, outs, scratch, args, flops=1e6, follows=()):
    n_in, n_out = len(args), len(outs)

    def run(*refs):
        source, refs = refs[:n_in], refs[n_in + len(follows) :]
        target = refs[:n_out]
        refs = (None,) * n_in + tuple(refs)
        arrived, left = refs[n_in + n_out : n_in + n_out + 2]
        held = refs[n_in + n_out + 2 :]
        here, there = held[:n_in], held[n_in : n_in + n_out]
        coming = {i: pltpu.make_async_copy(source[i], here[i], arrived.at[i]) for i in range(n_in)}
        going = {i: pltpu.make_async_copy(there[i], target[i], left.at[i]) for i in range(n_out)}
        sent = []
        for i in range(n_in):
            coming[i].start()

        def need(*which):
            for i in which:
                coming.pop(i).wait()

        def done(*which):
            for i in which:
                going[i].start()
                sent.append(i)

        kernel(need, done, *held)
        need(*list(coming))
        done(*[i for i in range(n_out) if i not in sent])
        for i in range(n_out):
            going[i].wait()

    return pl.pallas_call(
        run,
        out_shape=[jax.ShapeDtypeStruct(s, t) for s, t in outs],
        in_specs=[_HBM] * (n_in + len(follows)),
        out_specs=[_HBM] * n_out,
        scratch_shapes=[pltpu.SemaphoreType.DMA((n_in,)), pltpu.SemaphoreType.DMA((n_out,))]
        + [pltpu.VMEM(a.shape, a.dtype) for a in args]
        + [pltpu.VMEM(s, t) for s, t in outs]
        + scratch,
        compiler_params=pltpu.CompilerParams(vmem_limit_bytes=64 * 1024 * 1024),
        cost_estimate=pl.CostEstimate(flops=int(flops), bytes_accessed=4000000, transcendentals=0),
    )(*args, *follows)


def call_small(kernel, outs, scratch, args):
    return pl.pallas_call(
        kernel,
        out_shape=[jax.ShapeDtypeStruct(s, t) for s, t in outs],
        in_specs=[pl.BlockSpec(memory_space=pltpu.VMEM)] * len(args),
        out_specs=[pl.BlockSpec(memory_space=pltpu.VMEM)] * len(outs),
        scratch_shapes=scratch,
        compiler_params=pltpu.CompilerParams(vmem_limit_bytes=16 * 1024 * 1024),
        cost_estimate=pl.CostEstimate(flops=1000000, bytes_accessed=4000000, transcendentals=0),
    )(*args)


def shift_both():
    i = lax.broadcasted_iota(jnp.int32, (128, 256), 0)
    j = lax.broadcasted_iota(jnp.int32, (128, 256), 1)
    source = jnp.where(j < 128, j + 127, j + 1) % 128
    return jnp.where(i == source, 1.0, 0.0).astype(BF16)


def roll(value, shift, axis):
    shift %= value.shape[axis]
    return value if shift == 0 else pltpu.roll(value, shift, axis)


def split(plane):
    lead = plane.astype(BF16).astype(F32)
    return jnp.concatenate([lead, plane - lead], axis=0).astype(BF16)


def join(tile):
    both = tile.astype(F32)
    return both[:8] + both[8:]


ORDER = [
    ("l", 3), (0, 3), (1, 3), (2, 3), ("u", 3), ("u", 1), ("u", 2), ("u", 0), ("l", 0), ("l", 1),
    (0, 0), (1, 0), (2, 0), ("l", 2), (0, 1), (0, 2), (1, 1), (1, 2), (2, 1), (2, 2),
]
UP, DOWN = (0, 7), (5, 13)


def pack_y(
    need, done, feat, field, vel, cot, own_feat, own_fields, to_next, to_prev, turn
):
    need(0)
    for c in range(16):
        turn[pl.ds(c, 32, stride=16), :] = feat[c].astype(F32)
    for zy in range(32):
        tile = turn[zy * 16 : (zy + 1) * 16, :].astype(BF16)
        own_feat[zy] = tile
        z, y = divmod(zy, 8)
        if y >= 8 - PREV:
            to_next[z * PREV + y - (8 - PREV)] = tile
        if y < NEXT:
            to_prev[z * NEXT + y] = tile
    need(1, 2, 3)
    for i, (kind, z) in enumerate(ORDER):
        tile = split(field[z] if kind == "u" else cot[z] if kind == "l" else vel[kind, z])
        own_fields[i] = tile
        to_next[4 * PREV + i] = tile
        to_prev[4 * NEXT + i] = tile


def pack_z(own_feat, own_fields, before, after, _, to_up, to_down, up, down, moved, left):
    copies = []

    def move(source, at, out, to, count):
        copies.append(
            pltpu.make_async_copy(
                source.at[at : at + count], out.at[to : to + count], moved.at[len(copies)]
            )
        )

    for out, z, (first, stop) in ((up, 3, UP), (down, 0, DOWN)):
        n = stop - first
        move(before, z * PREV, out, 0, PREV)
        move(own_feat, z * 8, out, PREV, 8)
        move(after, z * NEXT, out, PREV + 8, NEXT)
        move(before, 4 * PREV + first, out, ROWS_IN, n)
        move(own_fields, first, out, ROWS_IN + n, n)
        move(after, 4 * NEXT + first, out, ROWS_IN + 2 * n, n)
    second = ROWS_IN + 3 * (DOWN[1] - DOWN[0])
    move(before, 2 * PREV - 1, down, second, 1)
    move(own_feat, 8, down, second + 1, 8)
    move(after, NEXT, down, second + 9, 1)
    for copy in copies:
        copy.start()
    out_up = pltpu.make_async_copy(up, to_up, left.at[0])
    out_down = pltpu.make_async_copy(down, to_down, left.at[1])
    for copy in copies[:6]:
        copy.wait()
    out_up.start()
    for copy in copies[6:]:
        copy.wait()
    out_down.start()
    out_up.wait()
    out_down.wait()


def fill_columns(columns, shifted, z, rows):
    for a in range(3):
        for b in range(3):
            at = pl.multiple_of(z * 144 + (a * 3 + b) * 16, 16)
            for y in rows:
                columns[pl.ds(at, 16), y * 128 : (y + 1) * 128] = shifted[
                    b, z, (y + a) * 16 : (y + a + 1) * 16, :
                ]


U0, LAM2, U1, LAM1, FACE = slice(0, 10), slice(10, 17), slice(35, 39), slice(39, 47), 47
VEL = (slice(17, 23), slice(23, 29), slice(29, 35))
FAR = [(2, 2), (3, 1), (3, 2), (1, -2), (0, -1), (0, -2)]


def stage_one(
    need, done, own_feat, before, after, below, above, field, vel, cot, w_rows,
    send_up, send_down, columns_own, coef, kept,
    shifted, columns, coef_above,
):
    u0, lam2 = kept.at[U0], kept.at[LAM2]
    velx = [kept.at[v] for v in VEL]
    shift_value = shift_both()
    need(0, 1, 2, 3, 4)
    for z in range(6):
        if z == 0:
            tiles = below[0:ROWS_IN].reshape(ROWS_IN * 16, 128)
        elif z == 5:
            tiles = above[0:ROWS_IN].reshape(ROWS_IN * 16, 128)
        else:
            p = z - 1
            tiles = jnp.concatenate(
                [
                    before[p * PREV : (p + 1) * PREV].reshape(PREV * 16, 128),
                    own_feat[p * 8 : (p + 1) * 8].reshape(128, 128),
                    after[p * NEXT : (p + 1) * NEXT].reshape(NEXT * 16, 128),
                ],
                axis=0,
            )
        shifted[1, z] = tiles
        both = jnp.dot(tiles, shift_value, preferred_element_type=F32).astype(BF16)
        shifted[0, z] = both[:, :128]
        shifted[2, z] = both[:, 128:]
    second = ROWS_IN + 3 * (DOWN[1] - DOWN[0])
    tiles = above[second : second + 10].reshape(160, 128)
    both = jnp.dot(tiles, shift_value, preferred_element_type=F32).astype(BF16)
    shifted[0, 6, 64:224, :] = both[:, :128]
    shifted[1, 6, 64:224, :] = tiles
    shifted[2, 6, 64:224, :] = both[:, 128:]

    need(5, 6, 7)

    def extended(kind, z, own):
        i = ORDER.index((kind, z))
        return jnp.concatenate(
            [join(before[4 * PREV + i]), own, join(after[4 * NEXT + i])], axis=0
        )

    def received(source, part, kind, z):
        n = part[1] - part[0]
        at = ROWS_IN + ORDER.index((kind, z)) - part[0]
        return jnp.concatenate([join(source[at + n * j]) for j in range(3)], axis=0)

    for j in range(3):
        u0[j] = received(below, UP, "u", 1 + j)
        u0[7 + j] = received(above, DOWN, "u", j)
        velx[j][0] = received(below, UP, j, 3)
        velx[j][5] = received(above, DOWN, j, 0)
    lam2[0] = received(below, UP, "l", 3)
    lam2[5] = received(above, DOWN, "l", 0)
    lam2[6] = received(above, DOWN, "l", 1)
    for z in range(4):
        u0[3 + z] = extended("u", z, field[z])
        lam2[1 + z] = extended("l", z, cot[z])
        for d in range(3):
            velx[d][1 + z] = extended(d, z, vel[d, z])

    def fill(z, carry):
        fill_columns(columns, shifted, z, range(ROWS_OUT))
        return carry

    lax.fori_loop(0, 6, fill, 0)
    fill_columns(columns, shifted, 6, range(4, 12))

    columns_own[...] = columns[0:864, 512:1536]
    done(2)
    need(8)
    w_value = w_rows[...]
    for p in range(4):
        plane = jnp.dot(
            w_value, columns[p * 144 : p * 144 + 432, :], preferred_element_type=F32
        )
        for y in range(ROWS_OUT):
            coef[p, (4 + y) * 16 : (5 + y) * 16, :] = plane[:, y * 128 : (y + 1) * 128]

    done(3)
    plane = jnp.dot(w_value, columns[576:1008, 512:1536], preferred_element_type=F32)
    for y in range(8):
        coef_above[y * 16 : (y + 1) * 16, :] = plane[:, y * 128 : (y + 1) * 128]

    def a(p, k):
        value = coef[p, pl.ds(k, 24, stride=16), :]
        return value + BASE[k % 5]

    pushed = [None] * 8

    def push(slot, value):
        pushed[slot] = value if pushed[slot] is None else pushed[slot] + value

    faces_z = []
    states = []
    carried = {}
    for p in range(4):
        rate = 1.0 + H * coef[p, pl.ds(15, 24, stride=16), :]
        u = u0[3 + p]
        lam = lam2[1 + p]
        state = u * rate
        push(p + 2, lam * rate)
        for d in range(3):
            beyond = lam2[2 + p] if d == 0 else roll(lam, -1, d - 1)
            drive = (-H) * (lam - beyond) * velx[d][1 + p]
            face = None
            for s in range(-2, 3):
                weight = a(p, 5 * d + s + 2)
                term = weight * (u0[3 + p + s] if d == 0 else roll(u, -s, d - 1))
                face = term if face is None else face + term
                back = drive * weight
                if d == 0:
                    push(p + 2 + s, back)
                    if (p, s) in FAR:
                        carried[p, s] = velx[0][1 + p] * weight
                else:
                    push(p + 2, roll(back, s, d - 1))
            face = (H * velx[d][1 + p]) * face
            if d == 0:
                faces_z.append(face)
                state = state - (face if p == 0 else face - faces_z[p - 1])
            else:
                state = state - (face - roll(face, 1, d - 1))
        states.append(state)
    u1_part, lam_part = kept.at[U1], kept.at[LAM1]
    for p in range(4):
        u1_part[p] = states[p]
    for j in range(8):
        lam_part[j] = pushed[j]
    kept[FACE] = faces_z[3]
    ups = [states[1], states[2], states[3], faces_z[3], pushed[5], pushed[6], pushed[7], pushed[4]]
    downs = [states[0], states[1], states[2], pushed[2], pushed[3], pushed[0], pushed[1], pushed[4]]
    for j in range(8):
        send_up[j] = ups[j][4:20]
        send_down[j] = downs[j][4:20]
    for out, keys in ((send_up, FAR[:3]), (send_down, FAR[3:])):
        out[8, 0:8, :] = carried[keys[0]][8:16]
        out[8, 8:16, :] = carried[keys[1]][8:16]
        out[9, 0:8, :] = carried[keys[2]][8:16]
        out[9, 8:16, :] = carried[keys[2]][8:16]
    face = (-H) * (lam2[5, 8:16] - lam2[6, 8:16]) * velx[0][5, 8:16]
    face = face * (BASE[0] + coef_above[pl.ds(0, 8, stride=16), :])
    send_down[7, 4:12, :] = pushed[4][8:16] + face


def patch_gram(need, done, columns_own, gram, full, line):
    need(0)
    total = None
    for p in range(4):
        part = lax.dot_general(
            columns_own[p * 144 : (p + 1) * 144, :],
            columns_own[p * 144 : p * 144 + 432, :],
            NT,
            preferred_element_type=F32,
        )
        total = part if total is None else total + part
    full[:, 0:432] = total
    line[...] = jnp.zeros((16, 1280), F32)

    def put(dz, dy, dx, count, a, b, a_other):
        to = dz * 400 + (dy + 2) * 80 + (dx + 2) * 16
        at = dz * 144 + a_other * 48
        group = (a * 3 + b) * 16
        line[:, to : to + 16 * count] = full[group : group + 16, at : at + 16 * count]

    for dz in range(3):
        for a in range(3):
            put(dz, a, 0, 3, 0, 0, a)
            for b in (1, 2):
                put(dz, a, -b, 1, 0, b, a)
        for a in (1, 2):
            put(dz, -a, 0, 3, a, 0, 0)
            for b in (1, 2):
                put(dz, -a, -b, 1, a, b, 0)
    for t in range(10):
        gram[t * 16 : (t + 1) * 16, :] = line[:, t * 128 : (t + 1) * 128]
    gram[160:192, :] = jnp.zeros((32, 128), F32)


def stage_two(
    need, done, below, above, state, coef, columns_own, gram,
    mixed, tiles, lam0,
    u1, lam1, turn, row,
):
    u0, lam2, u1_part, lam_part = state.at[U0], state.at[LAM2], state.at[U1], state.at[LAM1]
    velx = [state.at[v] for v in VEL]
    need(0, 1, 2, 3)

    def padded(value):
        zero = jnp.zeros((4, 128), F32)
        return jnp.concatenate([zero, value, zero], axis=0)

    low = [padded(below[j]) for j in range(8)]
    high = [padded(above[j]) for j in range(8)]
    for j in range(3):
        u1[j] = low[j]
        u1[7 + j] = high[j] + (state[FACE] if j == 0 else 0.0)
        u1[4 + j] = u1_part[1 + j]
    u1[3] = u1_part[0] + low[3]
    lam1[0] = low[4] + lam_part[1]
    lam1[1] = lam_part[2] + low[5]
    lam1[2] = lam_part[3] + low[6]
    lam1[3] = lam_part[4] + high[5]
    lam1[4] = lam_part[5] + high[6]
    lam1[5] = high[3] + lam_part[6]
    lam1[6] = high[4] + lam_part[7]

    pushed = [None] * 8

    def push(slot, value):
        pushed[slot] = value if pushed[slot] is None else pushed[slot] + value

    own_rows = slice(8, 16)
    lowest = lam_part[0][own_rows] + low[7][own_rows]
    highest = high[7][own_rows]
    fall = [lowest, lam1[0, own_rows], lam1[1, own_rows]]
    rise = [lam1[5, own_rows], lam1[6, own_rows], highest]
    outer = [(-H) * (fall[0] - fall[1]), (-H) * (fall[1] - fall[2])]
    inner = [(-H) * (rise[0] - rise[1]), (-H) * (rise[1] - rise[2])]
    edge = [
        outer[0] * below[8, 0:8, :] + outer[1] * below[8, 8:16, :],
        outer[1] * below[9, 0:8, :],
        inner[0] * above[9, 0:8, :],
        inner[0] * above[8, 8:16, :] + inner[1] * above[8, 0:8, :],
    ]

    for z in range(6):
        later, first = lam2[z], lam1[z]
        v, u = u1[z + 2], u0[z + 2]
        own = 1 <= z <= 4
        p = z - 1
        if own:
            push(z + 1, first * (1.0 + H * coef[p, pl.ds(15, 24, stride=16), :]))
        for d in range(3):
            speed = velx[d][z]
            beyond_later = lam2[z + 1] if d == 0 else roll(later, -1, d - 1)
            beyond_first = lam1[z + 1] if d == 0 else roll(first, -1, d - 1)
            drive_later = (-H) * (later - beyond_later) * speed
            drive_first = (-H) * (first - beyond_first) * speed
            for s in range(-2, 3):
                k = 5 * d + s + 2
                there_later = u1[z + 2 + s] if d == 0 else roll(v, -s, d - 1)
                there_first = u0[z + 2 + s] if d == 0 else roll(u, -s, d - 1)
                turn[z, pl.ds(k, 24, stride=16), :] = (
                    drive_later * there_later + drive_first * there_first
                )
                if own:
                    back = drive_first * (coef[p, pl.ds(k, 24, stride=16), :] + BASE[s + 2])
                    if d == 0:
                        push(z + 1 + s, back)
                    else:
                        push(z + 1, roll(back, s, d - 1))
        turn[z, pl.ds(15, 24, stride=16), :] = H * later * v + H * first * u
    for p in range(4):
        lam0[p] = pushed[2 + p][own_rows] + edge[p]
    done(2)

    for z in range(6):
        tiles[z] = turn[z, 7 * 16 : 17 * 16, :].astype(BF16)
    done(1)
    need(4)
    sum_w = None
    sum_g = None
    for p in range(4):
        mine = jnp.concatenate(
            [tiles[p + 1, (y + 1) * 16 : (y + 2) * 16, :] for y in range(8)], axis=1
        )
        part_w = lax.dot_general(
            mine, columns_own[p * 144 : p * 144 + 432, :], NT, preferred_element_type=F32
        )
        part_g = lax.dot_general(mine, mine, NT, preferred_element_type=F32)
        sum_w = part_w if sum_w is None else sum_w + part_w
        sum_g = part_g if sum_g is None else sum_g + part_g
    row[...] = jnp.zeros((16, 512), F32)
    row[:, 0:432] = sum_w
    row[:, 432:448] = sum_g
    for t in range(4):
        mixed[t * 16 : (t + 1) * 16, :] = row[:, t * 128 : (t + 1) * 128]
    need(5)
    mixed[64:256, :] = gram[...]


def stage_three(need, done, tiles, w_back, grad_feat, shifted, columns, turn_out):
    need(0)
    shift_value = shift_both()
    for z in range(6):
        shifted[1, z] = tiles[z]
        both = jnp.dot(tiles[z], shift_value, preferred_element_type=F32).astype(BF16)
        shifted[0, z] = both[:, :128]
        shifted[2, z] = both[:, 128:]

    def fill(z, carry):
        fill_columns(columns, shifted, z, range(8))
        return carry

    lax.fori_loop(0, 6, fill, 0)
    need(1)
    w_value = w_back[...]
    for p in range(4):
        plane = jnp.dot(
            w_value, columns[p * 144 : p * 144 + 432, :], preferred_element_type=F32
        )
        for y in range(8):
            turn_out[pl.ds(p * 8 + y, 16, stride=32), :] = plane[:, y * 128 : (y + 1) * 128]
    for c in range(16):
        grad_feat[c] = turn_out[c * 32 : (c + 1) * 32, :].astype(BF16)


def pieces(value):
    one = value.astype(BF16)
    rest = value - one.astype(F32)
    two = rest.astype(BF16)
    return one, two


def to_channel_major(value):
    i = lax.broadcasted_iota(jnp.int32, (432, 432), 0)
    j = lax.broadcasted_iota(jnp.int32, (432, 432), 1)
    place = jnp.where((i % 16) * 27 + i // 16 == j, 1.0, 0.0).astype(BF16)
    parts = [jnp.dot(v, place, preferred_element_type=F32) for v in pieces(value)]
    return parts[1] + parts[0]


def total_to_all(parts, out):
    total = parts[0]
    for n in range(1, parts.shape[0]):
        total = total + parts[n]
    for n in range(out.shape[0]):
        out[n] = total


def finish(cells, chunks, out_w, out_p, out_g, line, row, square, block, turn):
    for t in range(4):
        row[:, t * 128 : (t + 1) * 128] = chunks[t * 16 : (t + 1) * 16, :]
    for t in range(10):
        line[:, t * 128 : (t + 1) * 128] = chunks[64 + t * 16 : 80 + t * 16, :] * (1.0 / cells)
    out_g[...] = row[:, 432:448] * (1.0 / cells)
    for dz in range(3):
        for a in range(3):
            for b in range(3):
                group = (a * 3 + b) * 16
                for a_other in range(3):
                    to = dz * 144 + a_other * 48
                    at = dz * 400 + (a_other - a + 2) * 80 + (2 - b) * 16
                    square[group : group + 16, to : to + 48] = line[:, at : at + 48]
    square[144:288, 144:432] = square[0:144, 0:288]
    square[288:432, 288:432] = square[0:144, 0:144]
    block[...] = jnp.zeros((256, 256), F32)
    block[0:144, 0:144] = square[0:144, 144:288]
    turned = jnp.transpose(block[...])[0:144, 0:144]
    square[144:288, 0:144] = turned
    square[288:432, 144:288] = turned
    block[0:144, 0:144] = square[0:144, 288:432]
    square[288:432, 0:144] = jnp.transpose(block[...])[0:144, 0:144]
    square[432:448, :] = row[:, 0:432] * (1.0 / math.sqrt(cells))
    ready = to_channel_major(square[...])
    out_w[...] = ready[432:448, :]
    for t in range(4):
        wide = min(128, 432 - t * 128)
        for o in range(27):
            turn[t, pl.ds(o, 16, stride=27), 0:wide] = ready[
                o * 16 : (o + 1) * 16, t * 128 : t * 128 + wide
            ]
        out_p[:, t * 128 : t * 128 + wide] = turn[t, :, 0:wide]


def neighbours(to_next, to_prev, axis):
    size = lax.axis_size(axis)
    up = [(i, (i + 1) % size) for i in range(size)]
    down = [(j, i) for i, j in up]
    return lax.ppermute(to_next, axis, up), lax.ppermute(to_prev, axis, down)


def body(features, field, velocity, weight, cotangent):
    nz, ny = lax.axis_size("gz"), lax.axis_size("gy")
    cells = float(4096 * nz * ny)
    by_offset = weight.reshape(16, 16, 27)
    w_rows = by_offset.transpose(0, 2, 1).reshape(16, 432)
    w_back = by_offset.transpose(1, 2, 0)[:, ::-1, :].reshape(16, 432)
    tile = (16, 128)
    own_feat, own_fields, to_next, to_prev = call(
        pack_y,
        [((32,) + tile, BF16), ((20,) + tile, BF16), ((4 * NEXT + 20,) + tile, BF16),
         ((4 * NEXT + 20,) + tile, BF16)],
        [pltpu.VMEM((512, 128), F32)],
        (features.reshape(16, 32, 128), field, velocity, cotangent),
    )
    before, after = neighbours(to_next, to_prev, "gy")
    along_z = (ROWS_IN + 3 * (DOWN[1] - DOWN[0]) + 10,) * 2
    to_up, to_down = pl.pallas_call(
        pack_z,
        out_shape=[jax.ShapeDtypeStruct((n,) + tile, BF16) for n in along_z],
        in_specs=[_HBM] * 5,
        out_specs=[_HBM] * 2,
        scratch_shapes=[pltpu.VMEM((n,) + tile, BF16) for n in along_z]
        + [pltpu.SemaphoreType.DMA((15,)), pltpu.SemaphoreType.DMA((2,))],
        compiler_params=pltpu.CompilerParams(vmem_limit_bytes=64 * 1024 * 1024),
    )(own_feat, own_fields, before, after, w_rows)
    below, above = neighbours(to_up, to_down, "gz")
    send_up, send_down, columns_own, coef, state = call(
        stage_one,
        [((10, 16, 128), F32), ((10, 16, 128), F32), ((864, 1024), BF16),
         ((4, 384, 128), F32), ((48, 24, 128), F32)],
        [pltpu.VMEM((3, 7, ROWS_IN * 16, 128), BF16), pltpu.VMEM((1008, ROWS_OUT * 128), BF16),
         pltpu.VMEM((128, 128), F32)],
        (own_feat, before, after, below, above, field, velocity, cotangent, w_rows),
    )
    below1, above1 = neighbours(send_up, send_down, "gz")
    (gram,) = call(
        patch_gram,
        [((192, 128), F32)],
        [pltpu.VMEM((144, 512), F32), pltpu.VMEM((16, 1280), F32)],
        (columns_own,),
        5e8,
    )
    mixed, tiles, grad_field = call(
        stage_two,
        [((256, 128), F32), ((6, 160, 128), BF16), ((4, 8, 128), F32)],
        [pltpu.VMEM((10, 24, 128), F32), pltpu.VMEM((7, 24, 128), F32),
         pltpu.VMEM((6, 384, 128), F32), pltpu.VMEM((16, 512), F32)],
        (below1, above1, state, coef, columns_own, gram),
    )
    (grad_feat,) = call(
        stage_three,
        [((16, 32, 128), BF16)],
        [pltpu.VMEM((3, 6, 160, 128), BF16), pltpu.VMEM((864, 1024), BF16), pltpu.VMEM((512, 128), F32)],
        (tiles, w_back),
        1e8,
        (mixed,),
    )
    half = nz // 2
    line = [
        [(h * half + 4 * m + q) * ny + j for h in range(2) for q in range(4) for j in range(ny)]
        for m in range(half // 4)
    ]
    plane = [
        [(h * half + 4 * m + q) * ny + j for m in range(half // 4)]
        for h in range(2) for q in range(4) for j in range(ny)
    ]
    near, far = len(line[0]), len(plane[0])
    rows = 256 // near
    axes = ("gz", "gy")
    parts = mixed.reshape(near, rows, 128)
    parts = lax.all_to_all(parts, axes, 0, 0, axis_index_groups=line)
    (parts,) = call_small(total_to_all, [((far, rows, 128), F32)], [], (parts,))
    parts = lax.all_to_all(parts, axes, 0, 0, axis_index_groups=plane)
    (parts,) = call_small(total_to_all, [((near, rows, 128), F32)], [], (parts,))
    parts = lax.all_to_all(parts, axes, 0, 0, axis_index_groups=line).reshape(256, 128)
    grad_weight, factor_patch, factor_grad = call_small(
        lambda *refs: finish(cells, *refs),
        [((16, 432), F32), ((432, 432), F32), ((16, 16), F32)],
        [pltpu.VMEM((16, 1280), F32), pltpu.VMEM((16, 512), F32), pltpu.VMEM((448, 432), F32),
         pltpu.VMEM((256, 256), F32), pltpu.VMEM((4, 432, 128), F32)],
        (parts,),
    )
    return (grad_field, grad_feat.reshape(16, 4, 8, 128), grad_weight, factor_patch, factor_grad)


def solution(mesh):
    placed = (
        P(None, "gz", "gy", None),
        P("gz", "gy", None),
        P(None, "gz", "gy", None),
        P(),
        P("gz", "gy", None),
    )
    return jax.shard_map(
        body,
        mesh=mesh,
        in_specs=placed,
        out_specs=(P("gz", "gy", None), P(None, "gz", "gy", None), P(), P(), P()),
        check_vma=False,
    )
```
